32 devices in a mesh: case: 2 (over y), gx: 8 (over z, x), gy: 2 (over core).
Axes of the slice: x: 2, y: 2, z: 4, core: 2. Of those that a mesh axis runs over, the one named last changes fastest.
Arguments:
- fluid_state: float32 [19, 128, 32, 256], P(None, ('case', 'gx'), 'gy'), parts along dimension 1, may hold values from 0 to 1, as said below
- heat_state: float32 [7, 128, 32, 256], P(None, ('case', 'gx'), 'gy'), parts along dimension 1, may hold values from 0 to 1, as said below
- design: float32 [128, 32, 256], P(('case', 'gx'), 'gy'), parts along dimension 0, may hold values from 0 to 1
- cell_type: int32 [128, 32, 256], P(('case', 'gx'), 'gy'), parts along dimension 0, may hold values from 0 to 2, as said below
- boundary: int32 [128, 32, 256], P(('case', 'gx'), 'gy'), parts along dimension 0, may hold values from 0 to 2, as said below
- fluid_adjoint: float32 [19, 128, 32, 256], P(None, ('case', 'gx'), 'gy'), parts along dimension 1, may hold values from -4 to 4
- heat_adjoint: float32 [7, 128, 32, 256], P(None, ('case', 'gx'), 'gy'), parts along dimension 1, may hold values from -4 to 4
Outputs:
- fluid_costate: float32 [19, 128, 32, 256], P(None, ('case', 'gx'), 'gy'), parts along dimension 1
- heat_costate: float32 [7, 128, 32, 256], P(None, ('case', 'gx'), 'gy'), parts along dimension 1
- filtered_sensitivity: float32 [128, 32, 256], P(('case', 'gx'), 'gy'), parts along dimension 0
The draws below stay inside these ranges and needn't reach their ends.
There are 2 independent parts, one for each index of `case`. The reference program is written for one: setup_inputs(seed, part) draws one part's arguments, and reference() takes and returns one part's arrays. A program takes and returns all parts, laid end to end along the dimension named above; each array names one. Nothing has to cross between parts.
Inputs may be any that keep to these rules, and one draw needn't show every extreme that they name: `fluid_state`: positive populations near a flow equilibrium of density near 1 and speeds under 0.1. `heat_state`: positive populations near a heat equilibrium. `cell_type`: 0 a fluid cell, 1 a solid cell, 2 a design cell. `boundary`: 0 an ordinary cell, 1 an inlet cell, 2 an outlet cell.
All inputs are finite; a program needn't handle non-finite values.
Results may differ from the reference program's by a relative error of at most 0.00012.
Values sent between devices are 32-bit elements; how exact they have to be, the bound alone decides.
No kernel may reach another device: no remote copies, remote signals or barrier semaphores. Data moves between devices by JAX's collectives and lax.ppermute only.
A program may use at most 128 MiB of HBM per device.

```python
import jax
import jax.numpy as jnp
from jax import lax

RADIUS = 4
NX = 64
NY = 32
NZ = 256


fluid_vel = [(0, 0, 0), (1, 0, 0), (-1, 0, 0), (0, 1, 0), (0, -1, 0), (0, 0, 1), (0, 0, -1), (1, 1, 0), (-1, -1, 0), (1, -1, 0), (-1, 1, 0), (1, 0, 1), (-1, 0, -1), (1, 0, -1), (-1, 0, 1), (0, 1, 1), (0, -1, -1), (0, 1, -1), (0, -1, 1)]


fluid_wts = [1.0 / 3.0] + [1.0 / 18.0] * 6 + [1.0 / 36.0] * 12


heat_vel = fluid_vel[:7]


heat_wts = [0.25] + [0.125] * 6


def shared_flow(key):
    return jax.random.uniform(jax.random.fold_in(key, 11), (3, NX, NY, NZ), jnp.float32, -0.05, 0.05)


def populations(velocity, amount, jitter, table, weights, factor):
    result = []
    for position, (entry, weight) in enumerate(zip(table, weights)):
        along = entry[0] * velocity[0] + entry[1] * velocity[1] + entry[2] * velocity[2]
        result.append(weight * amount * (1.0 + factor * along) * (1.0 + jitter[position]))
    return jnp.stack(result).astype(jnp.float32)


def draw_fluid_state(key, part):
    velocity = shared_flow(key)
    key = jax.random.fold_in(key, 1)
    density = jax.random.uniform(jax.random.fold_in(key, 2), (NX, NY, NZ), jnp.float32, 0.9, 1.1)
    jitter = jax.random.uniform(jax.random.fold_in(key, 3), (19, NX, NY, NZ), jnp.float32, -0.2, 0.2)
    return populations(velocity, density, jitter, fluid_vel, fluid_wts, 3.0)


def draw_heat_state(key, part):
    velocity = shared_flow(key)
    key = jax.random.fold_in(key, 4)
    temper = jax.random.uniform(jax.random.fold_in(key, 2), (NX, NY, NZ), jnp.float32, 0.5, 1.5)
    jitter = jax.random.uniform(jax.random.fold_in(key, 3), (7, NX, NY, NZ), jnp.float32, -0.2, 0.2)
    return populations(velocity, temper, jitter, heat_vel, heat_wts, 4.0)


def draw_boundary(key, part):
    key = jax.random.fold_in(key, 5)
    labels_roll = jax.random.randint(key, (NX, NY, NZ), 0, 64)
    return jnp.where(labels_roll < 8, 1, jnp.where(labels_roll == 8, 2, 0)).astype(jnp.int32)


def draw_cell_type(key, part):
    key = jax.random.fold_in(key, 7)
    kinds_roll = jax.random.randint(key, (NX, NY, NZ), 0, 8)
    return jnp.where(kinds_roll == 0, 0, jnp.where(kinds_roll == 1, 1, 2)).astype(jnp.int32)


def draw_heat_adjoint(key, part):
    key = jax.random.fold_in(key, 6)
    phase = jax.random.randint(jax.random.fold_in(key, 1), (NX, NY, 1), 0, 4)
    heights = jnp.arange(NZ, dtype=jnp.int32)[None, None, :]
    signs = jnp.where((heights + phase) % 4 < 2, 1.0, -1.0).astype(jnp.float32)
    spread = jax.random.uniform(jax.random.fold_in(key, 2), (7, NX, NY, NZ), jnp.float32, 0.0, 1.0)
    magnitude = 2.0 + 2.0 * spread
    return (signs[None] * magnitude).astype(jnp.float32)


def steps_of(key, dims, cuts, smallest, largest):
    factor_of, own = 1.0, jax.random.fold_in(key, 6)
    for dim, shards_of in cuts:
        steps = jnp.exp(jax.random.uniform(jax.random.fold_in(own, dim), (shards_of,), jnp.float32, smallest / len(cuts), largest / len(cuts)))
        factor_of = factor_of * jnp.repeat(steps, dims[dim] // shards_of).reshape([-1 if axis == dim else 1 for axis in range(len(dims))])
    return factor_of


def noise(key, shape, deviation, most, pieces=(), kind=jnp.bfloat16):
    array = jax.random.normal(key, shape, jnp.float32) * deviation
    if len(pieces) > 0:
        array = steps_of(key, shape, pieces, -0.22, 0.18) * array
    return jnp.clip(array, min=-most, max=most).astype(kind)


def setup_inputs(seed: int = 0, part: int = 0) -> dict:
    arg_keys = jax.random.split(jax.random.key(seed), 8)
    part_keys = jax.random.split(jax.random.fold_in(arg_keys[7], part), 8)
    fluid_state = draw_fluid_state(jax.random.fold_in(jax.random.fold_in(arg_keys[7], part), 71), part)
    heat_state = draw_heat_state(jax.random.fold_in(jax.random.fold_in(arg_keys[7], part), 71), part)
    design = jnp.clip(1.0 * jax.random.uniform(part_keys[2], (NX, NY, NZ), jnp.float32) ** steps_of(part_keys[2], (NX, NY, NZ), ((0, 8), (1, 2)), -0.2, 0.2), 0.0, 1.0)
    cell_type = draw_cell_type(jax.random.fold_in(jax.random.fold_in(arg_keys[7], part), 71), part)
    boundary = draw_boundary(jax.random.fold_in(jax.random.fold_in(arg_keys[7], part), 71), part)
    fluid_adjoint = noise(part_keys[5], (19, NX, NY, NZ), 0.5, 4.0, ((1, 8), (2, 2)), jnp.float32)
    heat_adjoint = draw_heat_adjoint(jax.random.fold_in(jax.random.fold_in(arg_keys[7], part), 71), part)
    return {"fluid_state": fluid_state, "heat_state": heat_state, "design": design, "cell_type": cell_type, "boundary": boundary, "fluid_adjoint": fluid_adjoint, "heat_adjoint": heat_adjoint}


fluid_vel = [(0, 0, 0), (1, 0, 0), (-1, 0, 0), (0, 1, 0), (0, -1, 0), (0, 0, 1), (0, 0, -1), (1, 1, 0), (-1, -1, 0), (1, -1, 0), (-1, 1, 0), (1, 0, 1), (-1, 0, -1), (1, 0, -1), (-1, 0, 1), (0, 1, 1), (0, -1, -1), (0, 1, -1), (0, -1, 1)]
fluid_wts = [1.0 / 3.0] + [1.0 / 18.0] * 6 + [1.0 / 36.0] * 12
heat_vel = fluid_vel[:7]
heat_wts = [0.25] + [0.125] * 6
tau_fluid = 0.8
alpha_max = 4.0
ramp_shape = 0.1
heat_rate = 1.0
inlet_speed = 0.05
two_pi = 6.283185307179586
inlet_eq = [weight * (1.0 + 3.0 * inlet_speed * entry[2] + 4.5 * (inlet_speed * entry[2]) ** 2 - 1.5 * inlet_speed ** 2) for entry, weight in zip(fluid_vel, fluid_wts)]

def moment_sum(pops, table, column):
    result = jnp.zeros_like(pops[0])
    for position, entry in enumerate(table):
        if entry[column] == 1:
            result = result + pops[position]
        elif entry[column] == -1:
            result = result - pops[position]
    return result

def collide(fluid_pops, heat_pops, porosity, inlet_mask):
    density = lax.optimization_barrier(jnp.sum(fluid_pops, axis=0))
    drag_factor = 1.0 + alpha_max * ramp_shape * (1.0 - porosity) / (ramp_shape + porosity)
    inverse = 1.0 / (density * drag_factor)
    velocity = [moment_sum(fluid_pops, fluid_vel, column) * inverse for column in range(3)]
    speed_sq = velocity[0] * velocity[0] + velocity[1] * velocity[1] + velocity[2] * velocity[2]
    fluid_list = []
    for position, (entry, weight) in enumerate(zip(fluid_vel, fluid_wts)):
        along = entry[0] * velocity[0] + entry[1] * velocity[1] + entry[2] * velocity[2]
        equilib = weight * density * (1.0 + 3.0 * along + 4.5 * along * along - 1.5 * speed_sq)
        relaxed = fluid_pops[position] - (fluid_pops[position] - equilib) / tau_fluid
        fluid_list.append(jnp.where(inlet_mask, inlet_eq[position], relaxed))
    temper = lax.optimization_barrier(jnp.sum(heat_pops, axis=0))
    tau_heat = 0.55 + 0.9 * (1.0 - porosity)
    heat_list = []
    for position, (entry, weight) in enumerate(zip(heat_vel, heat_wts)):
        along = entry[0] * velocity[0] + entry[1] * velocity[1] + entry[2] * velocity[2]
        equilib = weight * temper * (1.0 + 4.0 * along)
        relaxed = heat_pops[position] - (heat_pops[position] - equilib) / tau_heat + weight * heat_rate * (1.0 - porosity)
        heat_list.append(jnp.where(inlet_mask, 0.0, relaxed))
    return (jnp.stack(fluid_list), jnp.stack(heat_list))

def propagate(pops, table, direction):
    return jnp.stack([jnp.roll(pops[position], (direction * entry[0], direction * entry[1], direction * entry[2]), axis=(0, 1, 2)) for position, entry in enumerate(table)])

def symbol_part(length):
    indices = jnp.arange(length, dtype=jnp.int32)
    return 2.0 - 2.0 * jnp.cos(indices.astype(jnp.float32) * (two_pi / length))

def reference(fluid_state, heat_state, design, cell_type, boundary, fluid_adjoint, heat_adjoint):
    porosity = jnp.where(cell_type == 2, design, jnp.where(cell_type == 1, 0.0, 1.0)).astype(jnp.float32)
    inlet_mask = boundary == 1
    outlet = (boundary == 2).astype(jnp.float32)

    def local_step(fluid_pops, heat_pops, field):
        return collide(fluid_pops, heat_pops, field, inlet_mask)
    post_zero, back_zero = jax.vjp(local_step, fluid_state, heat_state, porosity)
    fluid_one = propagate(post_zero[0], fluid_vel, 1)
    heat_one = propagate(post_zero[1], heat_vel, 1)
    post_one, back_one = jax.vjp(local_step, fluid_one, heat_one, porosity)
    heat_two = propagate(post_one[1], heat_vel, 1)
    seed_heat = heat_adjoint + (outlet * lax.optimization_barrier(jnp.sum(heat_two, axis=0)))[None]
    lam_fluid, lam_heat, sens_one = back_one((propagate(fluid_adjoint, fluid_vel, -1), propagate(seed_heat, heat_vel, -1)))
    fluid_costate, heat_costate, sens_zero = back_zero((propagate(lam_fluid, fluid_vel, -1), propagate(lam_heat, heat_vel, -1)))
    sensitivity = jnp.where(cell_type == 2, sens_zero + sens_one, 0.0).astype(jnp.float32)
    laplace = symbol_part(NX)[:, None, None] + symbol_part(NY)[None, :, None] + symbol_part(NZ)[None, None, :]
    gain = 1.0 / (1.0 + RADIUS * RADIUS * laplace)
    filtered = jnp.real(jnp.fft.ifftn(jnp.fft.fftn(sensitivity) * gain)).astype(jnp.float32)
    return (fluid_costate, heat_costate, filtered)
```

```python
import numpy as np
import jax
import jax.numpy as jnp
from jax import lax
from jax.experimental import pallas as pl
from jax.experimental.pallas import tpu as pltpu
from jax.sharding import PartitionSpec as P

RADIUS = 4

fluid_vel = [
    (0, 0, 0),
    (1, 0, 0),
    (-1, 0, 0),
    (0, 1, 0),
    (0, -1, 0),
    (0, 0, 1),
    (0, 0, -1),
    (1, 1, 0),
    (-1, -1, 0),
    (1, -1, 0),
    (-1, 1, 0),
    (1, 0, 1),
    (-1, 0, -1),
    (1, 0, -1),
    (-1, 0, 1),
    (0, 1, 1),
    (0, -1, -1),
    (0, 1, -1),
    (0, -1, 1),
]
fluid_wts = [1.0 / 3.0] + [1.0 / 18.0] * 6 + [1.0 / 36.0] * 12
inlet_speed = 0.05
inlet_eq = [
    weight
    * (
        1.0
        + 3.0 * inlet_speed * entry[2]
        + 4.5 * (inlet_speed * entry[2]) ** 2
        - 1.5 * inlet_speed**2
    )
    for entry, weight in zip(fluid_vel, fluid_wts)
]

VEL = fluid_vel + fluid_vel[:7]
COUNT = len(VEL)
STILL = [i for i in range(COUNT) if VEL[i][0] == 0]
PLUS = [i for i in range(COUNT) if VEL[i][0] == 1]
MINUS = [i for i in range(COUNT) if VEL[i][0] == -1]
YPLUS = [i for i in range(COUNT) if VEL[i][1] == 1]
YMINUS = [i for i in range(COUNT) if VEL[i][1] == -1]
FPLUS = [i for i in PLUS if i < 19]
FMINUS = [i for i in MINUS if i < 19]
FYPLUS = [i for i in YPLUS if i < 19]
FYMINUS = [i for i in YMINUS if i < 19]
PLACE = {}
for group, members in enumerate((STILL, PLUS, MINUS)):
    for slot, member in enumerate(members):
        PLACE[member] = (group, slot)

VMEM_BYTES = 24 * 1024 * 1024
F32 = jnp.float32


def params():
    return pltpu.CompilerParams(vmem_limit_bytes=VMEM_BYTES)


def shift_y(value, step, ghost):
    if step == 0:
        return value
    rows = value.shape[0]
    moved = pltpu.roll(value, step % rows, 0)
    place = lax.broadcasted_iota(jnp.int32, value.shape, 0)
    edge = 0 if step > 0 else rows - 1
    return jnp.where(place == edge, jnp.broadcast_to(ghost, value.shape), moved)


def shift_z(value, step):
    if step == 0:
        return value
    return pltpu.roll(value, step % value.shape[1], 1)


def pick(flag, first, second):
    return jnp.where(flag, first, second)


def tiles(rows, columns):
    return [
        (slice(r, r + 8), slice(c, c + 128)) for r in range(0, rows, 8) for c in range(0, columns, 128)
    ]


def porosity_of(design, kind):
    return jnp.where(kind == 2, design, jnp.where(kind == 1, 0.0, 1.0))


def heat_rate_of(porosity):
    return 1.0 / (0.55 + 0.9 * (1.0 - porosity))


def moments(pops, porosity):
    density = pops[0]
    for value in pops[1:]:
        density = density + value
    diff = {i: pops[i] - pops[i + 1] for i in range(1, 19, 2)}
    flux_x = diff[1] + diff[7] + diff[9] + diff[11] + diff[13]
    flux_y = diff[3] + diff[7] - diff[9] + diff[15] + diff[17]
    flux_z = diff[5] + diff[11] - diff[13] + diff[15] - diff[17]
    inverse = (0.1 + porosity) / (density * (0.5 + 0.6 * porosity))
    return density, (flux_x * inverse, flux_y * inverse, flux_z * inverse)


def along(entry, vector):
    total = None
    for part, value in zip(entry, vector):
        if part == 0:
            continue
        if total is None:
            total = value if part == 1 else -value
        else:
            total = total + value if part == 1 else total - value
    return total


def collide_fluid(pops, density, velocity, inlet):
    speed = velocity[0] * velocity[0] + velocity[1] * velocity[1] + velocity[2] * velocity[2]
    scaled = 1.25 * density
    base = scaled - 1.5 * scaled * speed
    result = [jnp.where(inlet, inlet_eq[0], base * (1.0 / 3.0) - 0.25 * pops[0])]
    for i in range(1, 19, 2):
        weight = fluid_wts[i]
        part = along(VEL[i], velocity)
        flow = scaled * part
        even = weight * base + (4.5 * weight) * (flow * part)
        odd = (3.0 * weight) * flow
        result.append(jnp.where(inlet, inlet_eq[i], even + odd - 0.25 * pops[i]))
        result.append(jnp.where(inlet, inlet_eq[i + 1], even - odd - 0.25 * pops[i + 1]))
    return result


def collide_heat(pops, velocity, porosity, inlet):
    temper = pops[0]
    for value in pops[1:]:
        temper = temper + value
    rate = heat_rate_of(porosity)
    keep = 1.0 - rate
    warm = rate * temper
    base = warm + (1.0 - porosity)
    result = [jnp.where(inlet, 0.0, keep * pops[0] + 0.25 * base)]
    for axis in range(3):
        i = 1 + 2 * axis
        odd = 0.5 * (warm * velocity[axis])
        even = 0.125 * base
        result.append(jnp.where(inlet, 0.0, keep * pops[i] + (even + odd)))
        result.append(jnp.where(inlet, 0.0, keep * pops[i + 1] + (even - odd)))
    return result


def collide_adjoint(density, velocity, heat, porosity, inlet, mu, nu):
    ux, uy, uz = velocity
    mu = [jnp.where(inlet, 0.0, value) for value in mu]
    nu = [jnp.where(inlet, 0.0, value) for value in nu]
    even = {i: mu[i] + mu[i + 1] for i in range(1, 19, 2)}
    odd = {i: mu[i] - mu[i + 1] for i in range(1, 19, 2)}
    wa, wb = 1.0 / 18.0, 1.0 / 36.0
    xy_sum, xz_sum, yz_sum = even[7] + even[9], even[11] + even[13], even[15] + even[17]
    m0 = mu[0] * (1.0 / 3.0) + wa * (even[1] + even[3] + even[5]) + wb * (xy_sum + xz_sum + yz_sum)
    m1x = wa * odd[1] + wb * (odd[7] + odd[9] + odd[11] + odd[13])
    m1y = wa * odd[3] + wb * (odd[7] - odd[9] + odd[15] + odd[17])
    m1z = wa * odd[5] + wb * (odd[11] - odd[13] + odd[15] - odd[17])
    mxx = wa * even[1] + wb * (xy_sum + xz_sum)
    myy = wa * even[3] + wb * (xy_sum + yz_sum)
    mzz = wa * even[5] + wb * (xz_sum + yz_sum)
    mxy = wb * (even[7] - even[9])
    mxz = wb * (even[11] - even[13])
    myz = wb * (even[15] - even[17])
    vx = mxx * ux + mxy * uy + mxz * uz
    vy = mxy * ux + myy * uy + myz * uz
    vz = mxz * ux + myz * uy + mzz * uz
    speed = ux * ux + uy * uy + uz * uz
    slope = (
        m0 * (1.0 - 1.5 * speed)
        + 3.0 * (ux * m1x + uy * m1y + uz * m1z)
        + 4.5 * (ux * vx + uy * vy + uz * vz)
    )
    rate = heat_rate_of(porosity)
    keep = 1.0 - rate
    temper = heat[0]
    for value in heat[1:]:
        temper = temper + value
    n0 = 0.25 * nu[0] + 0.125 * (nu[1] + nu[2] + nu[3] + nu[4] + nu[5] + nu[6])
    n1x, n1y, n1z = (0.125 * (nu[i] - nu[i + 1]) for i in (1, 3, 5))
    warm = 4.0 * rate * temper
    scaled = 3.75 * density
    bar_x = scaled * (m1x - m0 * ux + 3.0 * vx) + warm * n1x
    bar_y = scaled * (m1y - m0 * uy + 3.0 * vy) + warm * n1y
    bar_z = scaled * (m1z - m0 * uz + 3.0 * vz) + warm * n1z
    work = bar_x * ux + bar_y * uy + bar_z * uz
    ramp = 0.1 + porosity
    drag = 0.5 + 0.6 * porosity
    over = 1.0 / (density * drag)
    inverse = ramp * over
    b = (bar_x * inverse, bar_y * inverse, bar_z * inverse)
    a = 1.25 * slope - work * (drag * over)
    lam = [a - 0.25 * mu[0]]
    for i in range(1, 19, 2):
        part = along(VEL[i], b)
        lam.append((a + part) - 0.25 * mu[i])
        lam.append((a - part) - 0.25 * mu[i + 1])
    pull = n0 + 4.0 * (ux * n1x + uy * n1y + uz * n1z)
    a_heat = rate * pull
    lam_heat = [keep * value + a_heat for value in nu]
    dot = nu[0] * heat[0]
    for first, second in zip(nu[1:], heat[1:]):
        dot = dot + first * second
    sens = work * (0.44 / (ramp * drag)) - n0 + (0.9 * rate * rate) * (temper * pull - dot)
    return lam, lam_heat, sens


def plane_spec(members, cells, where=lambda x: x):
    _, rows, columns = cells
    return pl.BlockSpec((members, 1, rows, columns), lambda x: (0, where(x), 0, 0))


def field_spec(cells, where=lambda x: x):
    _, rows, columns = cells
    return pl.BlockSpec((1, rows, columns), lambda x: (where(x), 0, 0))


def whole_spec(shape):
    return pl.BlockSpec(tuple(shape), lambda x: (0,) * len(shape))


SCALARS = pl.BlockSpec(memory_space=pltpu.SMEM)


def struct(*shape):
    return jax.ShapeDtypeStruct(shape, F32)


def first_collision(fluid, heat, design, kind, label, adjoint):
    cells = design.shape
    depth, rows, columns = cells

    def kernel(fluid_ref, heat_ref, design_ref, kind_ref, label_ref, adj_ref, still, plus, minus, aux, msg):
        x = pl.program_id(0)
        groups = (still, plus, minus)
        for r, c in tiles(rows, columns):
            porosity = porosity_of(design_ref[0, r, c], kind_ref[0, r, c])
            inlet = label_ref[0, r, c] == 1
            pops = [fluid_ref[i, 0, r, c] for i in range(19)]
            density, velocity = moments(pops, porosity)
            for i, value in enumerate((density,) + velocity):
                aux[i, 0, r, c] = value
            post = collide_fluid(pops, density, velocity, inlet)
            warm = [heat_ref[i, 0, r, c] for i in range(7)]
            post = post + collide_heat(warm, velocity, porosity, inlet)
            for i, value in enumerate(post):
                group, slot = PLACE[i]
                groups[group][slot, 0, r, c] = value
        last = rows - 1
        for slot, i in enumerate(YPLUS):
            group, place = PLACE[i]
            msg[slot, pl.ds(x, 1), :] = groups[group][place, 0, last : last + 1, :]
        for slot, i in enumerate(YMINUS):
            group, place = PLACE[i]
            msg[6 + slot, pl.ds(x, 1), :] = groups[group][place, 0, 0:1, :]
        for slot, i in enumerate(FYPLUS):
            msg[12 + slot, pl.ds(x, 1), :] = adj_ref[i, 0, 0:1, :]
        for slot, i in enumerate(FYMINUS):
            msg[17 + slot, pl.ds(x, 1), :] = adj_ref[i, 0, last : last + 1, :]
        outlet = (label_ref[0] == 2).astype(F32)
        msg[22, pl.ds(x, 1), :] = outlet[0:1, :]
        msg[23, pl.ds(x, 1), :] = outlet[last : last + 1, :]

    return pl.pallas_call(
        kernel,
        grid=(depth,),
        in_specs=[
            plane_spec(19, cells),
            plane_spec(7, cells),
            field_spec(cells),
            field_spec(cells),
            field_spec(cells),
            plane_spec(19, cells),
        ],
        out_specs=[
            plane_spec(14, cells),
            plane_spec(6, cells),
            plane_spec(6, cells),
            plane_spec(4, cells),
            whole_spec((24, depth, columns)),
        ],
        out_shape=[
            struct(14, *cells),
            struct(6, *cells),
            struct(6, *cells),
            struct(4, *cells),
            struct(24, depth, columns),
        ],
        compiler_params=params(),
        name="first_collision",
    )(fluid, heat, design, kind, label, adjoint)


def first_faces(side, plus, minus, adjoint, label, rows_in):
    cells = label.shape
    depth, rows, columns = cells
    far = depth - 1

    def kernel(side_ref, plus_ref, minus_ref, adj_low, adj_high, lab_low, lab_high, rows_ref, *outs):
        even = side_ref[0] == 0

        def ghost(slot, x):
            return rows_ref[slot, x : x + 1, :]

        def emit(slot, first, second, high, low):
            first[slot] = pick(even, high, low)
            second[slot] = pick(even, low, high)

        for slot in range(6):
            i, j = PLUS[slot], MINUS[slot]
            high, low = plus_ref[slot, 0], minus_ref[slot, 0]
            if VEL[i][1]:
                table = YPLUS if VEL[i][1] > 0 else YMINUS
                place = table.index(i) + (0 if VEL[i][1] > 0 else 6)
                high = shift_y(high, VEL[i][1], ghost(place, far))
                table = YPLUS if VEL[j][1] > 0 else YMINUS
                place = table.index(j) + (0 if VEL[j][1] > 0 else 6)
                low = shift_y(low, VEL[j][1], ghost(place, 0))
            emit(slot, outs[0], outs[1], high, low)
        for slot in range(5):
            i, j = FPLUS[slot], FMINUS[slot]
            low, high = adj_low[i, 0], adj_high[j, 0]
            if VEL[i][1]:
                place = 12 + FYPLUS.index(i) if VEL[i][1] > 0 else 17 + FYMINUS.index(i)
                low = shift_y(low, -VEL[i][1], ghost(place, 0))
                place = 12 + FYPLUS.index(j) if VEL[j][1] > 0 else 17 + FYMINUS.index(j)
                high = shift_y(high, -VEL[j][1], ghost(place, far))
            emit(slot, outs[2], outs[3], high, low)
        emit(5, outs[2], outs[3], (lab_high[0] == 2).astype(F32), (lab_low[0] == 2).astype(F32))

    face = (6, rows, columns)
    return pl.pallas_call(
        kernel,
        grid=(1,),
        in_specs=[
            SCALARS,
            plane_spec(6, cells, lambda x: far),
            plane_spec(6, cells, lambda x: 0),
            plane_spec(19, cells, lambda x: 0),
            plane_spec(19, cells, lambda x: far),
            field_spec(cells, lambda x: 0),
            field_spec(cells, lambda x: far),
            whole_spec(rows_in.shape),
        ],
        out_specs=[whole_spec(face)] * 4,
        out_shape=[struct(*face)] * 4,
        compiler_params=params(),
        name="first_faces",
    )(side, plus, minus, adjoint, adjoint, label, label, rows_in)


def second_collision(side, still, plus, minus, rows_in, face_a, face_b, design, kind, label, heat_adjoint):
    cells = design.shape
    depth, rows, columns = cells
    far = depth - 1
    last = rows - 1

    def kernel(
        side_ref, still_ref, plus_ref, minus_ref, rows_ref, a_ref, b_ref, design_ref, kind_ref, label_ref, hadj,
        post, heat, aux, msg, moved, edge,
    ):
        x = pl.program_id(0)
        even = side_ref[0] == 0
        groups = (still_ref, plus_ref, minus_ref)
        for i in range(COUNT):
            group, slot = PLACE[i]
            value = groups[group][slot, 0]
            step = VEL[i]
            if step[1]:
                place = YPLUS.index(i) if step[1] > 0 else 6 + YMINUS.index(i)
                plane = jnp.clip(x - step[0], 0, far)
                value = shift_y(value, step[1], rows_ref[place, pl.ds(plane, 1), :])
            if step[0] == 1:
                value = pick(x == 0, pick(even, b_ref[slot], a_ref[slot]), value)
            elif step[0] == -1:
                value = pick(x == far, pick(even, a_ref[slot], b_ref[slot]), value)
            value = shift_z(value, step[2])
            if i < 19:
                moved[i] = value
            else:
                heat[i - 19, 0] = value
        for r, c in tiles(rows, columns):
            porosity = porosity_of(design_ref[0, r, c], kind_ref[0, r, c])
            inlet = label_ref[0, r, c] == 1
            pops = [moved[i, r, c] for i in range(19)]
            density, velocity = moments(pops, porosity)
            for i, value in enumerate((density,) + velocity):
                aux[i, 0, r, c] = value
            warm = [heat[i, 0, r, c] for i in range(7)]
            for i, value in enumerate(collide_heat(warm, velocity, porosity, inlet)):
                post[i, 0, r, c] = value
        here = pl.ds(x, 1)
        msg[0, here, :] = post[3, 0, last : last + 1, :]
        msg[1, here, :] = post[4, 0, 0:1, :]
        outlet = (label_ref[0] == 2).astype(F32)
        for slot, y in ((0, 0), (1, last)):
            row = slice(y, y + 1)
            inner = post[4, 0, 1:2, :] if y == 0 else post[3, 0, last - 1 : last, :]
            edge[slot, here, :] = (
                post[0, 0, row, :] + shift_z(post[5, 0, row, :], 1) + shift_z(post[6, 0, row, :], -1) + inner
            )
            edge[2 + slot, here, :] = post[1, 0, row, :]
            edge[4 + slot, here, :] = post[2, 0, row, :]
            edge[6 + slot, here, :] = outlet[row, :]
            edge[8 + slot, here, :] = hadj[3 + slot, 0, row, :]

        @pl.when(x == far)
        def _():
            zero = jnp.zeros((1, columns), F32)
            for slot in range(2):
                total = edge[slot] + shift_y(edge[2 + slot], 1, zero) + shift_y(edge[4 + slot], -1, zero)
                msg[2 + slot] = edge[8 + slot] + edge[6 + slot] * total
            msg[4] = jnp.zeros((depth, columns), F32)
            msg[4, 0:1, :] = edge[2, far : far + 1, :]
            msg[4, 1:2, :] = edge[3, far : far + 1, :]
            msg[4, 2:3, :] = edge[4, 0:1, :]
            msg[4, 3:4, :] = edge[5, 0:1, :]

    return pl.pallas_call(
        kernel,
        grid=(depth,),
        in_specs=[
            SCALARS,
            plane_spec(14, cells),
            plane_spec(6, cells, lambda x: jnp.maximum(x - 1, 0)),
            plane_spec(6, cells, lambda x: jnp.minimum(x + 1, far)),
            whole_spec(rows_in.shape),
            whole_spec(face_a.shape),
            whole_spec(face_b.shape),
            field_spec(cells),
            field_spec(cells),
            field_spec(cells),
            plane_spec(7, cells),
        ],
        out_specs=[
            plane_spec(7, cells),
            plane_spec(7, cells),
            plane_spec(4, cells),
            whole_spec((5, depth, columns)),
        ],
        out_shape=[struct(7, *cells), struct(7, *cells), struct(4, *cells), struct(5, depth, columns)],
        scratch_shapes=[pltpu.VMEM((19, rows, columns), F32), pltpu.VMEM((10, depth, columns), F32)],
        compiler_params=params(),
        name="second_collision",
    )(side, still, plus, minus, rows_in, face_a, face_b, design, kind, label, heat_adjoint)


def heat_faces(side, post, heat_adjoint, label, rows_in):
    cells = label.shape
    depth, rows, columns = cells
    far = depth - 1

    def kernel(side_ref, low, low_in, high_in, high, hadj_low, hadj_high, lab_low, lab_high, rows_ref, a_ref, b_ref):
        even = side_ref[0] == 0

        def partial(post_ref, x, other):
            total = post_ref[0, 0] + other
            total = total + shift_y(post_ref[3, 0], 1, rows_ref[0, x : x + 1, :])
            total = total + shift_y(post_ref[4, 0], -1, rows_ref[1, x : x + 1, :])
            return total + shift_z(post_ref[5, 0], 1) + shift_z(post_ref[6, 0], -1)

        high_seed = hadj_high[2, 0] + jnp.where(lab_high[0] == 2, partial(high, far, high_in[1, 0]), 0.0)
        low_seed = hadj_low[1, 0] + jnp.where(lab_low[0] == 2, partial(low, 0, low_in[2, 0]), 0.0)
        high_face, low_face = high[1, 0], low[2, 0]
        a_ref[0:rows] = pick(even, high_face, low_face)
        b_ref[0:rows] = pick(even, low_face, high_face)
        a_ref[rows : 2 * rows] = pick(even, high_seed, low_seed)
        b_ref[rows : 2 * rows] = pick(even, low_seed, high_seed)
        place = lax.broadcasted_iota(jnp.int32, (8, columns), 0)
        high_rows = jnp.where(
            place == 0,
            jnp.broadcast_to(rows_ref[4, 1:2, :], (8, columns)),
            jnp.broadcast_to(rows_ref[4, 0:1, :], (8, columns)),
        )
        low_rows = jnp.where(
            place == 0,
            jnp.broadcast_to(rows_ref[4, 3:4, :], (8, columns)),
            jnp.broadcast_to(rows_ref[4, 2:3, :], (8, columns)),
        )
        a_ref[2 * rows : 2 * rows + 8] = pick(even, high_rows, low_rows)
        b_ref[2 * rows : 2 * rows + 8] = pick(even, low_rows, high_rows)

    shape = (2 * rows + 8, columns)
    return pl.pallas_call(
        kernel,
        grid=(1,),
        in_specs=[
            SCALARS,
            plane_spec(7, cells, lambda x: 0),
            plane_spec(7, cells, lambda x: 1),
            plane_spec(7, cells, lambda x: far - 1),
            plane_spec(7, cells, lambda x: far),
            plane_spec(7, cells, lambda x: 0),
            plane_spec(7, cells, lambda x: far),
            field_spec(cells, lambda x: 0),
            field_spec(cells, lambda x: far),
            whole_spec(rows_in.shape),
        ],
        out_specs=[whole_spec(shape)] * 2,
        out_shape=[struct(*shape)] * 2,
        compiler_params=params(),
        name="heat_faces",
    )(side, post, post, post, post, heat_adjoint, heat_adjoint, label, label, rows_in)


def second_adjoint(
    side, adjoint, heat_adjoint, post, heat, aux, design, kind, label, rows_in, rows_heat, adj_a, adj_b, seed_a, seed_b
):
    cells = design.shape
    depth, rows, columns = cells
    far = depth - 1
    last = rows - 1

    def kernel(
        side_ref, adj, hadj, post_ref, heat_ref, aux_ref, design_ref, kind_ref, label_ref, rows_ref, hrows_ref,
        fa, fb, sa, sb, still, plus, minus, sens, msg, lit, moved,
    ):
        x = pl.program_id(0)
        even = side_ref[0] == 0
        tail = 2 * rows

        def from_left(where):
            return pick(even, sb[where], sa[where])

        def from_right(where):
            return pick(even, sa[where], sb[where])

        @pl.when(x == 0)
        def _():
            def body(plane, carry):
                here = pl.ds(plane, 1)
                total = post_ref[0, plane]
                left = post_ref[1, jnp.maximum(plane - 1, 0)]
                right = post_ref[2, jnp.minimum(plane + 1, far)]
                total = total + pick(plane == 0, from_left(slice(0, rows)), left)
                total = total + pick(plane == far, from_right(slice(0, rows)), right)
                total = total + shift_y(post_ref[3, plane], 1, hrows_ref[0, here, :])
                total = total + shift_y(post_ref[4, plane], -1, hrows_ref[1, here, :])
                total = total + shift_z(post_ref[5, plane], 1) + shift_z(post_ref[6, plane], -1)
                lit[plane] = jnp.where(label_ref[plane] == 2, total, 0.0)
                return carry

            lax.fori_loop(0, depth, body, 0)

        here = pl.ds(x, 1)
        after = jnp.minimum(x + 1, far)
        before = jnp.maximum(x - 1, 0)
        glow = lit[x]
        moved[19] = hadj[0, x] + glow
        ghost = from_right(slice(rows, tail)) + pick(even, fa[5], fb[5]) * post_ref[1, far]
        moved[20] = pick(x == far, ghost, hadj[1, after] + lit[after])
        ghost = from_left(slice(rows, tail)) + pick(even, fb[5], fa[5]) * post_ref[2, 0]
        moved[21] = pick(x == 0, ghost, hadj[2, before] + lit[before])
        left_low, left_high = from_left(slice(tail, tail + 1)), from_left(slice(tail + 1, tail + 2))
        right_low, right_high = from_right(slice(tail, tail + 1)), from_right(slice(tail + 1, tail + 2))
        above = post_ref[3, x, last : last + 1, :]
        above = above + pick(x == 0, left_high, 0.0) + pick(x == far, right_high, 0.0)
        ghost = hrows_ref[2, here, :] + rows_ref[22, here, :] * above
        moved[22] = shift_y(hadj[3, x] + glow, -1, ghost)
        below = post_ref[4, x, 0:1, :]
        below = below + pick(x == 0, left_low, 0.0) + pick(x == far, right_low, 0.0)
        ghost = hrows_ref[3, here, :] + rows_ref[23, here, :] * below
        moved[23] = shift_y(hadj[4, x] + glow, 1, ghost)
        moved[24] = shift_z(hadj[5, x] + glow, -1)
        moved[25] = shift_z(hadj[6, x] + glow, 1)
        for i in range(19):
            step = VEL[i]
            plane = x if step[0] == 0 else (after if step[0] == 1 else before)
            value = adj[i, plane]
            if step[1]:
                place = 12 + FYPLUS.index(i) if step[1] > 0 else 17 + FYMINUS.index(i)
                value = shift_y(value, -step[1], rows_ref[place, pl.ds(plane, 1), :])
            if step[0] == 1:
                slot = FPLUS.index(i)
                value = pick(x == far, pick(even, fa[slot], fb[slot]), value)
            elif step[0] == -1:
                slot = FMINUS.index(i)
                value = pick(x == 0, pick(even, fb[slot], fa[slot]), value)
            moved[i] = shift_z(value, -step[2])
        groups = (still, plus, minus)
        for r, c in tiles(rows, columns):
            porosity = porosity_of(design_ref[x, r, c], kind_ref[x, r, c])
            inlet = label_ref[x, r, c] == 1
            density, ux, uy, uz = (aux_ref[i, 0, r, c] for i in range(4))
            warm = [heat_ref[i, 0, r, c] for i in range(7)]
            mu = [moved[i, r, c] for i in range(19)]
            nu = [moved[19 + i, r, c] for i in range(7)]
            lam, lam_heat, part = collide_adjoint(density, (ux, uy, uz), warm, porosity, inlet, mu, nu)
            for i, value in enumerate(lam + lam_heat):
                group, slot = PLACE[i]
                groups[group][slot, 0, r, c] = value
            sens[0, r, c] = part
        for slot, i in enumerate(YPLUS):
            group, place = PLACE[i]
            msg[slot, here, :] = groups[group][place, 0, 0:1, :]
        for slot, i in enumerate(YMINUS):
            group, place = PLACE[i]
            msg[6 + slot, here, :] = groups[group][place, 0, last : last + 1, :]

    return pl.pallas_call(
        kernel,
        grid=(depth,),
        in_specs=[
            SCALARS,
            whole_spec(adjoint.shape),
            whole_spec(heat_adjoint.shape),
            whole_spec(post.shape),
            plane_spec(7, cells),
            plane_spec(4, cells),
            whole_spec(cells),
            whole_spec(cells),
            whole_spec(cells),
            whole_spec(rows_in.shape),
            whole_spec(rows_heat.shape),
            whole_spec(adj_a.shape),
            whole_spec(adj_b.shape),
            whole_spec(seed_a.shape),
            whole_spec(seed_b.shape),
        ],
        out_specs=[
            plane_spec(14, cells),
            plane_spec(6, cells),
            plane_spec(6, cells),
            field_spec(cells),
            whole_spec((12, depth, columns)),
        ],
        out_shape=[
            struct(14, *cells),
            struct(6, *cells),
            struct(6, *cells),
            struct(*cells),
            struct(12, depth, columns),
        ],
        scratch_shapes=[pltpu.VMEM(cells, F32), pltpu.VMEM((COUNT, rows, columns), F32)],
        compiler_params=params(),
        name="second_adjoint",
    )(
        side, adjoint, heat_adjoint, post, heat, aux, design, kind, label, rows_in, rows_heat, adj_a, adj_b,
        seed_a, seed_b,
    )


def costate_faces(side, plus, minus, rows_in):
    cells = plus.shape[1:]
    depth, rows, columns = cells
    far = depth - 1

    def kernel(side_ref, plus_ref, minus_ref, rows_ref, a_ref, b_ref):
        even = side_ref[0] == 0
        for slot in range(6):
            i, j = PLUS[slot], MINUS[slot]
            low, high = plus_ref[slot, 0], minus_ref[slot, 0]
            if VEL[i][1]:
                place = YPLUS.index(i) if VEL[i][1] > 0 else 6 + YMINUS.index(i)
                low = shift_y(low, -VEL[i][1], rows_ref[place, 0:1, :])
                place = YPLUS.index(j) if VEL[j][1] > 0 else 6 + YMINUS.index(j)
                high = shift_y(high, -VEL[j][1], rows_ref[place, far : far + 1, :])
            a_ref[slot] = pick(even, high, low)
            b_ref[slot] = pick(even, low, high)

    face = (6, rows, columns)
    return pl.pallas_call(
        kernel,
        grid=(1,),
        in_specs=[
            SCALARS,
            plane_spec(6, cells, lambda x: 0),
            plane_spec(6, cells, lambda x: far),
            whole_spec(rows_in.shape),
        ],
        out_specs=[whole_spec(face)] * 2,
        out_shape=[struct(*face)] * 2,
        compiler_params=params(),
        name="costate_faces",
    )(side, plus, minus, rows_in)


def multiply(first, second):
    return jnp.dot(first, second, precision=lax.Precision.HIGHEST, preferred_element_type=F32)


def first_adjoint(side, still, plus, minus, rows_in, face_a, face_b, aux, heat, design, kind, label, sens_one, waves):
    cells = design.shape
    depth, rows, columns = cells
    far = depth - 1
    half = columns // 2

    def kernel(
        side_ref, still_ref, plus_ref, minus_ref, rows_ref, a_ref, b_ref, aux_ref, heat_ref, design_ref, kind_ref,
        label_ref, sens_ref, waves_ref, fluid_out, heat_out, own, other, moved, total,
    ):
        x = pl.program_id(0)
        even = side_ref[0] == 0
        core = side_ref[1]
        after = jnp.minimum(x + 1, far)
        before = jnp.maximum(x - 1, 0)
        groups = (still_ref, plus_ref, minus_ref)
        for i in range(COUNT):
            group, slot = PLACE[i]
            value = groups[group][slot, 0]
            step = VEL[i]
            plane = x if step[0] == 0 else (after if step[0] == 1 else before)
            if step[1]:
                place = YPLUS.index(i) if step[1] > 0 else 6 + YMINUS.index(i)
                value = shift_y(value, -step[1], rows_ref[place, pl.ds(plane, 1), :])
            if step[0] == 1:
                value = pick(x == far, pick(even, a_ref[slot], b_ref[slot]), value)
            elif step[0] == -1:
                value = pick(x == 0, pick(even, b_ref[slot], a_ref[slot]), value)
            moved[i] = shift_z(value, -step[2])
        base = pl.multiple_of(x * rows, rows)
        for r, c in tiles(rows, columns):
            kinds = kind_ref[0, r, c]
            porosity = porosity_of(design_ref[0, r, c], kinds)
            inlet = label_ref[0, r, c] == 1
            density, ux, uy, uz = (aux_ref[i, 0, r, c] for i in range(4))
            warm = [heat_ref[i, 0, r, c] for i in range(7)]
            mu = [moved[i, r, c] for i in range(19)]
            nu = [moved[19 + i, r, c] for i in range(7)]
            lam, lam_heat, part = collide_adjoint(density, (ux, uy, uz), warm, porosity, inlet, mu, nu)
            for i, value in enumerate(lam):
                fluid_out[i, 0, r, c] = value
            for i, value in enumerate(lam_heat):
                heat_out[i, 0, r, c] = value
            total[pl.ds(base + r.start, 8), c] = jnp.where(kinds == 2, part + sens_ref[0, r, c], 0.0)

        @pl.when(x == far)
        def _():
            own[...] = multiply(total[...], waves_ref[core])
            other[...] = multiply(total[...], waves_ref[1 - core])

    flat = (depth * rows, half)
    return pl.pallas_call(
        kernel,
        grid=(depth,),
        in_specs=[
            SCALARS,
            plane_spec(14, cells),
            plane_spec(6, cells, lambda x: jnp.minimum(x + 1, far)),
            plane_spec(6, cells, lambda x: jnp.maximum(x - 1, 0)),
            whole_spec(rows_in.shape),
            whole_spec(face_a.shape),
            whole_spec(face_b.shape),
            plane_spec(4, cells),
            plane_spec(7, cells),
            field_spec(cells),
            field_spec(cells),
            field_spec(cells),
            field_spec(cells),
            whole_spec(waves.shape),
        ],
        out_specs=[plane_spec(19, cells), plane_spec(7, cells), whole_spec(flat), whole_spec(flat)],
        out_shape=[struct(19, *cells), struct(7, *cells), struct(*flat), struct(*flat)],
        scratch_shapes=[
            pltpu.VMEM((COUNT, rows, columns), F32),
            pltpu.VMEM((depth * rows, columns), F32),
        ],
        compiler_params=params(),
        name="first_adjoint",
    )(side, still, plus, minus, rows_in, face_a, face_b, aux, heat, design, kind, label, sens_one, waves)


def hartley(length):
    index = np.arange(length)
    angle = 2.0 * np.pi * ((index[:, None] * index[None, :]) % length) / length
    return (np.cos(angle) + np.sin(angle)) / np.sqrt(length)


def filter_tables(depth, count_y, count_z):
    half = count_z // 2
    wave_z = hartley(count_z)
    waves = np.stack([wave_z[:, :half], wave_z[:, half:]]).astype(np.float32)
    waves_back = np.stack([wave_z[:half], wave_z[half:]]).astype(np.float32)
    wave_y = np.kron(np.eye(depth), hartley(count_y)).astype(np.float32)
    symbol_y = 2.0 - 2.0 * np.cos(2.0 * np.pi * np.arange(count_y) / count_y)
    symbol_z = 2.0 - 2.0 * np.cos(2.0 * np.pi * np.arange(count_z) / count_z)
    weight = float(RADIUS * RADIUS)
    centre = (1.0 + weight * (2.0 + symbol_y[:, None] + symbol_z[None, :])) / weight
    ratio = 2.0 / (centre + np.sqrt(centre * centre - 4.0))
    peak = 1.0 / (weight * (1.0 / ratio - ratio))
    fields = np.stack([ratio, np.log(ratio) * depth, peak]).astype(np.float32)
    fields = np.stack([fields[:, :, :half], fields[:, :, half:]])
    return waves, waves_back, wave_y, fields


def to_modes(side, own, other, wave_y, fields, depth):
    flat, half = own.shape
    rows = flat // depth
    full = 2 * rows

    def kernel(side_ref, own_ref, other_ref, wave_ref, field_ref, modes, ends, both):
        core = side_ref[1]
        for x in range(depth):
            both[x * full : x * full + rows] = own_ref[x * rows : (x + 1) * rows]
            both[x * full + rows : (x + 1) * full] = other_ref[x * rows : (x + 1) * rows]
        modes[...] = multiply(wave_ref[...], both[...])
        ratio = field_ref[core, 0]
        head = modes[0:full]
        for x in range(1, depth):
            head = head * ratio + modes[x * full : (x + 1) * full]
        ends[0] = head
        tail = modes[(depth - 1) * full : depth * full]
        for x in range(depth - 2, -1, -1):
            tail = tail * ratio + modes[x * full : (x + 1) * full]
        ends[1] = tail

    return pl.pallas_call(
        kernel,
        grid=(1,),
        in_specs=[SCALARS, whole_spec(own.shape), whole_spec(own.shape), whole_spec(wave_y.shape), whole_spec(fields.shape)],
        out_specs=[whole_spec((depth * full, half)), whole_spec((2, full, half))],
        out_shape=[struct(depth * full, half), struct(2, full, half)],
        scratch_shapes=[pltpu.VMEM((depth * full, half), F32)],
        compiler_params=params(),
        name="to_modes",
    )(side, own, other, wave_y, fields)


def join_segments(side, ends, arrived, carry, fields, reach):
    shape = ends.shape

    def kernel(side_ref, ends_ref, in_ref, carry_ref, field_ref, ends_out, carry_out):
        core = side_ref[1]
        index = side_ref[2]
        place = lax.rem(index, reach)
        upper = lax.rem(lax.div(index, reach), 2) == 1
        rate = field_ref[core, 1]
        whole = jnp.exp(rate * float(reach))
        forward = jnp.exp(rate * place.astype(F32))
        backward = jnp.exp(rate * (reach - 1 - place).astype(F32))
        head, tail = ends_ref[0], ends_ref[1]
        head_in, tail_in = in_ref[0], in_ref[1]
        carry_out[0] = carry_ref[0] + pick(upper, forward * head_in, 0.0)
        carry_out[1] = carry_ref[1] + pick(upper, 0.0, backward * tail_in)
        ends_out[0] = pick(upper, head + whole * head_in, head_in + whole * head)
        ends_out[1] = pick(upper, tail_in + whole * tail, tail + whole * tail_in)

    return pl.pallas_call(
        kernel,
        grid=(1,),
        in_specs=[SCALARS, whole_spec(shape), whole_spec(shape), whole_spec(shape), whole_spec(fields.shape)],
        out_specs=[whole_spec(shape)] * 2,
        out_shape=[struct(*shape)] * 2,
        compiler_params=params(),
        name="join_segments",
    )(side, ends, arrived, carry, fields)


def from_modes(side, modes, ends, carry, wave_y, fields, depth, parts):
    half = modes.shape[1]
    full = modes.shape[0] // depth
    rows = full // 2

    def kernel(side_ref, modes_ref, ends_ref, carry_ref, wave_ref, field_ref, own, other, solved):
        core = side_ref[1]
        index = side_ref[2]
        ratio, rate, peak = field_ref[core, 0], field_ref[core, 1], field_ref[core, 2]
        around = 1.0 / (1.0 - jnp.exp(rate * float(parts)))
        left = carry_ref[0] + jnp.exp(rate * index.astype(F32)) * around * ends_ref[0]
        right = carry_ref[1] + jnp.exp(rate * (parts - 1 - index).astype(F32)) * around * ends_ref[1]
        run = left
        for x in range(depth):
            run = run * ratio + modes_ref[x * full : (x + 1) * full]
            solved[x * full : (x + 1) * full] = run
        run = right
        for x in range(depth - 1, -1, -1):
            run = run * ratio
            solved[x * full : (x + 1) * full] = peak * (solved[x * full : (x + 1) * full] + run)
            run = run + modes_ref[x * full : (x + 1) * full]
        back = multiply(wave_ref[...], solved[...])
        for x in range(depth):
            own[x * rows : (x + 1) * rows] = back[x * full : x * full + rows]
            other[x * rows : (x + 1) * rows] = back[x * full + rows : (x + 1) * full]

    flat = (depth * rows, half)
    return pl.pallas_call(
        kernel,
        grid=(1,),
        in_specs=[
            SCALARS,
            whole_spec(modes.shape),
            whole_spec(ends.shape),
            whole_spec(ends.shape),
            whole_spec(wave_y.shape),
            whole_spec(fields.shape),
        ],
        out_specs=[whole_spec(flat)] * 2,
        out_shape=[struct(*flat)] * 2,
        scratch_shapes=[pltpu.VMEM(modes.shape, F32)],
        compiler_params=params(),
        name="from_modes",
    )(side, modes, ends, carry, wave_y, fields)


def last_transform(side, own, other, waves_back):
    flat, half = own.shape

    def kernel(side_ref, own_ref, other_ref, wave_ref, out):
        core = side_ref[1]
        out[...] = multiply(own_ref[...], wave_ref[core]) + multiply(other_ref[...], wave_ref[1 - core])

    return pl.pallas_call(
        kernel,
        grid=(1,),
        in_specs=[SCALARS, whole_spec(own.shape), whole_spec(own.shape), whole_spec(waves_back.shape)],
        out_specs=whole_spec((flat, 2 * half)),
        out_shape=struct(flat, 2 * half),
        compiler_params=params(),
        name="last_transform",
    )(side, own, other, waves_back)


def per_device(fluid_state, heat_state, design, cell_type, boundary, fluid_adjoint, heat_adjoint):
    depth, rows, columns = design.shape
    parts = lax.axis_size("gx")
    index = lax.axis_index("gx")
    side = jnp.stack([index % 2, lax.axis_index("gy"), index]).astype(jnp.int32)
    waves, waves_back, wave_y, fields = filter_tables(depth, 2 * rows, columns)

    pairs_a = [(i, i ^ 1) for i in range(parts)]
    pairs_b = [(i, (i + 1) % parts if i % 2 else (i - 1) % parts) for i in range(parts)]

    def across(value):
        return lax.ppermute(value, "gy", [(0, 1), (1, 0)])

    def sideways(first, second):
        second = lax.ppermute(second, "gx", pairs_b)
        first = lax.ppermute(first, "gx", pairs_a)
        return first, second

    still, plus, minus, aux_zero, rows_one = first_collision(
        fluid_state, heat_state, design, cell_type, boundary, fluid_adjoint
    )
    rows_one = across(rows_one)
    face_a, face_b, adj_a, adj_b = first_faces(side, plus, minus, fluid_adjoint, boundary, rows_one)
    face_a, face_b = sideways(face_a, face_b)
    adj_a, adj_b = sideways(adj_a, adj_b)
    post, heat_one, aux_one, rows_heat = second_collision(
        side, still, plus, minus, rows_one, face_a, face_b, design, cell_type, boundary, heat_adjoint
    )
    rows_heat = across(rows_heat)
    seed_a, seed_b = heat_faces(side, post, heat_adjoint, boundary, rows_heat)
    seed_a, seed_b = sideways(seed_a, seed_b)
    still, plus, minus, sens_one, rows_two = second_adjoint(
        side, fluid_adjoint, heat_adjoint, post, heat_one, aux_one, design, cell_type, boundary, rows_one, rows_heat,
        adj_a, adj_b, seed_a, seed_b,
    )
    rows_two = across(rows_two)
    face_a, face_b = costate_faces(side, plus, minus, rows_two)
    face_a, face_b = sideways(face_a, face_b)
    fluid_costate, heat_costate, own, other = first_adjoint(
        side, still, plus, minus, rows_two, face_a, face_b, aux_zero, heat_state, design, cell_type, boundary,
        sens_one, waves,
    )
    other = across(other)
    modes, ends = to_modes(side, own, other, wave_y, fields, depth)
    carry = jnp.zeros_like(ends)
    reach = 1
    while reach < parts:
        arrived = lax.ppermute(ends, "gx", [(i, i ^ reach) for i in range(parts)])
        ends, carry = join_segments(side, ends, arrived, carry, fields, reach)
        reach = 2 * reach
    own, other = from_modes(side, modes, ends, carry, wave_y, fields, depth, parts)
    other = across(other)
    filtered = last_transform(side, own, other, waves_back)
    return (fluid_costate, heat_costate, filtered.reshape(depth, rows, columns))


def solution(mesh):
    return jax.shard_map(
        per_device,
        mesh=mesh,
        in_specs=(
            P(None, ("case", "gx"), "gy", None),
            P(None, ("case", "gx"), "gy", None),
            P(("case", "gx"), "gy", None),
            P(("case", "gx"), "gy", None),
            P(("case", "gx"), "gy", None),
            P(None, ("case", "gx"), "gy", None),
            P(None, ("case", "gx"), "gy", None),
        ),
        out_specs=(
            P(None, ("case", "gx"), "gy", None),
            P(None, ("case", "gx"), "gy", None),
            P(("case", "gx"), "gy", None),
        ),
        check_vma=False,
    )
```

```python
import numpy as np
import jax
import jax.numpy as jnp
from jax import lax
from jax.experimental import pallas as pl
from jax.experimental.pallas import tpu as pltpu
from jax.sharding import PartitionSpec as P

RADIUS = 4

fluid_vel = [
    (0, 0, 0),
    (1, 0, 0),
    (-1, 0, 0),
    (0, 1, 0),
    (0, -1, 0),
    (0, 0, 1),
    (0, 0, -1),
    (1, 1, 0),
    (-1, -1, 0),
    (1, -1, 0),
    (-1, 1, 0),
    (1, 0, 1),
    (-1, 0, -1),
    (1, 0, -1),
    (-1, 0, 1),
    (0, 1, 1),
    (0, -1, -1),
    (0, 1, -1),
    (0, -1, 1),
]
fluid_wts = [1.0 / 3.0] + [1.0 / 18.0] * 6 + [1.0 / 36.0] * 12
inlet_speed = 0.05
inlet_eq = [
    weight
    * (
        1.0
        + 3.0 * inlet_speed * entry[2]
        + 4.5 * (inlet_speed * entry[2]) ** 2
        - 1.5 * inlet_speed**2
    )
    for entry, weight in zip(fluid_vel, fluid_wts)
]

VEL = fluid_vel + fluid_vel[:7]
COUNT = len(VEL)
PLUS = [i for i in range(COUNT) if VEL[i][0] == 1]
MINUS = [i for i in range(COUNT) if VEL[i][0] == -1]
YPLUS = [i for i in range(COUNT) if VEL[i][1] == 1]
YMINUS = [i for i in range(COUNT) if VEL[i][1] == -1]
FPLUS = [i for i in PLUS if i < 19]
FMINUS = [i for i in MINUS if i < 19]
FYPLUS = [i for i in YPLUS if i < 19]
FYMINUS = [i for i in YMINUS if i < 19]

VMEM_BYTES = 24 * 1024 * 1024
F32 = jnp.float32


def params():
    return pltpu.CompilerParams(vmem_limit_bytes=VMEM_BYTES)


def cost(micros):
    return pl.CostEstimate(flops=0, bytes_accessed=int(micros * 1e4), transcendentals=0)


def shift_y(value, step, ghost):
    if step == 0:
        return value
    rows = value.shape[0]
    moved = pltpu.roll(value, step % rows, 0)
    place = lax.broadcasted_iota(jnp.int32, value.shape, 0)
    edge = 0 if step > 0 else rows - 1
    return jnp.where(place == edge, jnp.broadcast_to(ghost, value.shape), moved)


def shift_z(value, step):
    if step == 0:
        return value
    return pltpu.roll(value, step % value.shape[1], 1)


def pick(flag, first, second):
    return jnp.where(flag, first, second)


def tiles(rows, columns):
    return [
        (slice(r, r + 8), slice(c, c + 128)) for r in range(0, rows, 8) for c in range(0, columns, 128)
    ]


def porosity_of(design, kind):
    return jnp.where(kind == 2, design, jnp.where(kind == 1, 0.0, 1.0))


def heat_rate_of(porosity):
    return 1.0 / (0.55 + 0.9 * (1.0 - porosity))


def moments(pops, porosity):
    density = pops[0]
    for value in pops[1:]:
        density = density + value
    diff = {i: pops[i] - pops[i + 1] for i in range(1, 19, 2)}
    flux_x = diff[1] + diff[7] + diff[9] + diff[11] + diff[13]
    flux_y = diff[3] + diff[7] - diff[9] + diff[15] + diff[17]
    flux_z = diff[5] + diff[11] - diff[13] + diff[15] - diff[17]
    inverse = (0.1 + porosity) / (density * (0.5 + 0.6 * porosity))
    return density, (flux_x * inverse, flux_y * inverse, flux_z * inverse)


def along(entry, vector):
    total = None
    for part, value in zip(entry, vector):
        if part == 0:
            continue
        if total is None:
            total = value if part == 1 else -value
        else:
            total = total + value if part == 1 else total - value
    return total


def collide_fluid(pops, density, velocity, inlet):
    speed = velocity[0] * velocity[0] + velocity[1] * velocity[1] + velocity[2] * velocity[2]
    scaled = 1.25 * density
    base = scaled - 1.5 * scaled * speed
    result = [jnp.where(inlet, inlet_eq[0], base * (1.0 / 3.0) - 0.25 * pops[0])]
    for i in range(1, 19, 2):
        weight = fluid_wts[i]
        part = along(VEL[i], velocity)
        flow = scaled * part
        even = weight * base + (4.5 * weight) * (flow * part)
        odd = (3.0 * weight) * flow
        result.append(jnp.where(inlet, inlet_eq[i], even + odd - 0.25 * pops[i]))
        result.append(jnp.where(inlet, inlet_eq[i + 1], even - odd - 0.25 * pops[i + 1]))
    return result


def collide_heat(pops, velocity, porosity, inlet):
    temper = pops[0]
    for value in pops[1:]:
        temper = temper + value
    rate = heat_rate_of(porosity)
    keep = 1.0 - rate
    warm = rate * temper
    base = warm + (1.0 - porosity)
    result = [jnp.where(inlet, 0.0, keep * pops[0] + 0.25 * base)]
    for axis in range(3):
        i = 1 + 2 * axis
        odd = 0.5 * (warm * velocity[axis])
        even = 0.125 * base
        result.append(jnp.where(inlet, 0.0, keep * pops[i] + (even + odd)))
        result.append(jnp.where(inlet, 0.0, keep * pops[i + 1] + (even - odd)))
    return result


def collide_adjoint(density, velocity, heat, porosity, inlet, mu, nu):
    ux, uy, uz = velocity
    mu = [jnp.where(inlet, 0.0, value) for value in mu]
    nu = [jnp.where(inlet, 0.0, value) for value in nu]
    even = {i: mu[i] + mu[i + 1] for i in range(1, 19, 2)}
    odd = {i: mu[i] - mu[i + 1] for i in range(1, 19, 2)}
    wa, wb = 1.0 / 18.0, 1.0 / 36.0
    xy_sum, xz_sum, yz_sum = even[7] + even[9], even[11] + even[13], even[15] + even[17]
    m0 = mu[0] * (1.0 / 3.0) + wa * (even[1] + even[3] + even[5]) + wb * (xy_sum + xz_sum + yz_sum)
    m1x = wa * odd[1] + wb * (odd[7] + odd[9] + odd[11] + odd[13])
    m1y = wa * odd[3] + wb * (odd[7] - odd[9] + odd[15] + odd[17])
    m1z = wa * odd[5] + wb * (odd[11] - odd[13] + odd[15] - odd[17])
    mxx = wa * even[1] + wb * (xy_sum + xz_sum)
    myy = wa * even[3] + wb * (xy_sum + yz_sum)
    mzz = wa * even[5] + wb * (xz_sum + yz_sum)
    mxy = wb * (even[7] - even[9])
    mxz = wb * (even[11] - even[13])
    myz = wb * (even[15] - even[17])
    vx = mxx * ux + mxy * uy + mxz * uz
    vy = mxy * ux + myy * uy + myz * uz
    vz = mxz * ux + myz * uy + mzz * uz
    speed = ux * ux + uy * uy + uz * uz
    slope = (
        m0 * (1.0 - 1.5 * speed)
        + 3.0 * (ux * m1x + uy * m1y + uz * m1z)
        + 4.5 * (ux * vx + uy * vy + uz * vz)
    )
    rate = heat_rate_of(porosity)
    keep = 1.0 - rate
    temper = heat[0]
    for value in heat[1:]:
        temper = temper + value
    n0 = 0.25 * nu[0] + 0.125 * (nu[1] + nu[2] + nu[3] + nu[4] + nu[5] + nu[6])
    n1x, n1y, n1z = (0.125 * (nu[i] - nu[i + 1]) for i in (1, 3, 5))
    warm = 4.0 * rate * temper
    scaled = 3.75 * density
    bar_x = scaled * (m1x - m0 * ux + 3.0 * vx) + warm * n1x
    bar_y = scaled * (m1y - m0 * uy + 3.0 * vy) + warm * n1y
    bar_z = scaled * (m1z - m0 * uz + 3.0 * vz) + warm * n1z
    work = bar_x * ux + bar_y * uy + bar_z * uz
    ramp = 0.1 + porosity
    drag = 0.5 + 0.6 * porosity
    over = 1.0 / (density * drag)
    inverse = ramp * over
    b = (bar_x * inverse, bar_y * inverse, bar_z * inverse)
    a = 1.25 * slope - work * (drag * over)
    lam = [a - 0.25 * mu[0]]
    for i in range(1, 19, 2):
        part = along(VEL[i], b)
        lam.append((a + part) - 0.25 * mu[i])
        lam.append((a - part) - 0.25 * mu[i + 1])
    pull = n0 + 4.0 * (ux * n1x + uy * n1y + uz * n1z)
    a_heat = rate * pull
    lam_heat = [keep * value + a_heat for value in nu]
    dot = nu[0] * heat[0]
    for first, second in zip(nu[1:], heat[1:]):
        dot = dot + first * second
    sens = work * (0.44 / (ramp * drag)) - n0 + (0.9 * rate * rate) * (temper * pull - dot)
    return lam, lam_heat, sens


IN_VMEM = pl.BlockSpec(memory_space=pltpu.VMEM)
IN_HBM = pl.BlockSpec(memory_space=pltpu.HBM)
IN_SMEM = pl.BlockSpec(memory_space=pltpu.SMEM)


def vmem(*shape):
    return pltpu.VMEM(shape, F32)


def hbm(*shape):
    return pltpu.HBM(shape, F32)


def in_hbm(value):
    return pltpu.with_memory_space_constraint(value, pltpu.HBM)


def call(kernel, name, specs, outs, args, scratch=(), aliases=None, micros=1.0):
    spec_of = {"v": IN_VMEM, "h": IN_HBM, "s": IN_SMEM}
    single = len(outs) == 1
    args = [
        pltpu.with_memory_space_constraint(value, pltpu.VMEM) if letter == "v" else value
        for letter, value in zip(specs, args)
    ]
    out_specs = [IN_HBM if out.memory_space == pltpu.HBM else IN_VMEM for out in outs]
    return pl.pallas_call(
        kernel,
        in_specs=[spec_of[letter] for letter in specs],
        out_specs=out_specs[0] if single else out_specs,
        out_shape=outs[0] if single else outs,
        scratch_shapes=list(scratch),
        input_output_aliases=aliases or {},
        compiler_params=params(),
        cost_estimate=cost(micros),
        name=name,
    )(*args)


def row_slot(i):
    return YPLUS.index(i) if VEL[i][1] > 0 else 6 + YMINUS.index(i)


def adjoint_slot(i):
    return 5 + FYPLUS.index(i) if VEL[i][1] > 0 else 10 + FYMINUS.index(i)


def for_planes(planes, body):
    if isinstance(planes, tuple):
        for x in planes:
            body(x)
    else:

        def step(x, carry):
            body(x)
            return carry

        lax.fori_loop(planes[0], planes[-1] + 1, step, 0)


def neighbour(x, step, far):
    plane = x + step
    if isinstance(x, int) and (plane < 0 or plane > far):
        return None
    return plane


def moved_population(source, i, x, direction, slot_of, rows_ref, low, high, far):
    step = tuple(direction * part for part in VEL[i])
    plane = neighbour(x, -step[0], far)
    if plane is None:
        value = low() if step[0] == 1 else high()
    else:
        value = source[i, plane]
        if step[1]:
            value = shift_y(value, step[1], rows_ref[slot_of(i), pl.ds(plane, 1), :])
    return shift_z(value, step[2])


def first_collision(side, fluid, heat, design, kind, label):
    cells = design.shape
    depth, rows, columns = cells
    far = depth - 1
    last = rows - 1

    def kernel(side_ref, fluid_in, heat_in, design_in, kind_in, label_in, post, heat, aux, porosity, label, chosen,
               sides, msg, design, kind, sem):
        fields = (
            pltpu.make_async_copy(design_in, design, sem.at[0]),
            pltpu.make_async_copy(kind_in, kind, sem.at[1]),
            pltpu.make_async_copy(label_in, label, sem.at[2]),
        )

        def loads(x):
            return (
                pltpu.make_async_copy(fluid_in.at[:, x], post.at[0:19, x], sem.at[3 + 2 * x]),
                pltpu.make_async_copy(heat_in.at[:, x], heat.at[:, x], sem.at[4 + 2 * x]),
            )

        for copy in fields:
            copy.start()
        for x in range(depth):
            for copy in loads(x):
                copy.start()
        for copy in fields:
            copy.wait()

        def body(x):
            here = pl.ds(x, 1)
            kinds = kind[x]
            porosity[x] = porosity_of(design[x], kinds)
            chosen[x] = jnp.where(kinds == 2, 1.0, 0.0)
            for copy in loads(x):
                copy.wait()
            for r, c in tiles(rows, columns):
                phi = porosity[x, r, c]
                inlet = label[x, r, c] == 1
                pops = [post[i, x, r, c] for i in range(19)]
                density, velocity = moments(pops, phi)
                for i, value in enumerate((density,) + velocity):
                    aux[i, x, r, c] = value
                warm = [heat[i, x, r, c] for i in range(7)]
                result = collide_fluid(pops, density, velocity, inlet) + collide_heat(warm, velocity, phi, inlet)
                for i, value in enumerate(result):
                    post[i, x, r, c] = value
            for i in YPLUS:
                msg[row_slot(i), here, :] = post[i, x, last : last + 1, :]
            for i in YMINUS:
                msg[row_slot(i), here, :] = post[i, x, 0:1, :]

        for_planes(range(depth), body)
        for slot in range(6):
            sides[slot] = post[PLUS[slot], far]
            sides[6 + slot] = post[MINUS[slot], 0]

    return call(
        kernel,
        "first_collision",
        "shhhhh",
        [
            vmem(COUNT, *cells),
            vmem(7, *cells),
            vmem(4, *cells),
            vmem(*cells),
            pltpu.VMEM(cells, jnp.int32),
            vmem(*cells),
            vmem(12, rows, columns),
            vmem(12, depth, columns),
        ],
        (side, fluid, heat, design, kind, label),
        scratch=[pltpu.VMEM(cells, F32), pltpu.VMEM(cells, jnp.int32), pltpu.SemaphoreType.DMA((3 + 2 * depth,))],
        micros=2.0,
    )


def crossing_faces(name, side, sides, rows_in, direction):
    _, rows, columns = sides.shape
    far = rows_in.shape[1] - 1
    place, other = (far, 0) if direction == 1 else (0, far)

    def kernel(side_ref, sides_ref, rows_ref, a_ref, b_ref):
        even = side_ref[0] == 0
        for slot in range(6):
            i, j = PLUS[slot], MINUS[slot]
            plus, minus = sides_ref[slot], sides_ref[6 + slot]
            if VEL[i][1]:
                plus = shift_y(plus, direction * VEL[i][1], rows_ref[row_slot(i), place : place + 1, :])
                minus = shift_y(minus, direction * VEL[j][1], rows_ref[row_slot(j), other : other + 1, :])
            high, low = (plus, minus) if direction == 1 else (minus, plus)
            a_ref[slot] = pick(even, high, low)
            b_ref[slot] = pick(even, low, high)

    return call(kernel, name, "svv", [vmem(6, rows, columns)] * 2, (side, sides, rows_in), micros=0.5)


def second_planes(planes, source, rows_ref, low, high, porosity_ref, label_ref, post, heat, aux, moved):
    _, depth, rows, columns = source.shape
    far = depth - 1

    def body(x):
        for i in range(COUNT):
            value = moved_population(
                source, i, x, 1, row_slot, rows_ref, lambda: low(PLUS.index(i)), lambda: high(MINUS.index(i)), far
            )
            if i < 19:
                moved[i] = value
            else:
                heat[i - 19, x] = value
        for r, c in tiles(rows, columns):
            porosity = porosity_ref[x, r, c]
            inlet = label_ref[x, r, c] == 1
            pops = [moved[i, r, c] for i in range(19)]
            density, velocity = moments(pops, porosity)
            for i, value in enumerate((density,) + velocity):
                aux[i, x, r, c] = value
            warm = [heat[i, x, r, c] for i in range(7)]
            for i, value in enumerate(collide_heat(warm, velocity, porosity, inlet)):
                post[i, x, r, c] = value

    for_planes(planes, body)


def second_interior(source, rows_in, porosity, label, adjoint, heat_adjoint):
    cells = label.shape
    depth, rows, columns = cells
    far = depth - 1

    def kernel(source, rows_ref, porosity, label, adj_in, hadj_in, post, heat, aux, adj, hadj, moved, sem):
        copies = [pltpu.make_async_copy(adj_in, adj, sem.at[0]), pltpu.make_async_copy(hadj_in, hadj, sem.at[1])]
        for copy in copies:
            copy.start()
        second_planes(range(1, far), source, rows_ref, None, None, porosity, label, post, heat, aux, moved)
        for copy in copies:
            copy.wait()

    return call(
        kernel,
        "second_interior",
        "vvvvhh",
        [vmem(7, *cells), vmem(7, *cells), vmem(4, *cells), vmem(19, *cells), vmem(7, *cells)],
        (source, rows_in, porosity, label, adjoint, heat_adjoint),
        scratch=[pltpu.VMEM((19, rows, columns), F32), pltpu.SemaphoreType.DMA((2,))],
        micros=3.0,
    )


def second_boundary(side, source, rows_in, face_a, face_b, porosity, label, adjoint, heat_adjoint, post, heat, aux):
    cells = label.shape
    depth, rows, columns = cells
    far = depth - 1
    last = rows - 1

    def kernel(side_ref, source, rows_ref, a_ref, b_ref, porosity, label, adj, hadj, post_in, heat_in, aux_in,
               post, heat, aux, msg, moved):
        even = side_ref[0] == 0

        def low(slot):
            return pick(even, b_ref[slot], a_ref[slot])

        def high(slot):
            return pick(even, a_ref[slot], b_ref[slot])

        second_planes((0, far), source, rows_ref, low, high, porosity, label, post, heat, aux, moved)

        def rows_of(x, carry):
            here = pl.ds(x, 1)
            msg[0, here, :] = post[3, x, last : last + 1, :]
            msg[1, here, :] = post[4, x, 0:1, :]
            for i in FYPLUS:
                msg[adjoint_slot(i), here, :] = adj[i, x, 0:1, :]
            for i in FYMINUS:
                msg[adjoint_slot(i), here, :] = adj[i, x, last : last + 1, :]
            msg[15, here, :] = jnp.where(label[x, 0:1, :] == 2, 1.0, 0.0)
            msg[16, here, :] = jnp.where(label[x, last : last + 1, :] == 2, 1.0, 0.0)
            for slot, y in ((0, 0), (1, last)):
                row = slice(y, y + 1)
                total = post[4, x, 1:2, :] if y == 0 else post[3, x, last - 1 : last, :]
                total = total + post[0, x, row, :]
                total = total + shift_z(post[5, x, row, :], 1) + shift_z(post[6, x, row, :], -1)
                left = post[1, jnp.maximum(x - 1, 0), row, :]
                right = post[2, jnp.minimum(x + 1, far), row, :]
                total = total + pick(x == 0, jnp.zeros_like(left), left) + pick(x == far, jnp.zeros_like(right), right)
                msg[2 + slot, here, :] = hadj[3 + slot, x, row, :] + jnp.where(label[x, row, :] == 2, total, 0.0)
            return carry

        lax.fori_loop(0, depth, rows_of, 0)
        msg[4] = jnp.zeros((depth, columns), F32)
        msg[4, 0:1, :] = post[1, far, 0:1, :]
        msg[4, 1:2, :] = post[1, far, last : last + 1, :]
        msg[4, 2:3, :] = post[2, 0, 0:1, :]
        msg[4, 3:4, :] = post[2, 0, last : last + 1, :]

    return call(
        kernel,
        "second_boundary",
        "svvvvvvvvvvv",
        [vmem(7, *cells), vmem(7, *cells), vmem(4, *cells), vmem(17, depth, columns)],
        (side, source, rows_in, face_a, face_b, porosity, label, adjoint, heat_adjoint, post, heat, aux),
        scratch=[pltpu.VMEM((19, rows, columns), F32)],
        aliases={9: 0, 10: 1, 11: 2},
        micros=1.5,
    )


def heat_faces(side, post, heat_adjoint, label, rows_in):
    depth, rows, columns = label.shape
    far = depth - 1

    def kernel(side_ref, post, hadj, label, rows_ref, a_ref, b_ref):
        even = side_ref[0] == 0

        def partial(x, other):
            total = post[0, x] + other
            total = total + shift_y(post[3, x], 1, rows_ref[0, x : x + 1, :])
            total = total + shift_y(post[4, x], -1, rows_ref[1, x : x + 1, :])
            return total + shift_z(post[5, x], 1) + shift_z(post[6, x], -1)

        high_seed = hadj[2, far] + jnp.where(label[far] == 2, partial(far, post[1, far - 1]), 0.0)
        low_seed = hadj[1, 0] + jnp.where(label[0] == 2, partial(0, post[2, 1]), 0.0)
        high_face, low_face = post[1, far], post[2, 0]
        a_ref[0:rows] = pick(even, high_face, low_face)
        b_ref[0:rows] = pick(even, low_face, high_face)
        a_ref[rows : 2 * rows] = pick(even, high_seed, low_seed)
        b_ref[rows : 2 * rows] = pick(even, low_seed, high_seed)
        place = lax.broadcasted_iota(jnp.int32, (8, columns), 0)

        def spread(slot):
            return jnp.broadcast_to(rows_ref[4, slot : slot + 1, :], (8, columns))

        high_rows = jnp.where(place == 0, spread(1), spread(0))
        low_rows = jnp.where(place == 0, spread(3), spread(2))
        a_ref[2 * rows : 2 * rows + 8] = pick(even, high_rows, low_rows)
        b_ref[2 * rows : 2 * rows + 8] = pick(even, low_rows, high_rows)

    shape = (2 * rows + 8, columns)
    return call(
        kernel, "heat_faces", "svvvv", [vmem(*shape)] * 2, (side, post, heat_adjoint, label, rows_in), micros=0.5
    )


def adjoint_faces(side, adjoint, label, rows_in, after):
    depth, rows, columns = label.shape
    far = depth - 1

    def kernel(side_ref, adj, label, rows_ref, after_ref, a_ref, b_ref):
        even = side_ref[0] == 0
        for slot in range(5):
            i, j = FPLUS[slot], FMINUS[slot]
            low, high = adj[i, 0], adj[j, far]
            if VEL[i][1]:
                low = shift_y(low, -VEL[i][1], rows_ref[adjoint_slot(i), 0:1, :])
                high = shift_y(high, -VEL[j][1], rows_ref[adjoint_slot(j), far : far + 1, :])
            a_ref[slot] = pick(even, high, low)
            b_ref[slot] = pick(even, low, high)
        low = jnp.where(label[0] == 2, 1.0, 0.0)
        high = jnp.where(label[far] == 2, 1.0, 0.0)
        a_ref[5] = pick(even, high, low)
        b_ref[5] = pick(even, low, high)

    face = (6, rows, columns)
    return call(
        kernel, "adjoint_faces", "svvvv", [vmem(*face)] * 2, (side, adjoint, label, rows_in, after), micros=1.0
    )


def second_adjoint(planes, name, side, fixed, arrived, state, micros):
    adj, hadj, post, heat, aux, porosity, label, rows_in = fixed
    cells = label.shape
    depth, rows, columns = cells
    far = depth - 1
    last = rows - 1
    first = state is None
    boundary = isinstance(planes, tuple)
    lit_planes = range(planes[0] - 1, planes[-1] + 2) if first else ((0, far) if boundary else ())

    def kernel(*refs):
        refs = list(refs)
        side_ref, adj, hadj, post, heat, aux, porosity, label, rows_ref = refs[:9]
        refs = refs[9:]
        if boundary:
            fa, fb, sa, sb = refs[:4]
        refs = refs[len(arrived) :]
        if not first:
            refs = refs[3:]
        lam, sens, lit = refs[:3]
        msg = refs[3] if boundary else None
        sides = refs[4] if boundary else None
        moved = refs[-1]
        even = side_ref[0] == 0
        tail = 2 * rows

        def from_left(where):
            return pick(even, sb[where], sa[where])

        def from_right(where):
            return pick(even, sa[where], sb[where])

        def light(x):
            here = pl.ds(x, 1)
            before, after = neighbour(x, -1, far), neighbour(x, 1, far)
            total = post[0, x]
            total = total + (from_left(slice(0, rows)) if before is None else post[1, before])
            total = total + (from_right(slice(0, rows)) if after is None else post[2, after])
            total = total + shift_y(post[3, x], 1, rows_ref[0, here, :])
            total = total + shift_y(post[4, x], -1, rows_ref[1, here, :])
            total = total + shift_z(post[5, x], 1) + shift_z(post[6, x], -1)
            lit[x] = jnp.where(label[x] == 2, total, 0.0)

        if lit_planes:
            for_planes(lit_planes, light)

        def body(x):
            here = pl.ds(x, 1)
            before, after = neighbour(x, -1, far), neighbour(x, 1, far)
            glow = lit[x]
            moved[19] = hadj[0, x] + glow
            if after is None:
                moved[20] = from_right(slice(rows, tail)) + pick(even, fa[5], fb[5]) * post[1, far]
            else:
                moved[20] = hadj[1, after] + lit[after]
            if before is None:
                moved[21] = from_left(slice(rows, tail)) + pick(even, fb[5], fa[5]) * post[2, 0]
            else:
                moved[21] = hadj[2, before] + lit[before]
            above = post[3, x, last : last + 1, :]
            below = post[4, x, 0:1, :]
            if before is None:
                above = above + from_left(slice(tail + 1, tail + 2))
                below = below + from_left(slice(tail, tail + 1))
            if after is None:
                above = above + from_right(slice(tail + 1, tail + 2))
                below = below + from_right(slice(tail, tail + 1))
            moved[22] = shift_y(hadj[3, x] + glow, -1, rows_ref[2, here, :] + rows_ref[15, here, :] * above)
            moved[23] = shift_y(hadj[4, x] + glow, 1, rows_ref[3, here, :] + rows_ref[16, here, :] * below)
            moved[24] = shift_z(hadj[5, x] + glow, -1)
            moved[25] = shift_z(hadj[6, x] + glow, 1)
            for i in range(19):
                moved[i] = moved_population(
                    adj,
                    i,
                    x,
                    -1,
                    adjoint_slot,
                    rows_ref,
                    lambda: pick(even, fb[FMINUS.index(i)], fa[FMINUS.index(i)]),
                    lambda: pick(even, fa[FPLUS.index(i)], fb[FPLUS.index(i)]),
                    far,
                )
            for r, c in tiles(rows, columns):
                inlet = label[x, r, c] == 1
                density, ux, uy, uz = (aux[i, x, r, c] for i in range(4))
                warm = [heat[i, x, r, c] for i in range(7)]
                mu = [moved[i, r, c] for i in range(19)]
                nu = [moved[19 + i, r, c] for i in range(7)]
                result, result_heat, part = collide_adjoint(
                    density, (ux, uy, uz), warm, porosity[x, r, c], inlet, mu, nu
                )
                for i, value in enumerate(result + result_heat):
                    lam[i, x, r, c] = value
                sens[x, r, c] = part

        for_planes(planes, body)
        if boundary:
            for slot in range(6):
                sides[slot] = lam[PLUS[slot], 0]
                sides[6 + slot] = lam[MINUS[slot], far]

            def rows_of(x, carry):
                here = pl.ds(x, 1)
                for i in YPLUS:
                    msg[row_slot(i), here, :] = lam[i, x, 0:1, :]
                for i in YMINUS:
                    msg[row_slot(i), here, :] = lam[i, x, last : last + 1, :]
                return carry

            lax.fori_loop(0, depth, rows_of, 0)

    outs = [vmem(COUNT, *cells), vmem(*cells), vmem(*cells)]
    if boundary:
        outs += [vmem(12, depth, columns), vmem(12, rows, columns)]
    args = (side,) + fixed + arrived + (() if first else state)
    base = len(args) - 3
    return call(
        kernel,
        name,
        "s" + "v" * (len(args) - 1),
        outs,
        args,
        scratch=[pltpu.VMEM((COUNT, rows, columns), F32)],
        aliases=None if first else {base: 0, base + 1: 1, base + 2: 2},
        micros=micros,
    )


def multiply(first, second):
    return jnp.dot(first, second, precision=lax.Precision.HIGHEST, preferred_element_type=F32)


def first_adjoint(planes, name, side, lam, rows_in, fixed, arrived, state, waves, micros):
    aux, heat, porosity, label, chosen, sens_one = fixed
    cells = label.shape
    depth, rows, columns = cells
    far = depth - 1
    half = columns // 2
    first = state is None
    count = len(planes)

    def kernel(*refs):
        refs = list(refs)
        side_ref, lam, rows_ref, aux, heat, porosity, label, chosen, sens_ref, waves_ref = refs[:10]
        refs = refs[10:]
        if not first:
            a_ref, b_ref = refs[:2]
            refs = refs[6:]
        fluid_out, heat_out, own, other, moved, out, total, sem = refs
        even = side_ref[0] == 0
        core = side_ref[1]

        def place(x):
            return planes.index(x) if isinstance(x, int) else x - planes[0]

        def stores(x):
            n = place(x)
            return (
                pltpu.make_async_copy(out.at[0:19, n], fluid_out.at[:, x], sem.at[2 * n]),
                pltpu.make_async_copy(out.at[19:26, n], heat_out.at[:, x], sem.at[2 * n + 1]),
            )

        def body(x):
            n = place(x)
            for i in range(COUNT):
                moved[i] = moved_population(
                    lam,
                    i,
                    x,
                    -1,
                    row_slot,
                    rows_ref,
                    lambda: pick(even, b_ref[MINUS.index(i)], a_ref[MINUS.index(i)]),
                    lambda: pick(even, a_ref[PLUS.index(i)], b_ref[PLUS.index(i)]),
                    far,
                )
            for r, c in tiles(rows, columns):
                inlet = label[x, r, c] == 1
                density, ux, uy, uz = (aux[i, x, r, c] for i in range(4))
                warm = [heat[i, x, r, c] for i in range(7)]
                mu = [moved[i, r, c] for i in range(19)]
                nu = [moved[19 + i, r, c] for i in range(7)]
                result, result_heat, part = collide_adjoint(
                    density, (ux, uy, uz), warm, porosity[x, r, c], inlet, mu, nu
                )
                for i, value in enumerate(result + result_heat):
                    out[i, n, r, c] = value
                total[n, r, c] = jnp.where(chosen[x, r, c] > 0.0, part + sens_ref[x, r, c], 0.0)
            for copy in stores(x):
                copy.start()

        for_planes(planes, body)
        flat = total[...].reshape(count * rows, columns)
        ours = multiply(flat, waves_ref[core]).reshape(count, rows, half)
        theirs = multiply(flat, waves_ref[1 - core]).reshape(count, rows, half)
        for n, x in enumerate(planes):
            own[x] = ours[n]
            other[x] = theirs[n]

        def finish(x):
            for copy in stores(x):
                copy.wait()

        for_planes(planes, finish)

    args = (side, lam, rows_in) + fixed + (waves,)
    if not first:
        args = args + arrived + state
    base = len(args) - 4
    specs = "s" + "v" * (len(args) - 1)
    if not first:
        specs = specs[:base] + "hhvv"
    return call(
        kernel,
        name,
        specs,
        [hbm(19, *cells), hbm(7, *cells), vmem(depth, rows, half), vmem(depth, rows, half)],
        args,
        scratch=[
            pltpu.VMEM((COUNT, rows, columns), F32),
            pltpu.VMEM((COUNT, count, rows, columns), F32),
            pltpu.VMEM((count, rows, columns), F32),
            pltpu.SemaphoreType.DMA((2 * count,)),
        ],
        aliases=None if first else {base + n: n for n in range(4)},
        micros=micros,
    )


def hartley(length):
    index = np.arange(length)
    angle = 2.0 * np.pi * ((index[:, None] * index[None, :]) % length) / length
    return (np.cos(angle) + np.sin(angle)) / np.sqrt(length)


def filter_tables(depth, count_y, count_z):
    half = count_z // 2
    wave_z = hartley(count_z)
    waves = np.stack([wave_z[:, :half], wave_z[:, half:]]).astype(np.float32)
    waves_back = np.stack([wave_z[:half], wave_z[half:]]).astype(np.float32)
    wave_y = np.kron(np.eye(depth), hartley(count_y)).astype(np.float32)
    symbol_y = 2.0 - 2.0 * np.cos(2.0 * np.pi * np.arange(count_y) / count_y)
    symbol_z = 2.0 - 2.0 * np.cos(2.0 * np.pi * np.arange(count_z) / count_z)
    weight = float(RADIUS * RADIUS)
    centre = (1.0 + weight * (2.0 + symbol_y[:, None] + symbol_z[None, :])) / weight
    ratio = 2.0 / (centre + np.sqrt(centre * centre - 4.0))
    peak = 1.0 / (weight * (1.0 / ratio - ratio))
    fields = np.stack([ratio, np.log(ratio) * depth, peak]).astype(np.float32)
    fields = np.stack([fields[:, :, :half], fields[:, :, half:]])
    return waves, waves_back, wave_y, fields


def to_modes(side, own, other, wave_y, fields):
    depth, rows, half = own.shape
    full = 2 * rows

    def kernel(side_ref, own_ref, other_ref, wave_ref, field_ref, modes, ends, both):
        core = side_ref[1]
        for x in range(depth):
            both[x * full : x * full + rows] = own_ref[x]
            both[x * full + rows : (x + 1) * full] = other_ref[x]
        modes[...] = multiply(wave_ref[...], both[...])
        ratio = field_ref[core, 0]
        head = modes[0:full]
        for x in range(1, depth):
            head = head * ratio + modes[x * full : (x + 1) * full]
        ends[0] = head
        tail = modes[(depth - 1) * full : depth * full]
        for x in range(depth - 2, -1, -1):
            tail = tail * ratio + modes[x * full : (x + 1) * full]
        ends[1] = tail

    return call(
        kernel,
        "to_modes",
        "svvvv",
        [vmem(depth * full, half), vmem(2, full, half)],
        (side, own, other, wave_y, fields),
        scratch=[pltpu.VMEM((depth * full, half), F32)],
    )


def join_segments(side, ends, arrived, carry, fields, reach):
    first = carry is None

    def kernel(*refs):
        side_ref, ends_ref, in_ref, field_ref = refs[:4]
        carry_ref = None if first else refs[4]
        ends_out, carry_out = refs[-2:]
        core = side_ref[1]
        index = side_ref[2]
        place = lax.rem(index, reach)
        upper = lax.rem(lax.div(index, reach), 2) == 1
        rate = field_ref[core, 1]
        whole = jnp.exp(rate * float(reach))
        forward = jnp.exp(rate * place.astype(F32))
        backward = jnp.exp(rate * (reach - 1 - place).astype(F32))
        head, tail = ends_ref[0], ends_ref[1]
        head_in, tail_in = in_ref[0], in_ref[1]
        left = pick(upper, forward * head_in, jnp.zeros_like(head))
        right = pick(upper, jnp.zeros_like(head), backward * tail_in)
        carry_out[0] = left if first else carry_ref[0] + left
        carry_out[1] = right if first else carry_ref[1] + right
        ends_out[0] = pick(upper, head + whole * head_in, head_in + whole * head)
        ends_out[1] = pick(upper, tail_in + whole * tail, tail + whole * tail_in)

    args = (side, ends, arrived, fields) + (() if first else (carry,))
    return call(kernel, "join_segments", "s" + "v" * (len(args) - 1), [vmem(*ends.shape)] * 2, args, micros=0.3)


def from_modes(side, modes, ends, carry, wave_y, fields, depth, parts):
    half = modes.shape[1]
    full = modes.shape[0] // depth
    rows = full // 2

    def kernel(side_ref, modes_ref, ends_ref, carry_ref, wave_ref, field_ref, own, other, solved):
        core = side_ref[1]
        index = side_ref[2]
        ratio, rate, peak = field_ref[core, 0], field_ref[core, 1], field_ref[core, 2]
        around = 1.0 / (1.0 - jnp.exp(rate * float(parts)))
        left = carry_ref[0] + jnp.exp(rate * index.astype(F32)) * around * ends_ref[0]
        right = carry_ref[1] + jnp.exp(rate * (parts - 1 - index).astype(F32)) * around * ends_ref[1]
        run = left
        for x in range(depth):
            run = run * ratio + modes_ref[x * full : (x + 1) * full]
            solved[x * full : (x + 1) * full] = run
        run = right
        for x in range(depth - 1, -1, -1):
            run = run * ratio
            solved[x * full : (x + 1) * full] = peak * (solved[x * full : (x + 1) * full] + run)
            run = run + modes_ref[x * full : (x + 1) * full]
        back = multiply(wave_ref[...], solved[...])
        for x in range(depth):
            own[x * rows : (x + 1) * rows] = back[x * full : x * full + rows]
            other[x * rows : (x + 1) * rows] = back[x * full + rows : (x + 1) * full]

    flat = (depth * rows, half)
    return call(
        kernel,
        "from_modes",
        "svvvvv",
        [vmem(*flat)] * 2,
        (side, modes, ends, carry, wave_y, fields),
        scratch=[pltpu.VMEM(modes.shape, F32)],
    )


def last_transform(side, own, other, waves_back, depth):
    flat, half = own.shape
    rows = flat // depth

    def kernel(side_ref, own_ref, other_ref, wave_ref, out_ref, out, sem):
        core = side_ref[1]
        result = multiply(own_ref[...], wave_ref[core]) + multiply(other_ref[...], wave_ref[1 - core])
        out[...] = result.reshape(depth, rows, 2 * half)
        copy = pltpu.make_async_copy(out, out_ref, sem.at[0])
        copy.start()
        copy.wait()

    shape = (depth, rows, 2 * half)
    return call(
        kernel,
        "last_transform",
        "svvv",
        [hbm(*shape)],
        (side, own, other, waves_back),
        scratch=[pltpu.VMEM(shape, F32), pltpu.SemaphoreType.DMA((1,))],
    )


def per_device(fluid_state, heat_state, design, cell_type, boundary, fluid_adjoint, heat_adjoint):
    depth, rows, columns = design.shape
    far = depth - 1
    parts = lax.axis_size("gx")
    index = lax.axis_index("gx")
    side = jnp.stack([index % 2, lax.axis_index("gy"), index]).astype(jnp.int32)
    waves, waves_back, wave_y, fields = filter_tables(depth, 2 * rows, columns)

    pairs_a = [(i, i ^ 1) for i in range(parts)]
    pairs_b = [(i, (i + 1) % parts if i % 2 else (i - 1) % parts) for i in range(parts)]

    def across(value):
        return lax.ppermute(value, "gy", [(0, 1), (1, 0)])

    def sideways(first, second):
        second = lax.ppermute(second, "gx", pairs_b)
        first = lax.ppermute(first, "gx", pairs_a)
        return first, second

    fluid_state, heat_state, design, cell_type, boundary, fluid_adjoint, heat_adjoint = (
        in_hbm(value)
        for value in (fluid_state, heat_state, design, cell_type, boundary, fluid_adjoint, heat_adjoint)
    )
    post, heat_zero, aux_zero, porosity, label, chosen, sides, rows_one = first_collision(
        side, fluid_state, heat_state, design, cell_type, boundary
    )
    rows_one = across(rows_one)
    face_a, face_b = crossing_faces("first_faces", side, sides, rows_one, 1)
    face_a, face_b = sideways(face_a, face_b)
    post_one, heat_one, aux_one, adj, hadj = second_interior(
        post, rows_one, porosity, label, fluid_adjoint, heat_adjoint
    )
    post_one, heat_one, aux_one, rows_heat = second_boundary(
        side, post, rows_one, face_a, face_b, porosity, label, adj, hadj, post_one, heat_one, aux_one
    )
    rows_heat = across(rows_heat)
    seed_a, seed_b = heat_faces(side, post_one, hadj, label, rows_heat)
    adj_a, adj_b = adjoint_faces(side, adj, label, rows_heat, seed_a)
    seed_a, seed_b = sideways(seed_a, seed_b)
    adj_a, adj_b = sideways(adj_a, adj_b)
    fixed = (adj, hadj, post_one, heat_one, aux_one, porosity, label, rows_heat)
    state = second_adjoint(range(2, far - 1), "adjoint_inner", side, fixed, (), None, 2.5)
    lam, sens_one, lit, rows_two, sides = second_adjoint(
        (0, 1, far - 1, far), "adjoint_outer", side, fixed, (adj_a, adj_b, seed_a, seed_b), tuple(state), 1.5
    )
    rows_two = across(rows_two)
    face_a, face_b = crossing_faces("costate_faces", side, sides, rows_two, -1)
    face_a, face_b = sideways(face_a, face_b)
    fixed = (aux_zero, heat_zero, porosity, label, chosen, sens_one)
    state = first_adjoint(range(1, far), "costate_inner", side, lam, rows_two, fixed, None, None, waves, 5.0)
    fluid_costate, heat_costate, own, other = first_adjoint(
        (0, far), "costate_outer", side, lam, rows_two, fixed, (face_a, face_b), tuple(state), waves, 1.5
    )
    other = across(other)
    modes, ends = to_modes(side, own, other, wave_y, fields)
    carry = None
    reach = 1
    while reach < parts:
        arrived = lax.ppermute(ends, "gx", [(i, i ^ reach) for i in range(parts)])
        ends, carry = join_segments(side, ends, arrived, carry, fields, reach)
        reach = 2 * reach
    own, other = from_modes(side, modes, ends, carry, wave_y, fields, depth, parts)
    other = across(other)
    return (fluid_costate, heat_costate, last_transform(side, own, other, waves_back, depth))


def solution(mesh):
    return jax.shard_map(
        per_device,
        mesh=mesh,
        in_specs=(
            P(None, ("case", "gx"), "gy", None),
            P(None, ("case", "gx"), "gy", None),
            P(("case", "gx"), "gy", None),
            P(("case", "gx"), "gy", None),
            P(("case", "gx"), "gy", None),
            P(None, ("case", "gx"), "gy", None),
            P(None, ("case", "gx"), "gy", None),
        ),
        out_specs=(
            P(None, ("case", "gx"), "gy", None),
            P(None, ("case", "gx"), "gy", None),
            P(("case", "gx"), "gy", None),
        ),
        check_vma=False,
    )
```

```python
import numpy as np
import jax
import jax.numpy as jnp
from jax import lax
from jax.experimental import pallas as pl
from jax.experimental.pallas import tpu as pltpu
from jax.sharding import PartitionSpec as P

RADIUS = 4

fluid_vel = [
    (0, 0, 0),
    (1, 0, 0),
    (-1, 0, 0),
    (0, 1, 0),
    (0, -1, 0),
    (0, 0, 1),
    (0, 0, -1),
    (1, 1, 0),
    (-1, -1, 0),
    (1, -1, 0),
    (-1, 1, 0),
    (1, 0, 1),
    (-1, 0, -1),
    (1, 0, -1),
    (-1, 0, 1),
    (0, 1, 1),
    (0, -1, -1),
    (0, 1, -1),
    (0, -1, 1),
]
fluid_wts = [1.0 / 3.0] + [1.0 / 18.0] * 6 + [1.0 / 36.0] * 12
inlet_speed = 0.05
inlet_eq = [
    weight
    * (
        1.0
        + 3.0 * inlet_speed * entry[2]
        + 4.5 * (inlet_speed * entry[2]) ** 2
        - 1.5 * inlet_speed**2
    )
    for entry, weight in zip(fluid_vel, fluid_wts)
]

VEL = fluid_vel + fluid_vel[:7]
COUNT = len(VEL)
PLUS = [i for i in range(COUNT) if VEL[i][0] == 1]
MINUS = [i for i in range(COUNT) if VEL[i][0] == -1]
YPLUS = [i for i in range(COUNT) if VEL[i][1] == 1]
YMINUS = [i for i in range(COUNT) if VEL[i][1] == -1]
FPLUS = [i for i in PLUS if i < 19]
FMINUS = [i for i in MINUS if i < 19]
FYPLUS = [i for i in YPLUS if i < 19]
FYMINUS = [i for i in YMINUS if i < 19]

VMEM_BYTES = 24 * 1024 * 1024
F32 = jnp.float32


def params():
    return pltpu.CompilerParams(vmem_limit_bytes=VMEM_BYTES)


def cost(micros):
    return pl.CostEstimate(flops=0, bytes_accessed=int(micros * 1e4), transcendentals=0)


def shift_y(value, step, ghost):
    if step == 0:
        return value
    rows = value.shape[0]
    moved = pltpu.roll(value, step % rows, 0)
    place = lax.broadcasted_iota(jnp.int32, value.shape, 0)
    edge = 0 if step > 0 else rows - 1
    return jnp.where(place == edge, jnp.broadcast_to(ghost, value.shape), moved)


def shift_z(value, step):
    if step == 0:
        return value
    return pltpu.roll(value, step % value.shape[1], 1)


def pick(flag, first, second):
    return jnp.where(flag, first, second)


def tiles(rows, columns):
    return [
        (slice(r, r + 8), slice(c, c + 128)) for r in range(0, rows, 8) for c in range(0, columns, 128)
    ]


def porosity_of(design, kind):
    return jnp.where(kind == 2, design, jnp.where(kind == 1, 0.0, 1.0))


def heat_rate_of(porosity):
    return 1.0 / (0.55 + 0.9 * (1.0 - porosity))


def moments(pops, porosity):
    density = pops[0]
    for value in pops[1:]:
        density = density + value
    diff = {i: pops[i] - pops[i + 1] for i in range(1, 19, 2)}
    flux_x = diff[1] + diff[7] + diff[9] + diff[11] + diff[13]
    flux_y = diff[3] + diff[7] - diff[9] + diff[15] + diff[17]
    flux_z = diff[5] + diff[11] - diff[13] + diff[15] - diff[17]
    inverse = (0.1 + porosity) / (density * (0.5 + 0.6 * porosity))
    return density, (flux_x * inverse, flux_y * inverse, flux_z * inverse)


def along(entry, vector):
    total = None
    for part, value in zip(entry, vector):
        if part == 0:
            continue
        if total is None:
            total = value if part == 1 else -value
        else:
            total = total + value if part == 1 else total - value
    return total


def collide_fluid(pops, density, velocity, inlet):
    speed = velocity[0] * velocity[0] + velocity[1] * velocity[1] + velocity[2] * velocity[2]
    scaled = 1.25 * density
    base = scaled - 1.5 * scaled * speed
    result = [jnp.where(inlet, inlet_eq[0], base * (1.0 / 3.0) - 0.25 * pops[0])]
    for i in range(1, 19, 2):
        weight = fluid_wts[i]
        part = along(VEL[i], velocity)
        flow = scaled * part
        even = weight * base + (4.5 * weight) * (flow * part)
        odd = (3.0 * weight) * flow
        result.append(jnp.where(inlet, inlet_eq[i], even + odd - 0.25 * pops[i]))
        result.append(jnp.where(inlet, inlet_eq[i + 1], even - odd - 0.25 * pops[i + 1]))
    return result


def collide_heat(pops, velocity, porosity, inlet):
    temper = pops[0]
    for value in pops[1:]:
        temper = temper + value
    rate = heat_rate_of(porosity)
    keep = 1.0 - rate
    warm = rate * temper
    base = warm + (1.0 - porosity)
    result = [jnp.where(inlet, 0.0, keep * pops[0] + 0.25 * base)]
    for axis in range(3):
        i = 1 + 2 * axis
        odd = 0.5 * (warm * velocity[axis])
        even = 0.125 * base
        result.append(jnp.where(inlet, 0.0, keep * pops[i] + (even + odd)))
        result.append(jnp.where(inlet, 0.0, keep * pops[i + 1] + (even - odd)))
    return result


def collide_adjoint(density, velocity, heat, porosity, inlet, mu, nu):
    ux, uy, uz = velocity
    mu = [jnp.where(inlet, 0.0, value) for value in mu]
    nu = [jnp.where(inlet, 0.0, value) for value in nu]
    even = {i: mu[i] + mu[i + 1] for i in range(1, 19, 2)}
    odd = {i: mu[i] - mu[i + 1] for i in range(1, 19, 2)}
    wa, wb = 1.0 / 18.0, 1.0 / 36.0
    xy_sum, xz_sum, yz_sum = even[7] + even[9], even[11] + even[13], even[15] + even[17]
    m0 = mu[0] * (1.0 / 3.0) + wa * (even[1] + even[3] + even[5]) + wb * (xy_sum + xz_sum + yz_sum)
    m1x = wa * odd[1] + wb * (odd[7] + odd[9] + odd[11] + odd[13])
    m1y = wa * odd[3] + wb * (odd[7] - odd[9] + odd[15] + odd[17])
    m1z = wa * odd[5] + wb * (odd[11] - odd[13] + odd[15] - odd[17])
    mxx = wa * even[1] + wb * (xy_sum + xz_sum)
    myy = wa * even[3] + wb * (xy_sum + yz_sum)
    mzz = wa * even[5] + wb * (xz_sum + yz_sum)
    mxy = wb * (even[7] - even[9])
    mxz = wb * (even[11] - even[13])
    myz = wb * (even[15] - even[17])
    vx = mxx * ux + mxy * uy + mxz * uz
    vy = mxy * ux + myy * uy + myz * uz
    vz = mxz * ux + myz * uy + mzz * uz
    speed = ux * ux + uy * uy + uz * uz
    slope = (
        m0 * (1.0 - 1.5 * speed)
        + 3.0 * (ux * m1x + uy * m1y + uz * m1z)
        + 4.5 * (ux * vx + uy * vy + uz * vz)
    )
    rate = heat_rate_of(porosity)
    keep = 1.0 - rate
    temper = heat[0]
    for value in heat[1:]:
        temper = temper + value
    n0 = 0.25 * nu[0] + 0.125 * (nu[1] + nu[2] + nu[3] + nu[4] + nu[5] + nu[6])
    n1x, n1y, n1z = (0.125 * (nu[i] - nu[i + 1]) for i in (1, 3, 5))
    warm = 4.0 * rate * temper
    scaled = 3.75 * density
    bar_x = scaled * (m1x - m0 * ux + 3.0 * vx) + warm * n1x
    bar_y = scaled * (m1y - m0 * uy + 3.0 * vy) + warm * n1y
    bar_z = scaled * (m1z - m0 * uz + 3.0 * vz) + warm * n1z
    work = bar_x * ux + bar_y * uy + bar_z * uz
    ramp = 0.1 + porosity
    drag = 0.5 + 0.6 * porosity
    over = 1.0 / (density * drag)
    inverse = ramp * over
    b = (bar_x * inverse, bar_y * inverse, bar_z * inverse)
    a = 1.25 * slope - work * (drag * over)
    lam = [a - 0.25 * mu[0]]
    for i in range(1, 19, 2):
        part = along(VEL[i], b)
        lam.append((a + part) - 0.25 * mu[i])
        lam.append((a - part) - 0.25 * mu[i + 1])
    pull = n0 + 4.0 * (ux * n1x + uy * n1y + uz * n1z)
    a_heat = rate * pull
    lam_heat = [keep * value + a_heat for value in nu]
    dot = nu[0] * heat[0]
    for first, second in zip(nu[1:], heat[1:]):
        dot = dot + first * second
    sens = work * (0.44 / (ramp * drag)) - n0 + (0.9 * rate * rate) * (temper * pull - dot)
    return lam, lam_heat, sens


IN_VMEM = pl.BlockSpec(memory_space=pltpu.VMEM)
IN_HBM = pl.BlockSpec(memory_space=pltpu.HBM)


def vmem(*shape):
    return pltpu.VMEM(shape, F32)


def hbm(*shape):
    return pltpu.HBM(shape, F32)


def in_hbm(value):
    return pltpu.with_memory_space_constraint(value, pltpu.HBM)


def call(kernel, name, specs, outs, args, scratch=(), aliases=None, micros=1.0):
    spec_of = {"v": IN_VMEM, "h": IN_HBM}
    single = len(outs) == 1
    args = [
        pltpu.with_memory_space_constraint(value, pltpu.VMEM) if letter == "v" else value
        for letter, value in zip(specs, args)
    ]
    out_specs = [IN_HBM if out.memory_space == pltpu.HBM else IN_VMEM for out in outs]
    return pl.pallas_call(
        kernel,
        in_specs=[spec_of[letter] for letter in specs],
        out_specs=out_specs[0] if single else out_specs,
        out_shape=outs[0] if single else outs,
        scratch_shapes=list(scratch),
        input_output_aliases=aliases or {},
        compiler_params=params(),
        cost_estimate=cost(micros),
        name=name,
    )(*args)


def row_slot(i):
    return YPLUS.index(i) if VEL[i][1] > 0 else 6 + YMINUS.index(i)


def adjoint_slot(i):
    return 5 + FYPLUS.index(i) if VEL[i][1] > 0 else 10 + FYMINUS.index(i)


def for_planes(planes, body):
    if isinstance(planes, tuple):
        for x in planes:
            body(x)
    else:

        def step(x, carry):
            body(x)
            return carry

        lax.fori_loop(planes[0], planes[-1] + 1, step, 0)


def neighbour(x, step, far):
    plane = x + step
    if isinstance(x, int) and (plane < 0 or plane > far):
        return None
    return plane


def moved_population(source, i, x, direction, slot_of, rows_ref, low, high, far):
    step = tuple(direction * part for part in VEL[i])
    plane = neighbour(x, -step[0], far)
    if plane is None:
        value = low() if step[0] == 1 else high()
    else:
        value = source[i, plane]
        if step[1]:
            value = shift_y(value, step[1], rows_ref[slot_of(i), pl.ds(plane, 1), :])
    return shift_z(value, step[2])


def first_collision(fluid, heat, design, kind, label):
    cells = design.shape
    depth, rows, columns = cells
    far = depth - 1
    last = rows - 1

    def kernel(fluid_in, heat_in, design_in, kind_in, label_in, post, heat, aux, porosity, label, chosen,
               sides, msg, design, kind, sem):
        fields = (
            pltpu.make_async_copy(design_in, design, sem.at[0]),
            pltpu.make_async_copy(kind_in, kind, sem.at[1]),
            pltpu.make_async_copy(label_in, label, sem.at[2]),
        )

        def loads(x):
            return (
                pltpu.make_async_copy(fluid_in.at[:, x], post.at[0:19, x], sem.at[3 + 2 * x]),
                pltpu.make_async_copy(heat_in.at[:, x], heat.at[:, x], sem.at[4 + 2 * x]),
            )

        for copy in fields:
            copy.start()
        for x in range(depth):
            for copy in loads(x):
                copy.start()
        for copy in fields:
            copy.wait()

        def body(x):
            here = pl.ds(x, 1)
            kinds = kind[x]
            porosity[x] = porosity_of(design[x], kinds)
            chosen[x] = jnp.where(kinds == 2, 1.0, 0.0)
            for copy in loads(x):
                copy.wait()
            for r, c in tiles(rows, columns):
                phi = porosity[x, r, c]
                inlet = label[x, r, c] == 1
                pops = [post[i, x, r, c] for i in range(19)]
                density, velocity = moments(pops, phi)
                for i, value in enumerate((density,) + velocity):
                    aux[i, x, r, c] = value
                warm = [heat[i, x, r, c] for i in range(7)]
                result = collide_fluid(pops, density, velocity, inlet) + collide_heat(warm, velocity, phi, inlet)
                for i, value in enumerate(result):
                    post[i, x, r, c] = value
            for i in YPLUS:
                msg[row_slot(i), here, :] = post[i, x, last : last + 1, :]
            for i in YMINUS:
                msg[row_slot(i), here, :] = post[i, x, 0:1, :]

        for_planes(range(depth), body)
        for slot in range(6):
            sides[slot] = post[PLUS[slot], far]
            sides[6 + slot] = post[MINUS[slot], 0]

    return call(
        kernel,
        "first_collision",
        "hhhhh",
        [
            vmem(COUNT, *cells),
            vmem(7, *cells),
            vmem(4, *cells),
            vmem(*cells),
            pltpu.VMEM(cells, jnp.int32),
            vmem(*cells),
            vmem(12, rows, columns),
            vmem(12, depth, columns),
        ],
        (fluid, heat, design, kind, label),
        scratch=[pltpu.VMEM(cells, F32), pltpu.VMEM(cells, jnp.int32), pltpu.SemaphoreType.DMA((3 + 2 * depth,))],
        micros=2.0,
    )


def crossing_faces(name, sides, rows_in, direction):
    _, rows, columns = sides.shape
    far = rows_in.shape[1] - 1
    place, other = (far, 0) if direction == 1 else (0, far)

    def kernel(sides_ref, rows_ref, a_ref, b_ref):
        even = lax.rem(lax.axis_index("gx"), 2) == 0
        for slot in range(6):
            i, j = PLUS[slot], MINUS[slot]
            plus, minus = sides_ref[slot], sides_ref[6 + slot]
            if VEL[i][1]:
                plus = shift_y(plus, direction * VEL[i][1], rows_ref[row_slot(i), place : place + 1, :])
                minus = shift_y(minus, direction * VEL[j][1], rows_ref[row_slot(j), other : other + 1, :])
            high, low = (plus, minus) if direction == 1 else (minus, plus)
            a_ref[slot] = pick(even, high, low)
            b_ref[slot] = pick(even, low, high)

    return call(kernel, name, "vv", [vmem(6, rows, columns)] * 2, (sides, rows_in), micros=0.5)


def second_planes(planes, source, rows_ref, low, high, porosity_ref, label_ref, post, heat, aux, moved):
    _, depth, rows, columns = source.shape
    far = depth - 1

    def body(x):
        for i in range(COUNT):
            value = moved_population(
                source, i, x, 1, row_slot, rows_ref, lambda: low(PLUS.index(i)), lambda: high(MINUS.index(i)), far
            )
            if i < 19:
                moved[i] = value
            else:
                heat[i - 19, x] = value
        for r, c in tiles(rows, columns):
            porosity = porosity_ref[x, r, c]
            inlet = label_ref[x, r, c] == 1
            pops = [moved[i, r, c] for i in range(19)]
            density, velocity = moments(pops, porosity)
            for i, value in enumerate((density,) + velocity):
                aux[i, x, r, c] = value
            warm = [heat[i, x, r, c] for i in range(7)]
            for i, value in enumerate(collide_heat(warm, velocity, porosity, inlet)):
                post[i, x, r, c] = value

    for_planes(planes, body)


def second_interior(source, rows_in, porosity, label):
    cells = label.shape
    depth, rows, columns = cells
    far = depth - 1

    def kernel(source, rows_ref, porosity, label, post, heat, aux, moved):
        second_planes(range(1, far), source, rows_ref, None, None, porosity, label, post, heat, aux, moved)

    return call(
        kernel,
        "second_interior",
        "vvvv",
        [vmem(7, *cells), vmem(7, *cells), vmem(4, *cells)],
        (source, rows_in, porosity, label),
        scratch=[pltpu.VMEM((19, rows, columns), F32)],
        micros=3.0,
    )


def second_boundary(source, rows_in, face_a, face_b, porosity, label, adjoint, heat_adjoint, post, heat, aux):
    cells = label.shape
    depth, rows, columns = cells
    far = depth - 1
    last = rows - 1

    def kernel(source, rows_ref, a_ref, b_ref, porosity, label, adj, hadj, post_in, heat_in, aux_in,
               post, heat, aux, msg, moved):
        even = lax.rem(lax.axis_index("gx"), 2) == 0

        def low(slot):
            return pick(even, b_ref[slot], a_ref[slot])

        def high(slot):
            return pick(even, a_ref[slot], b_ref[slot])

        second_planes((0, far), source, rows_ref, low, high, porosity, label, post, heat, aux, moved)

        def rows_of(x, carry):
            here = pl.ds(x, 1)
            msg[0, here, :] = post[3, x, last : last + 1, :]
            msg[1, here, :] = post[4, x, 0:1, :]
            for i in FYPLUS:
                msg[adjoint_slot(i), here, :] = adj[i, x, 0:1, :]
            for i in FYMINUS:
                msg[adjoint_slot(i), here, :] = adj[i, x, last : last + 1, :]
            msg[15, here, :] = jnp.where(label[x, 0:1, :] == 2, 1.0, 0.0)
            msg[16, here, :] = jnp.where(label[x, last : last + 1, :] == 2, 1.0, 0.0)
            for slot, y in ((0, 0), (1, last)):
                row = slice(y, y + 1)
                total = post[4, x, 1:2, :] if y == 0 else post[3, x, last - 1 : last, :]
                total = total + post[0, x, row, :]
                total = total + shift_z(post[5, x, row, :], 1) + shift_z(post[6, x, row, :], -1)
                left = post[1, jnp.maximum(x - 1, 0), row, :]
                right = post[2, jnp.minimum(x + 1, far), row, :]
                total = total + pick(x == 0, jnp.zeros_like(left), left) + pick(x == far, jnp.zeros_like(right), right)
                msg[2 + slot, here, :] = hadj[3 + slot, x, row, :] + jnp.where(label[x, row, :] == 2, total, 0.0)
            return carry

        lax.fori_loop(0, depth, rows_of, 0)
        msg[4] = jnp.zeros((depth, columns), F32)
        msg[4, 0:1, :] = post[1, far, 0:1, :]
        msg[4, 1:2, :] = post[1, far, last : last + 1, :]
        msg[4, 2:3, :] = post[2, 0, 0:1, :]
        msg[4, 3:4, :] = post[2, 0, last : last + 1, :]

    return call(
        kernel,
        "second_boundary",
        "vvvvvvvvvvv",
        [vmem(7, *cells), vmem(7, *cells), vmem(4, *cells), vmem(17, depth, columns)],
        (source, rows_in, face_a, face_b, porosity, label, adjoint, heat_adjoint, post, heat, aux),
        scratch=[pltpu.VMEM((19, rows, columns), F32)],
        aliases={8: 0, 9: 1, 10: 2},
        micros=1.5,
    )


def heat_faces(post, heat_adjoint, label, rows_in):
    depth, rows, columns = label.shape
    far = depth - 1

    def kernel(post, hadj, label, rows_ref, a_ref, b_ref):
        even = lax.rem(lax.axis_index("gx"), 2) == 0

        def partial(x, other):
            total = post[0, x] + other
            total = total + shift_y(post[3, x], 1, rows_ref[0, x : x + 1, :])
            total = total + shift_y(post[4, x], -1, rows_ref[1, x : x + 1, :])
            return total + shift_z(post[5, x], 1) + shift_z(post[6, x], -1)

        high_seed = hadj[2, far] + jnp.where(label[far] == 2, partial(far, post[1, far - 1]), 0.0)
        low_seed = hadj[1, 0] + jnp.where(label[0] == 2, partial(0, post[2, 1]), 0.0)
        high_face, low_face = post[1, far], post[2, 0]
        a_ref[0:rows] = pick(even, high_face, low_face)
        b_ref[0:rows] = pick(even, low_face, high_face)
        a_ref[rows : 2 * rows] = pick(even, high_seed, low_seed)
        b_ref[rows : 2 * rows] = pick(even, low_seed, high_seed)
        place = lax.broadcasted_iota(jnp.int32, (8, columns), 0)

        def spread(slot):
            return jnp.broadcast_to(rows_ref[4, slot : slot + 1, :], (8, columns))

        high_rows = jnp.where(place == 0, spread(1), spread(0))
        low_rows = jnp.where(place == 0, spread(3), spread(2))
        a_ref[2 * rows : 2 * rows + 8] = pick(even, high_rows, low_rows)
        b_ref[2 * rows : 2 * rows + 8] = pick(even, low_rows, high_rows)

    shape = (2 * rows + 8, columns)
    return call(
        kernel, "heat_faces", "vvvv", [vmem(*shape)] * 2, (post, heat_adjoint, label, rows_in), micros=0.5
    )


def adjoint_faces(adjoint, label, rows_in, after):
    depth, rows, columns = label.shape
    far = depth - 1

    def kernel(adj, label, rows_ref, after_ref, a_ref, b_ref):
        even = lax.rem(lax.axis_index("gx"), 2) == 0
        for slot in range(5):
            i, j = FPLUS[slot], FMINUS[slot]
            low, high = adj[i, 0], adj[j, far]
            if VEL[i][1]:
                low = shift_y(low, -VEL[i][1], rows_ref[adjoint_slot(i), 0:1, :])
                high = shift_y(high, -VEL[j][1], rows_ref[adjoint_slot(j), far : far + 1, :])
            a_ref[slot] = pick(even, high, low)
            b_ref[slot] = pick(even, low, high)
        low = jnp.where(label[0] == 2, 1.0, 0.0)
        high = jnp.where(label[far] == 2, 1.0, 0.0)
        a_ref[5] = pick(even, high, low)
        b_ref[5] = pick(even, low, high)

    face = (6, rows, columns)
    return call(
        kernel, "adjoint_faces", "vvvv", [vmem(*face)] * 2, (adjoint, label, rows_in, after), micros=1.0
    )


def second_adjoint(planes, name, fixed, arrived, state, micros):
    adj, hadj, post, heat, aux, porosity, label, rows_in = fixed
    cells = label.shape
    depth, rows, columns = cells
    far = depth - 1
    last = rows - 1
    first = state is None
    boundary = isinstance(planes, tuple)
    lit_planes = range(planes[0] - 1, planes[-1] + 2) if first else ((0, far) if boundary else ())

    def kernel(*refs):
        refs = list(refs)
        adj, hadj, post, heat, aux, porosity, label, rows_ref = refs[:8]
        refs = refs[8:]
        if boundary:
            fa, fb, sa, sb = refs[:4]
        refs = refs[len(arrived) :]
        if not first:
            refs = refs[3:]
        lam, sens, lit = refs[:3]
        msg = refs[3] if boundary else None
        sides = refs[4] if boundary else None
        moved = refs[-1]
        even = lax.rem(lax.axis_index("gx"), 2) == 0
        tail = 2 * rows

        def from_left(where):
            return pick(even, sb[where], sa[where])

        def from_right(where):
            return pick(even, sa[where], sb[where])

        def light(x):
            here = pl.ds(x, 1)
            before, after = neighbour(x, -1, far), neighbour(x, 1, far)
            total = post[0, x]
            total = total + (from_left(slice(0, rows)) if before is None else post[1, before])
            total = total + (from_right(slice(0, rows)) if after is None else post[2, after])
            total = total + shift_y(post[3, x], 1, rows_ref[0, here, :])
            total = total + shift_y(post[4, x], -1, rows_ref[1, here, :])
            total = total + shift_z(post[5, x], 1) + shift_z(post[6, x], -1)
            lit[x] = jnp.where(label[x] == 2, total, 0.0)

        if lit_planes:
            for_planes(lit_planes, light)

        def body(x):
            here = pl.ds(x, 1)
            before, after = neighbour(x, -1, far), neighbour(x, 1, far)
            glow = lit[x]
            moved[19] = hadj[0, x] + glow
            if after is None:
                moved[20] = from_right(slice(rows, tail)) + pick(even, fa[5], fb[5]) * post[1, far]
            else:
                moved[20] = hadj[1, after] + lit[after]
            if before is None:
                moved[21] = from_left(slice(rows, tail)) + pick(even, fb[5], fa[5]) * post[2, 0]
            else:
                moved[21] = hadj[2, before] + lit[before]
            above = post[3, x, last : last + 1, :]
            below = post[4, x, 0:1, :]
            if before is None:
                above = above + from_left(slice(tail + 1, tail + 2))
                below = below + from_left(slice(tail, tail + 1))
            if after is None:
                above = above + from_right(slice(tail + 1, tail + 2))
                below = below + from_right(slice(tail, tail + 1))
            moved[22] = shift_y(hadj[3, x] + glow, -1, rows_ref[2, here, :] + rows_ref[15, here, :] * above)
            moved[23] = shift_y(hadj[4, x] + glow, 1, rows_ref[3, here, :] + rows_ref[16, here, :] * below)
            moved[24] = shift_z(hadj[5, x] + glow, -1)
            moved[25] = shift_z(hadj[6, x] + glow, 1)
            for i in range(19):
                moved[i] = moved_population(
                    adj,
                    i,
                    x,
                    -1,
                    adjoint_slot,
                    rows_ref,
                    lambda: pick(even, fb[FMINUS.index(i)], fa[FMINUS.index(i)]),
                    lambda: pick(even, fa[FPLUS.index(i)], fb[FPLUS.index(i)]),
                    far,
                )
            for r, c in tiles(rows, columns):
                inlet = label[x, r, c] == 1
                density, ux, uy, uz = (aux[i, x, r, c] for i in range(4))
                warm = [heat[i, x, r, c] for i in range(7)]
                mu = [moved[i, r, c] for i in range(19)]
                nu = [moved[19 + i, r, c] for i in range(7)]
                result, result_heat, part = collide_adjoint(
                    density, (ux, uy, uz), warm, porosity[x, r, c], inlet, mu, nu
                )
                for i, value in enumerate(result + result_heat):
                    lam[i, x, r, c] = value
                sens[x, r, c] = part

        for_planes(planes, body)
        if boundary:
            for slot in range(6):
                sides[slot] = lam[PLUS[slot], 0]
                sides[6 + slot] = lam[MINUS[slot], far]

            def rows_of(x, carry):
                here = pl.ds(x, 1)
                for i in YPLUS:
                    msg[row_slot(i), here, :] = lam[i, x, 0:1, :]
                for i in YMINUS:
                    msg[row_slot(i), here, :] = lam[i, x, last : last + 1, :]
                return carry

            lax.fori_loop(0, depth, rows_of, 0)

    outs = [vmem(COUNT, *cells), vmem(*cells), vmem(*cells)]
    if boundary:
        outs += [vmem(12, depth, columns), vmem(12, rows, columns)]
    args = fixed + arrived + (() if first else state)
    base = len(args) - 3
    return call(
        kernel,
        name,
        "v" * len(args),
        outs,
        args,
        scratch=[pltpu.VMEM((COUNT, rows, columns), F32)],
        aliases=None if first else {base: 0, base + 1: 1, base + 2: 2},
        micros=micros,
    )


def multiply(first, second):
    return jnp.dot(first, second, precision=lax.Precision.HIGHEST, preferred_element_type=F32)


def first_adjoint(planes, name, lam, rows_in, fixed, arrived, state, waves, micros):
    aux, heat, porosity, label, chosen, sens_one = fixed
    cells = label.shape
    depth, rows, columns = cells
    far = depth - 1
    half = columns // 2
    first = state is None
    count = len(planes)

    def kernel(*refs):
        refs = list(refs)
        lam, rows_ref, aux, heat, porosity, label, chosen, sens_ref, waves_ref = refs[:9]
        refs = refs[9:]
        if not first:
            a_ref, b_ref = refs[:2]
            refs = refs[6:]
        fluid_out, heat_out, own, other, moved, out, total, sem = refs
        even = lax.rem(lax.axis_index("gx"), 2) == 0
        core = lax.axis_index("gy")

        def place(x):
            return planes.index(x) if isinstance(x, int) else x - planes[0]

        def stores(x):
            n = place(x)
            return (
                pltpu.make_async_copy(out.at[0:19, n], fluid_out.at[:, x], sem.at[2 * n]),
                pltpu.make_async_copy(out.at[19:26, n], heat_out.at[:, x], sem.at[2 * n + 1]),
            )

        def body(x):
            n = place(x)
            for i in range(COUNT):
                moved[i] = moved_population(
                    lam,
                    i,
                    x,
                    -1,
                    row_slot,
                    rows_ref,
                    lambda: pick(even, b_ref[MINUS.index(i)], a_ref[MINUS.index(i)]),
                    lambda: pick(even, a_ref[PLUS.index(i)], b_ref[PLUS.index(i)]),
                    far,
                )
            for r, c in tiles(rows, columns):
                inlet = label[x, r, c] == 1
                density, ux, uy, uz = (aux[i, x, r, c] for i in range(4))
                warm = [heat[i, x, r, c] for i in range(7)]
                mu = [moved[i, r, c] for i in range(19)]
                nu = [moved[19 + i, r, c] for i in range(7)]
                result, result_heat, part = collide_adjoint(
                    density, (ux, uy, uz), warm, porosity[x, r, c], inlet, mu, nu
                )
                for i, value in enumerate(result + result_heat):
                    out[i, n, r, c] = value
                total[n, r, c] = jnp.where(chosen[x, r, c] > 0.0, part + sens_ref[x, r, c], 0.0)
            for copy in stores(x):
                copy.start()

        for_planes(planes, body)
        flat = total[...].reshape(count * rows, columns)
        ours = multiply(flat, waves_ref[core]).reshape(count, rows, half)
        theirs = multiply(flat, waves_ref[1 - core]).reshape(count, rows, half)
        for n, x in enumerate(planes):
            own[x] = ours[n]
            other[x] = theirs[n]

        def finish(x):
            for copy in stores(x):
                copy.wait()

        for_planes(planes, finish)

    args = (lam, rows_in) + fixed + (waves,)
    if not first:
        args = args + arrived + state
    base = len(args) - 4
    specs = "v" * len(args)
    if not first:
        specs = specs[:base] + "hhvv"
    return call(
        kernel,
        name,
        specs,
        [hbm(19, *cells), hbm(7, *cells), vmem(depth, rows, half), vmem(depth, rows, half)],
        args,
        scratch=[
            pltpu.VMEM((COUNT, rows, columns), F32),
            pltpu.VMEM((COUNT, count, rows, columns), F32),
            pltpu.VMEM((count, rows, columns), F32),
            pltpu.SemaphoreType.DMA((2 * count,)),
        ],
        aliases=None if first else {base + n: n for n in range(4)},
        micros=micros,
    )


def hartley(length):
    index = np.arange(length)
    angle = 2.0 * np.pi * ((index[:, None] * index[None, :]) % length) / length
    return (np.cos(angle) + np.sin(angle)) / np.sqrt(length)


def filter_tables(depth, count_y, count_z):
    half = count_z // 2
    wave_z = hartley(count_z)
    waves = np.stack([wave_z[:, :half], wave_z[:, half:]]).astype(np.float32)
    waves_back = np.stack([wave_z[:half], wave_z[half:]]).astype(np.float32)
    wave_y = np.kron(np.eye(depth), hartley(count_y)).astype(np.float32)
    symbol_y = 2.0 - 2.0 * np.cos(2.0 * np.pi * np.arange(count_y) / count_y)
    symbol_z = 2.0 - 2.0 * np.cos(2.0 * np.pi * np.arange(count_z) / count_z)
    weight = float(RADIUS * RADIUS)
    centre = (1.0 + weight * (2.0 + symbol_y[:, None] + symbol_z[None, :])) / weight
    ratio = 2.0 / (centre + np.sqrt(centre * centre - 4.0))
    peak = 1.0 / (weight * (1.0 / ratio - ratio))
    fields = np.stack([ratio, np.log(ratio) * depth, peak]).astype(np.float32)
    fields = np.stack([fields[:, :, :half], fields[:, :, half:]])
    return waves, waves_back, wave_y, fields


def to_modes(own, other, wave_y, fields):
    depth, rows, half = own.shape
    full = 2 * rows

    def kernel(own_ref, other_ref, wave_ref, field_ref, modes, ends, both):
        core = lax.axis_index("gy")
        for x in range(depth):
            both[x * full : x * full + rows] = own_ref[x]
            both[x * full + rows : (x + 1) * full] = other_ref[x]
        modes[...] = multiply(wave_ref[...], both[...])
        ratio = field_ref[core, 0]
        head = modes[0:full]
        for x in range(1, depth):
            head = head * ratio + modes[x * full : (x + 1) * full]
        ends[0] = head
        tail = modes[(depth - 1) * full : depth * full]
        for x in range(depth - 2, -1, -1):
            tail = tail * ratio + modes[x * full : (x + 1) * full]
        ends[1] = tail

    return call(
        kernel,
        "to_modes",
        "vvvv",
        [vmem(depth * full, half), vmem(2, full, half)],
        (own, other, wave_y, fields),
        scratch=[pltpu.VMEM((depth * full, half), F32)],
    )


def join_segments(ends, arrived, carry, fields, reach):
    first = carry is None

    def kernel(*refs):
        ends_ref, in_ref, field_ref = refs[:3]
        carry_ref = None if first else refs[3]
        ends_out, carry_out = refs[-2:]
        core = lax.axis_index("gy")
        index = lax.axis_index("gx")
        place = lax.rem(index, reach)
        upper = lax.rem(lax.div(index, reach), 2) == 1
        rate = field_ref[core, 1]
        whole = jnp.exp(rate * float(reach))
        forward = jnp.exp(rate * place.astype(F32))
        backward = jnp.exp(rate * (reach - 1 - place).astype(F32))
        head, tail = ends_ref[0], ends_ref[1]
        head_in, tail_in = in_ref[0], in_ref[1]
        left = pick(upper, forward * head_in, jnp.zeros_like(head))
        right = pick(upper, jnp.zeros_like(head), backward * tail_in)
        carry_out[0] = left if first else carry_ref[0] + left
        carry_out[1] = right if first else carry_ref[1] + right
        ends_out[0] = pick(upper, head + whole * head_in, head_in + whole * head)
        ends_out[1] = pick(upper, tail_in + whole * tail, tail + whole * tail_in)

    args = (ends, arrived, fields) + (() if first else (carry,))
    return call(kernel, "join_segments", "v" * len(args), [vmem(*ends.shape)] * 2, args, micros=0.3)


def from_modes(modes, ends, carry, wave_y, fields, depth, parts):
    half = modes.shape[1]
    full = modes.shape[0] // depth
    rows = full // 2

    def kernel(modes_ref, ends_ref, carry_ref, wave_ref, field_ref, own, other, solved):
        core = lax.axis_index("gy")
        index = lax.axis_index("gx")
        ratio, rate, peak = field_ref[core, 0], field_ref[core, 1], field_ref[core, 2]
        around = 1.0 / (1.0 - jnp.exp(rate * float(parts)))
        left = carry_ref[0] + jnp.exp(rate * index.astype(F32)) * around * ends_ref[0]
        right = carry_ref[1] + jnp.exp(rate * (parts - 1 - index).astype(F32)) * around * ends_ref[1]
        run = left
        for x in range(depth):
            run = run * ratio + modes_ref[x * full : (x + 1) * full]
            solved[x * full : (x + 1) * full] = run
        run = right
        for x in range(depth - 1, -1, -1):
            run = run * ratio
            solved[x * full : (x + 1) * full] = peak * (solved[x * full : (x + 1) * full] + run)
            run = run + modes_ref[x * full : (x + 1) * full]
        back = multiply(wave_ref[...], solved[...])
        for x in range(depth):
            own[x * rows : (x + 1) * rows] = back[x * full : x * full + rows]
            other[x * rows : (x + 1) * rows] = back[x * full + rows : (x + 1) * full]

    flat = (depth * rows, half)
    return call(
        kernel,
        "from_modes",
        "vvvvv",
        [vmem(*flat)] * 2,
        (modes, ends, carry, wave_y, fields),
        scratch=[pltpu.VMEM(modes.shape, F32)],
    )


def last_transform(own, other, waves_back, depth):
    flat, half = own.shape
    rows = flat // depth

    def kernel(own_ref, other_ref, wave_ref, out_ref, out, sem):
        core = lax.axis_index("gy")
        result = multiply(own_ref[...], wave_ref[core]) + multiply(other_ref[...], wave_ref[1 - core])
        out[...] = result.reshape(depth, rows, 2 * half)
        copy = pltpu.make_async_copy(out, out_ref, sem.at[0])
        copy.start()
        copy.wait()

    shape = (depth, rows, 2 * half)
    return call(
        kernel,
        "last_transform",
        "vvv",
        [hbm(*shape)],
        (own, other, waves_back),
        scratch=[pltpu.VMEM(shape, F32), pltpu.SemaphoreType.DMA((1,))],
    )


def per_device(fluid_state, heat_state, design, cell_type, boundary, fluid_adjoint, heat_adjoint):
    depth, rows, columns = design.shape
    far = depth - 1
    parts = lax.axis_size("gx")
    waves, waves_back, wave_y, fields = filter_tables(depth, 2 * rows, columns)

    pairs_a = [(i, i ^ 1) for i in range(parts)]
    pairs_b = [(i, (i + 1) % parts if i % 2 else (i - 1) % parts) for i in range(parts)]

    def across(value):
        return lax.ppermute(value, "gy", [(0, 1), (1, 0)])

    def sideways(first, second):
        first = lax.ppermute(first, "gx", pairs_a)
        second = lax.ppermute(second, "gx", pairs_b)
        return first, second

    fluid_state, heat_state, design, cell_type, boundary = (
        in_hbm(value) for value in (fluid_state, heat_state, design, cell_type, boundary)
    )
    adj, hadj = fluid_adjoint, heat_adjoint
    post, heat_zero, aux_zero, porosity, label, chosen, sides, rows_one = first_collision(
        fluid_state, heat_state, design, cell_type, boundary
    )
    rows_one = across(rows_one)
    face_a, face_b = crossing_faces("first_faces", sides, rows_one, 1)
    face_a, face_b = sideways(face_a, face_b)
    post_one, heat_one, aux_one = second_interior(post, rows_one, porosity, label)
    post_one, heat_one, aux_one, rows_heat = second_boundary(
        post, rows_one, face_a, face_b, porosity, label, adj, hadj, post_one, heat_one, aux_one
    )
    rows_heat = across(rows_heat)
    seed_a, seed_b = heat_faces(post_one, hadj, label, rows_heat)
    adj_a, adj_b = adjoint_faces(adj, label, rows_heat, seed_a)
    seed_a, seed_b = sideways(seed_a, seed_b)
    adj_a, adj_b = sideways(adj_a, adj_b)
    fixed = (adj, hadj, post_one, heat_one, aux_one, porosity, label, rows_heat)
    state = second_adjoint(range(2, far - 1), "adjoint_inner", fixed, (), None, 2.5)
    lam, sens_one, lit, rows_two, sides = second_adjoint(
        (0, 1, far - 1, far), "adjoint_outer", fixed, (adj_a, adj_b, seed_a, seed_b), tuple(state), 1.5
    )
    rows_two = across(rows_two)
    face_a, face_b = crossing_faces("costate_faces", sides, rows_two, -1)
    face_a, face_b = sideways(face_a, face_b)
    fixed = (aux_zero, heat_zero, porosity, label, chosen, sens_one)
    state = first_adjoint(range(1, far), "costate_inner", lam, rows_two, fixed, None, None, waves, 5.0)
    fluid_costate, heat_costate, own, other = first_adjoint(
        (0, far), "costate_outer", lam, rows_two, fixed, (face_a, face_b), tuple(state), waves, 1.5
    )
    other = across(other)
    modes, ends = to_modes(own, other, wave_y, fields)
    carry = None
    reach = 1
    while reach < parts:
        arrived = lax.ppermute(ends, "gx", [(i, i ^ reach) for i in range(parts)])
        ends, carry = join_segments(ends, arrived, carry, fields, reach)
        reach = 2 * reach
    own, other = from_modes(modes, ends, carry, wave_y, fields, depth, parts)
    other = across(other)
    return (fluid_costate, heat_costate, last_transform(own, other, waves_back, depth))


def solution(mesh):
    return jax.shard_map(
        per_device,
        mesh=mesh,
        in_specs=(
            P(None, ("case", "gx"), "gy", None),
            P(None, ("case", "gx"), "gy", None),
            P(("case", "gx"), "gy", None),
            P(("case", "gx"), "gy", None),
            P(("case", "gx"), "gy", None),
            P(None, ("case", "gx"), "gy", None),
            P(None, ("case", "gx"), "gy", None),
        ),
        out_specs=(
            P(None, ("case", "gx"), "gy", None),
            P(None, ("case", "gx"), "gy", None),
            P(("case", "gx"), "gy", None),
        ),
        check_vma=False,
    )
```

```python
import numpy as np
import jax
import jax.numpy as jnp
from jax import lax
from jax.experimental import pallas as pl
from jax.experimental.pallas import tpu as pltpu
from jax.sharding import PartitionSpec as P

RADIUS = 4

fluid_vel = [
    (0, 0, 0),
    (1, 0, 0),
    (-1, 0, 0),
    (0, 1, 0),
    (0, -1, 0),
    (0, 0, 1),
    (0, 0, -1),
    (1, 1, 0),
    (-1, -1, 0),
    (1, -1, 0),
    (-1, 1, 0),
    (1, 0, 1),
    (-1, 0, -1),
    (1, 0, -1),
    (-1, 0, 1),
    (0, 1, 1),
    (0, -1, -1),
    (0, 1, -1),
    (0, -1, 1),
]
fluid_wts = [1.0 / 3.0] + [1.0 / 18.0] * 6 + [1.0 / 36.0] * 12
inlet_speed = 0.05
inlet_eq = [
    weight
    * (
        1.0
        + 3.0 * inlet_speed * entry[2]
        + 4.5 * (inlet_speed * entry[2]) ** 2
        - 1.5 * inlet_speed**2
    )
    for entry, weight in zip(fluid_vel, fluid_wts)
]

VEL = fluid_vel + fluid_vel[:7]
COUNT = len(VEL)
PLUS = [i for i in range(COUNT) if VEL[i][0] == 1]
MINUS = [i for i in range(COUNT) if VEL[i][0] == -1]
YPLUS = [i for i in range(COUNT) if VEL[i][1] == 1]
YMINUS = [i for i in range(COUNT) if VEL[i][1] == -1]
FPLUS = [i for i in PLUS if i < 19]
FMINUS = [i for i in MINUS if i < 19]
FYPLUS = [i for i in YPLUS if i < 19]
FYMINUS = [i for i in YMINUS if i < 19]

VMEM_BYTES = 24 * 1024 * 1024
F32 = jnp.float32


def params():
    return pltpu.CompilerParams(vmem_limit_bytes=VMEM_BYTES)


def cost(micros):
    return pl.CostEstimate(flops=int(micros * 1e9), bytes_accessed=0, transcendentals=0)


def shift_y(value, step, ghost):
    if step == 0:
        return value
    rows = value.shape[0]
    moved = pltpu.roll(value, step % rows, 0)
    place = lax.broadcasted_iota(jnp.int32, value.shape, 0)
    edge = 0 if step > 0 else rows - 1
    return jnp.where(place == edge, jnp.broadcast_to(ghost, value.shape), moved)


def shift_z(value, step):
    if step == 0:
        return value
    return pltpu.roll(value, step % value.shape[1], 1)


def pick(flag, first, second):
    return jnp.where(flag, first, second)


def tiles(rows, columns):
    return [
        (slice(r, r + 8), slice(c, c + 128)) for r in range(0, rows, 8) for c in range(0, columns, 128)
    ]


def porosity_of(design, kind):
    return jnp.where(kind == 2, design, jnp.where(kind == 1, 0.0, 1.0))


def heat_rate_of(porosity):
    return 1.0 / (0.55 + 0.9 * (1.0 - porosity))


def moments(pops, porosity):
    density = pops[0]
    for value in pops[1:]:
        density = density + value
    diff = {i: pops[i] - pops[i + 1] for i in range(1, 19, 2)}
    flux_x = diff[1] + diff[7] + diff[9] + diff[11] + diff[13]
    flux_y = diff[3] + diff[7] - diff[9] + diff[15] + diff[17]
    flux_z = diff[5] + diff[11] - diff[13] + diff[15] - diff[17]
    inverse = (0.1 + porosity) / (density * (0.5 + 0.6 * porosity))
    return density, (flux_x * inverse, flux_y * inverse, flux_z * inverse)


def along(entry, vector):
    total = None
    for part, value in zip(entry, vector):
        if part == 0:
            continue
        if total is None:
            total = value if part == 1 else -value
        else:
            total = total + value if part == 1 else total - value
    return total


def collide_fluid(pops, density, velocity, inlet):
    speed = velocity[0] * velocity[0] + velocity[1] * velocity[1] + velocity[2] * velocity[2]
    scaled = 1.25 * density
    base = scaled - 1.5 * scaled * speed
    result = [jnp.where(inlet, inlet_eq[0], base * (1.0 / 3.0) - 0.25 * pops[0])]
    for i in range(1, 19, 2):
        weight = fluid_wts[i]
        part = along(VEL[i], velocity)
        flow = scaled * part
        even = weight * base + (4.5 * weight) * (flow * part)
        odd = (3.0 * weight) * flow
        result.append(jnp.where(inlet, inlet_eq[i], even + odd - 0.25 * pops[i]))
        result.append(jnp.where(inlet, inlet_eq[i + 1], even - odd - 0.25 * pops[i + 1]))
    return result


def collide_heat(pops, velocity, porosity, inlet):
    temper = pops[0]
    for value in pops[1:]:
        temper = temper + value
    rate = heat_rate_of(porosity)
    keep = 1.0 - rate
    warm = rate * temper
    base = warm + (1.0 - porosity)
    result = [jnp.where(inlet, 0.0, keep * pops[0] + 0.25 * base)]
    for axis in range(3):
        i = 1 + 2 * axis
        odd = 0.5 * (warm * velocity[axis])
        even = 0.125 * base
        result.append(jnp.where(inlet, 0.0, keep * pops[i] + (even + odd)))
        result.append(jnp.where(inlet, 0.0, keep * pops[i + 1] + (even - odd)))
    return result


def collide_adjoint(density, velocity, heat, porosity, inlet, mu, nu):
    ux, uy, uz = velocity
    mu = [jnp.where(inlet, 0.0, value) for value in mu]
    nu = [jnp.where(inlet, 0.0, value) for value in nu]
    even = {i: mu[i] + mu[i + 1] for i in range(1, 19, 2)}
    odd = {i: mu[i] - mu[i + 1] for i in range(1, 19, 2)}
    wa, wb = 1.0 / 18.0, 1.0 / 36.0
    xy_sum, xz_sum, yz_sum = even[7] + even[9], even[11] + even[13], even[15] + even[17]
    m0 = mu[0] * (1.0 / 3.0) + wa * (even[1] + even[3] + even[5]) + wb * (xy_sum + xz_sum + yz_sum)
    m1x = wa * odd[1] + wb * (odd[7] + odd[9] + odd[11] + odd[13])
    m1y = wa * odd[3] + wb * (odd[7] - odd[9] + odd[15] + odd[17])
    m1z = wa * odd[5] + wb * (odd[11] - odd[13] + odd[15] - odd[17])
    mxx = wa * even[1] + wb * (xy_sum + xz_sum)
    myy = wa * even[3] + wb * (xy_sum + yz_sum)
    mzz = wa * even[5] + wb * (xz_sum + yz_sum)
    mxy = wb * (even[7] - even[9])
    mxz = wb * (even[11] - even[13])
    myz = wb * (even[15] - even[17])
    vx = mxx * ux + mxy * uy + mxz * uz
    vy = mxy * ux + myy * uy + myz * uz
    vz = mxz * ux + myz * uy + mzz * uz
    speed = ux * ux + uy * uy + uz * uz
    slope = (
        m0 * (1.0 - 1.5 * speed)
        + 3.0 * (ux * m1x + uy * m1y + uz * m1z)
        + 4.5 * (ux * vx + uy * vy + uz * vz)
    )
    rate = heat_rate_of(porosity)
    keep = 1.0 - rate
    temper = heat[0]
    for value in heat[1:]:
        temper = temper + value
    n0 = 0.25 * nu[0] + 0.125 * (nu[1] + nu[2] + nu[3] + nu[4] + nu[5] + nu[6])
    n1x, n1y, n1z = (0.125 * (nu[i] - nu[i + 1]) for i in (1, 3, 5))
    warm = 4.0 * rate * temper
    scaled = 3.75 * density
    bar_x = scaled * (m1x - m0 * ux + 3.0 * vx) + warm * n1x
    bar_y = scaled * (m1y - m0 * uy + 3.0 * vy) + warm * n1y
    bar_z = scaled * (m1z - m0 * uz + 3.0 * vz) + warm * n1z
    work = bar_x * ux + bar_y * uy + bar_z * uz
    ramp = 0.1 + porosity
    drag = 0.5 + 0.6 * porosity
    over = 1.0 / (density * drag)
    inverse = ramp * over
    b = (bar_x * inverse, bar_y * inverse, bar_z * inverse)
    a = 1.25 * slope - work * (drag * over)
    lam = [a - 0.25 * mu[0]]
    for i in range(1, 19, 2):
        part = along(VEL[i], b)
        lam.append((a + part) - 0.25 * mu[i])
        lam.append((a - part) - 0.25 * mu[i + 1])
    pull = n0 + 4.0 * (ux * n1x + uy * n1y + uz * n1z)
    a_heat = rate * pull
    lam_heat = [keep * value + a_heat for value in nu]
    dot = nu[0] * heat[0]
    for first, second in zip(nu[1:], heat[1:]):
        dot = dot + first * second
    sens = work * (0.44 / (ramp * drag)) - n0 + (0.9 * rate * rate) * (temper * pull - dot)
    return lam, lam_heat, sens


IN_VMEM = pl.BlockSpec(memory_space=pltpu.VMEM)
IN_HBM = pl.BlockSpec(memory_space=pltpu.HBM)


def vmem(*shape):
    return pltpu.VMEM(shape, F32)


def hbm(*shape):
    return pltpu.HBM(shape, F32)


def in_hbm(value):
    return pltpu.with_memory_space_constraint(value, pltpu.HBM)


def call(kernel, name, specs, outs, args, scratch=(), aliases=None, micros=0.0):
    spec_of = {"v": IN_VMEM, "h": IN_HBM}
    single = len(outs) == 1
    args = [
        pltpu.with_memory_space_constraint(value, pltpu.VMEM) if letter == "v" else value
        for letter, value in zip(specs, args)
    ]
    out_specs = [IN_HBM if out.memory_space == pltpu.HBM else IN_VMEM for out in outs]
    return pl.pallas_call(
        kernel,
        in_specs=[spec_of[letter] for letter in specs],
        out_specs=out_specs[0] if single else out_specs,
        out_shape=outs[0] if single else outs,
        scratch_shapes=list(scratch),
        input_output_aliases=aliases or {},
        compiler_params=params(),
        cost_estimate=cost(micros),
        name=name,
    )(*args)


def row_slot(i):
    return YPLUS.index(i) if VEL[i][1] > 0 else 6 + YMINUS.index(i)


def adjoint_slot(i):
    return 5 + FYPLUS.index(i) if VEL[i][1] > 0 else 10 + FYMINUS.index(i)


def for_planes(planes, body):
    if isinstance(planes, tuple):
        for x in planes:
            body(x)
    else:

        def step(x, carry):
            body(x)
            return carry

        lax.fori_loop(planes[0], planes[-1] + 1, step, 0)


def neighbour(x, step, far):
    plane = x + step
    if isinstance(x, int) and (plane < 0 or plane > far):
        return None
    return plane


def moved_population(source, i, x, direction, slot_of, rows_ref, low, high, far):
    step = tuple(direction * part for part in VEL[i])
    plane = neighbour(x, -step[0], far)
    if plane is None:
        value = low() if step[0] == 1 else high()
    else:
        value = source[i, plane]
        if step[1]:
            value = shift_y(value, step[1], rows_ref[slot_of(i), pl.ds(plane, 1), :])
    return shift_z(value, step[2])


def first_collision(fluid, heat, design, kind, label):
    cells = design.shape
    depth, rows, columns = cells
    far = depth - 1
    last = rows - 1

    def kernel(fluid_in, heat_in, design_in, kind_in, label_in, post, heat, aux, porosity, label, chosen,
               sides, msg, design, kind, sem):
        fields = (
            pltpu.make_async_copy(design_in, design, sem.at[0]),
            pltpu.make_async_copy(kind_in, kind, sem.at[1]),
            pltpu.make_async_copy(label_in, label, sem.at[2]),
        )

        def loads(x):
            return (
                pltpu.make_async_copy(fluid_in.at[:, x], post.at[0:19, x], sem.at[3 + 2 * x]),
                pltpu.make_async_copy(heat_in.at[:, x], heat.at[:, x], sem.at[4 + 2 * x]),
            )

        for copy in fields:
            copy.start()
        for x in range(depth):
            for copy in loads(x):
                copy.start()
        for copy in fields:
            copy.wait()

        def body(x):
            here = pl.ds(x, 1)
            kinds = kind[x]
            porosity[x] = porosity_of(design[x], kinds)
            chosen[x] = jnp.where(kinds == 2, 1.0, 0.0)
            for copy in loads(x):
                copy.wait()
            for r, c in tiles(rows, columns):
                phi = porosity[x, r, c]
                inlet = label[x, r, c] == 1
                pops = [post[i, x, r, c] for i in range(19)]
                density, velocity = moments(pops, phi)
                for i, value in enumerate((density,) + velocity):
                    aux[i, x, r, c] = value
                warm = [heat[i, x, r, c] for i in range(7)]
                result = collide_fluid(pops, density, velocity, inlet) + collide_heat(warm, velocity, phi, inlet)
                for i, value in enumerate(result):
                    post[i, x, r, c] = value
            for i in YPLUS:
                msg[row_slot(i), here, :] = post[i, x, last : last + 1, :]
            for i in YMINUS:
                msg[row_slot(i), here, :] = post[i, x, 0:1, :]

        for_planes(range(depth), body)
        for slot in range(6):
            sides[slot] = post[PLUS[slot], far]
            sides[6 + slot] = post[MINUS[slot], 0]

    return call(
        kernel,
        "first_collision",
        "hhhhh",
        [
            vmem(COUNT, *cells),
            vmem(7, *cells),
            vmem(4, *cells),
            vmem(*cells),
            pltpu.VMEM(cells, jnp.int32),
            vmem(*cells),
            vmem(12, rows, columns),
            vmem(12, depth, columns),
        ],
        (fluid, heat, design, kind, label),
        scratch=[pltpu.VMEM(cells, F32), pltpu.VMEM(cells, jnp.int32), pltpu.SemaphoreType.DMA((3 + 2 * depth,))],
        micros=0.0,
    )


def crossing_faces(name, sides, rows_in, direction):
    _, rows, columns = sides.shape
    far = rows_in.shape[1] - 1
    place, other = (far, 0) if direction == 1 else (0, far)

    def kernel(sides_ref, rows_ref, a_ref, b_ref):
        even = lax.rem(lax.axis_index("gx"), 2) == 0
        for slot in range(6):
            i, j = PLUS[slot], MINUS[slot]
            plus, minus = sides_ref[slot], sides_ref[6 + slot]
            if VEL[i][1]:
                plus = shift_y(plus, direction * VEL[i][1], rows_ref[row_slot(i), place : place + 1, :])
                minus = shift_y(minus, direction * VEL[j][1], rows_ref[row_slot(j), other : other + 1, :])
            high, low = (plus, minus) if direction == 1 else (minus, plus)
            a_ref[slot] = pick(even, high, low)
            b_ref[slot] = pick(even, low, high)

    return call(kernel, name, "vv", [vmem(6, rows, columns)] * 2, (sides, rows_in), micros=0.0)


def second_planes(planes, source, rows_ref, low, high, porosity_ref, label_ref, post, heat, aux, moved):
    _, depth, rows, columns = source.shape
    far = depth - 1

    def body(x):
        for i in range(COUNT):
            value = moved_population(
                source, i, x, 1, row_slot, rows_ref, lambda: low(PLUS.index(i)), lambda: high(MINUS.index(i)), far
            )
            if i < 19:
                moved[i] = value
            else:
                heat[i - 19, x] = value
        for r, c in tiles(rows, columns):
            porosity = porosity_ref[x, r, c]
            inlet = label_ref[x, r, c] == 1
            pops = [moved[i, r, c] for i in range(19)]
            density, velocity = moments(pops, porosity)
            for i, value in enumerate((density,) + velocity):
                aux[i, x, r, c] = value
            warm = [heat[i, x, r, c] for i in range(7)]
            for i, value in enumerate(collide_heat(warm, velocity, porosity, inlet)):
                post[i, x, r, c] = value

    for_planes(planes, body)


def second_interior(source, rows_in, porosity, label):
    cells = label.shape
    depth, rows, columns = cells
    far = depth - 1

    def kernel(source, rows_ref, porosity, label, post, heat, aux, moved):
        second_planes(range(1, far), source, rows_ref, None, None, porosity, label, post, heat, aux, moved)

    return call(
        kernel,
        "second_interior",
        "vvvv",
        [vmem(7, *cells), vmem(7, *cells), vmem(4, *cells)],
        (source, rows_in, porosity, label),
        scratch=[pltpu.VMEM((19, rows, columns), F32)],
        micros=0.0,
    )


def second_boundary(source, rows_in, face_a, face_b, porosity, label, adjoint, heat_adjoint, post, heat, aux):
    cells = label.shape
    depth, rows, columns = cells
    far = depth - 1
    last = rows - 1

    def kernel(source, rows_ref, a_ref, b_ref, porosity, label, adj, hadj, post_in, heat_in, aux_in,
               post, heat, aux, msg, moved):
        even = lax.rem(lax.axis_index("gx"), 2) == 0

        def low(slot):
            return pick(even, b_ref[slot], a_ref[slot])

        def high(slot):
            return pick(even, a_ref[slot], b_ref[slot])

        second_planes((0, far), source, rows_ref, low, high, porosity, label, post, heat, aux, moved)

        def rows_of(x, carry):
            here = pl.ds(x, 1)
            msg[0, here, :] = post[3, x, last : last + 1, :]
            msg[1, here, :] = post[4, x, 0:1, :]
            for i in FYPLUS:
                msg[adjoint_slot(i), here, :] = adj[i, x, 0:1, :]
            for i in FYMINUS:
                msg[adjoint_slot(i), here, :] = adj[i, x, last : last + 1, :]
            msg[15, here, :] = jnp.where(label[x, 0:1, :] == 2, 1.0, 0.0)
            msg[16, here, :] = jnp.where(label[x, last : last + 1, :] == 2, 1.0, 0.0)
            for slot, y in ((0, 0), (1, last)):
                row = slice(y, y + 1)
                total = post[4, x, 1:2, :] if y == 0 else post[3, x, last - 1 : last, :]
                total = total + post[0, x, row, :]
                total = total + shift_z(post[5, x, row, :], 1) + shift_z(post[6, x, row, :], -1)
                left = post[1, jnp.maximum(x - 1, 0), row, :]
                right = post[2, jnp.minimum(x + 1, far), row, :]
                total = total + pick(x == 0, jnp.zeros_like(left), left) + pick(x == far, jnp.zeros_like(right), right)
                msg[2 + slot, here, :] = hadj[3 + slot, x, row, :] + jnp.where(label[x, row, :] == 2, total, 0.0)
            return carry

        lax.fori_loop(0, depth, rows_of, 0)
        msg[4] = jnp.zeros((depth, columns), F32)
        msg[4, 0:1, :] = post[1, far, 0:1, :]
        msg[4, 1:2, :] = post[1, far, last : last + 1, :]
        msg[4, 2:3, :] = post[2, 0, 0:1, :]
        msg[4, 3:4, :] = post[2, 0, last : last + 1, :]

    return call(
        kernel,
        "second_boundary",
        "vvvvvvvvvvv",
        [vmem(7, *cells), vmem(7, *cells), vmem(4, *cells), vmem(17, depth, columns)],
        (source, rows_in, face_a, face_b, porosity, label, adjoint, heat_adjoint, post, heat, aux),
        scratch=[pltpu.VMEM((19, rows, columns), F32)],
        aliases={8: 0, 9: 1, 10: 2},
        micros=0.0,
    )


def heat_faces(post, heat_adjoint, label, rows_in):
    depth, rows, columns = label.shape
    far = depth - 1

    def kernel(post, hadj, label, rows_ref, a_ref, b_ref):
        even = lax.rem(lax.axis_index("gx"), 2) == 0

        def partial(x, other):
            total = post[0, x] + other
            total = total + shift_y(post[3, x], 1, rows_ref[0, x : x + 1, :])
            total = total + shift_y(post[4, x], -1, rows_ref[1, x : x + 1, :])
            return total + shift_z(post[5, x], 1) + shift_z(post[6, x], -1)

        high_seed = hadj[2, far] + jnp.where(label[far] == 2, partial(far, post[1, far - 1]), 0.0)
        low_seed = hadj[1, 0] + jnp.where(label[0] == 2, partial(0, post[2, 1]), 0.0)
        high_face, low_face = post[1, far], post[2, 0]
        a_ref[0:rows] = pick(even, high_face, low_face)
        b_ref[0:rows] = pick(even, low_face, high_face)
        a_ref[rows : 2 * rows] = pick(even, high_seed, low_seed)
        b_ref[rows : 2 * rows] = pick(even, low_seed, high_seed)
        place = lax.broadcasted_iota(jnp.int32, (8, columns), 0)

        def spread(slot):
            return jnp.broadcast_to(rows_ref[4, slot : slot + 1, :], (8, columns))

        high_rows = jnp.where(place == 0, spread(1), spread(0))
        low_rows = jnp.where(place == 0, spread(3), spread(2))
        a_ref[2 * rows : 2 * rows + 8] = pick(even, high_rows, low_rows)
        b_ref[2 * rows : 2 * rows + 8] = pick(even, low_rows, high_rows)

    shape = (2 * rows + 8, columns)
    return call(
        kernel, "heat_faces", "vvvv", [vmem(*shape)] * 2, (post, heat_adjoint, label, rows_in), micros=0.5
    )


def source_weights(aux, heat, porosity, label, chosen, x, k):
    density, ux, uy, uz = (aux[i, x] for i in range(4))
    phi = porosity[x]
    valid = jnp.logical_and(label[x] != 1, chosen[x] > 0.0)
    over = 0.44 / ((0.1 + phi) * (0.5 + 0.6 * phi))
    rate = heat_rate_of(phi)
    temper = heat[0, x]
    for i in range(1, 7):
        temper = temper + heat[i, x]
    part = along(VEL[k], (ux, uy, uz))
    weight = over * (0.5 * rate * temper) * part - 0.125
    weight = weight + (0.9 * rate * rate) * (temper * (0.125 + 0.5 * part) - heat[k, x])
    scale = jnp.where(valid, 3.75 * over * density, 0.0)
    return ux, uy, uz, scale, jnp.where(valid, weight, 0.0)


def adjoint_faces(adjoint, label, rows_in, aux, heat, porosity, chosen, after):
    depth, rows, columns = label.shape
    far = depth - 1

    def kernel(adj, label, rows_ref, aux, heat, porosity, chosen, after_ref, a_ref, b_ref):
        even = lax.rem(lax.axis_index("gx"), 2) == 0

        def emit(slot, high, low):
            a_ref[slot] = pick(even, high, low)
            b_ref[slot] = pick(even, low, high)

        for slot in range(5):
            i, j = FPLUS[slot], FMINUS[slot]
            low, high = adj[i, 0], adj[j, far]
            if VEL[i][1]:
                low = shift_y(low, -VEL[i][1], rows_ref[adjoint_slot(i), 0:1, :])
                high = shift_y(high, -VEL[j][1], rows_ref[adjoint_slot(j), far : far + 1, :])
            emit(slot, high, low)
        emit(5, jnp.where(label[far] == 2, 1.0, 0.0), jnp.where(label[0] == 2, 1.0, 0.0))
        highs = source_weights(aux, heat, porosity, label, chosen, far, 1)
        lows = source_weights(aux, heat, porosity, label, chosen, 0, 2)
        for slot, (high, low) in enumerate(zip(highs, lows)):
            emit(6 + slot, high, low)

    face = (11, rows, columns)
    return call(
        kernel,
        "adjoint_faces",
        "vvvvvvvv",
        [vmem(*face)] * 2,
        (adjoint, label, rows_in, aux, heat, porosity, chosen, after),
    )


def second_adjoint(planes, name, fixed, arrived, state, micros):
    adj, hadj, post, heat, aux, porosity, label, rows_in = fixed
    cells = label.shape
    depth, rows, columns = cells
    far = depth - 1
    last = rows - 1
    first = state is None
    boundary = isinstance(planes, tuple)
    lit_planes = range(planes[0] - 1, planes[-1] + 2) if first else ((0, far) if boundary else ())

    def kernel(*refs):
        refs = list(refs)
        adj, hadj, post, heat, aux, porosity, label, rows_ref = refs[:8]
        refs = refs[8:]
        if boundary:
            fa, fb, sa, sb = refs[:4]
        refs = refs[len(arrived) :]
        if not first:
            refs = refs[3:]
        lam, sens, lit = refs[:3]
        msg = refs[3] if boundary else None
        sides = refs[4] if boundary else None
        moved = refs[-1]
        even = lax.rem(lax.axis_index("gx"), 2) == 0
        tail = 2 * rows

        def from_left(where):
            return pick(even, sb[where], sa[where])

        def from_right(where):
            return pick(even, sa[where], sb[where])

        def light(x):
            here = pl.ds(x, 1)
            before, after = neighbour(x, -1, far), neighbour(x, 1, far)
            total = post[0, x]
            total = total + (from_left(slice(0, rows)) if before is None else post[1, before])
            total = total + (from_right(slice(0, rows)) if after is None else post[2, after])
            total = total + shift_y(post[3, x], 1, rows_ref[0, here, :])
            total = total + shift_y(post[4, x], -1, rows_ref[1, here, :])
            total = total + shift_z(post[5, x], 1) + shift_z(post[6, x], -1)
            lit[x] = jnp.where(label[x] == 2, total, 0.0)

        if lit_planes:
            for_planes(lit_planes, light)

        def body(x):
            here = pl.ds(x, 1)
            before, after = neighbour(x, -1, far), neighbour(x, 1, far)
            glow = lit[x]
            moved[19] = hadj[0, x] + glow
            if after is None:
                moved[20] = from_right(slice(rows, tail)) + pick(even, fa[5], fb[5]) * post[1, far]
            else:
                moved[20] = hadj[1, after] + lit[after]
            if before is None:
                moved[21] = from_left(slice(rows, tail)) + pick(even, fb[5], fa[5]) * post[2, 0]
            else:
                moved[21] = hadj[2, before] + lit[before]
            above = post[3, x, last : last + 1, :]
            below = post[4, x, 0:1, :]
            if before is None:
                above = above + from_left(slice(tail + 1, tail + 2))
                below = below + from_left(slice(tail, tail + 1))
            if after is None:
                above = above + from_right(slice(tail + 1, tail + 2))
                below = below + from_right(slice(tail, tail + 1))
            moved[22] = shift_y(hadj[3, x] + glow, -1, rows_ref[2, here, :] + rows_ref[15, here, :] * above)
            moved[23] = shift_y(hadj[4, x] + glow, 1, rows_ref[3, here, :] + rows_ref[16, here, :] * below)
            moved[24] = shift_z(hadj[5, x] + glow, -1)
            moved[25] = shift_z(hadj[6, x] + glow, 1)
            for i in range(19):
                moved[i] = moved_population(
                    adj,
                    i,
                    x,
                    -1,
                    adjoint_slot,
                    rows_ref,
                    lambda: pick(even, fb[FMINUS.index(i)], fa[FMINUS.index(i)]),
                    lambda: pick(even, fa[FPLUS.index(i)], fb[FPLUS.index(i)]),
                    far,
                )
            for r, c in tiles(rows, columns):
                inlet = label[x, r, c] == 1
                density, ux, uy, uz = (aux[i, x, r, c] for i in range(4))
                warm = [heat[i, x, r, c] for i in range(7)]
                mu = [moved[i, r, c] for i in range(19)]
                nu = [moved[19 + i, r, c] for i in range(7)]
                result, result_heat, part = collide_adjoint(
                    density, (ux, uy, uz), warm, porosity[x, r, c], inlet, mu, nu
                )
                for i, value in enumerate(result + result_heat):
                    lam[i, x, r, c] = value
                sens[x, r, c] = part

        for_planes(planes, body)
        if boundary:
            for slot in range(6):
                sides[slot] = lam[PLUS[slot], 0]
                sides[6 + slot] = lam[MINUS[slot], far]

            def rows_of(x, carry):
                here = pl.ds(x, 1)
                for i in YPLUS:
                    msg[row_slot(i), here, :] = lam[i, x, 0:1, :]
                for i in YMINUS:
                    msg[row_slot(i), here, :] = lam[i, x, last : last + 1, :]
                return carry

            lax.fori_loop(0, depth, rows_of, 0)

    outs = [vmem(COUNT, *cells), vmem(*cells), vmem(*cells)]
    if boundary:
        outs += [vmem(12, depth, columns), vmem(12, rows, columns)]
    args = fixed + arrived + (() if first else state)
    base = len(args) - 3
    return call(
        kernel,
        name,
        "v" * len(args),
        outs,
        args,
        scratch=[pltpu.VMEM((COUNT, rows, columns), F32)],
        aliases=None if first else {base: 0, base + 1: 1, base + 2: 2},
        micros=micros,
    )


def arriving(lam, rows_ref, moved, x, far, low, high):
    for i in range(COUNT):
        moved[i] = moved_population(
            lam, i, x, -1, row_slot, rows_ref, lambda: low(MINUS.index(i)), lambda: high(PLUS.index(i)), far
        )


def first_sensitivity(lam, rows_in, fixed, sens_one, weights_a, weights_b, waves):
    aux, heat, porosity, label, chosen = fixed
    depth, rows, columns = label.shape
    far = depth - 1
    half = columns // 2
    count = depth + 2

    def kernel(lam, rows_ref, aux, heat, porosity, label, chosen, sens_ref, a_ref, b_ref, waves_ref,
               own, other, moved, total):
        even = lax.rem(lax.axis_index("gx"), 2) == 0
        core = lax.axis_index("gy")

        def nothing(slot):
            return jnp.zeros((rows, columns), F32)

        def body(x):
            arriving(lam, rows_ref, moved, x, far, nothing, nothing)
            for r, c in tiles(rows, columns):
                inlet = label[x, r, c] == 1
                density, ux, uy, uz = (aux[i, x, r, c] for i in range(4))
                warm = [heat[i, x, r, c] for i in range(7)]
                mu = [moved[i, r, c] for i in range(19)]
                nu = [moved[19 + i, r, c] for i in range(7)]
                _, _, part = collide_adjoint(density, (ux, uy, uz), warm, porosity[x, r, c], inlet, mu, nu)
                total[x, r, c] = jnp.where(chosen[x, r, c] > 0.0, part + sens_ref[x, r, c], 0.0)

        for_planes((0, far), body)
        for_planes(range(1, far), body)
        for place, x, members, first, second in ((depth, 0, PLUS, b_ref, a_ref), (depth + 1, far, MINUS, a_ref, b_ref)):
            vector = [pick(even, first[6 + slot], second[6 + slot]) for slot in range(3)]
            scale = pick(even, first[9], second[9])
            speed = vector[0] * vector[0] + vector[1] * vector[1] + vector[2] * vector[2]
            result = jnp.zeros((rows, columns), F32)
            for i in members:
                value = lam[i, x]
                if VEL[i][1]:
                    value = shift_y(value, -VEL[i][1], rows_ref[row_slot(i), x : x + 1, :])
                value = shift_z(value, -VEL[i][2])
                if i < 19:
                    part = along(VEL[i], vector)
                    result = result + (fluid_wts[i] * scale) * (part - speed + 3.0 * part * part) * value
                else:
                    result = result + pick(even, first[10], second[10]) * value
            total[place] = result
        flat = total[...].reshape(count * rows, columns)
        own[...] = multiply(flat, waves_ref[core]).reshape(count, rows, half)
        other[...] = multiply(flat, waves_ref[1 - core]).reshape(count, rows, half)

    args = (lam, rows_in) + fixed + (sens_one, weights_a, weights_b, waves)
    return call(
        kernel,
        "first_sensitivity",
        "v" * len(args),
        [vmem(count, rows, half)] * 2,
        args,
        scratch=[pltpu.VMEM((COUNT, rows, columns), F32), pltpu.VMEM((count, rows, columns), F32)],
    )


def first_adjoint(groups, name, lam, rows_in, fixed, arrived, early_planes, early):
    aux, heat, porosity, label = fixed
    cells = label.shape
    depth, rows, columns = cells
    far = depth - 1
    planes = [x for group in groups for x in group]
    count = len(planes)
    last = early is not None

    def kernel(*refs):
        refs = list(refs)
        lam, rows_ref, aux, heat, porosity, label = refs[:6]
        refs = refs[6:]
        if last:
            b_ref, a_ref, early_ref, fluid_out, heat_out, token, moved, out, sem = refs
            token[...] = jnp.zeros((8, 128), F32)
        else:
            out, moved = refs
        even = lax.rem(lax.axis_index("gx"), 2) == 0

        def place(x):
            return planes.index(x) if isinstance(x, int) else x - groups[-1][0] + count - len(groups[-1])

        def writes(source, n, x, slot):
            return (
                pltpu.make_async_copy(source.at[0:19, n], fluid_out.at[:, x], sem.at[2 * slot]),
                pltpu.make_async_copy(source.at[19:26, n], heat_out.at[:, x], sem.at[2 * slot + 1]),
            )

        def low(slot):
            return pick(even, b_ref[slot], a_ref[slot])

        def high(slot):
            return pick(even, a_ref[slot], b_ref[slot])

        def body(x):
            n = place(x)
            arriving(lam, rows_ref, moved, x, far, low, high)
            for r, c in tiles(rows, columns):
                inlet = label[x, r, c] == 1
                density, ux, uy, uz = (aux[i, x, r, c] for i in range(4))
                warm = [heat[i, x, r, c] for i in range(7)]
                mu = [moved[i, r, c] for i in range(19)]
                nu = [moved[19 + i, r, c] for i in range(7)]
                result, result_heat, _ = collide_adjoint(density, (ux, uy, uz), warm, porosity[x, r, c], inlet, mu, nu)
                for i, value in enumerate(result + result_heat):
                    out[i, n, r, c] = value
            if last:
                for copy in writes(out, n, x, n):
                    copy.start()

        early_copies = []
        if last:
            for n, x in enumerate(early_planes):
                early_copies += writes(early_ref, n, x, count + n)
        for copy in early_copies:
            copy.start()
        for group in groups:
            for_planes(group, body)
        if last:

            def finish(x):
                for copy in writes(out, place(x), x, place(x)):
                    copy.wait()

            for group in groups:
                for_planes(group, finish)
        for copy in early_copies:
            copy.wait()

    buffer = (COUNT, count, rows, columns)
    moved = pltpu.VMEM((COUNT, rows, columns), F32)
    args = (lam, rows_in) + fixed + arrived + ((early,) if last else ())
    if last:
        outs = [hbm(19, *cells), hbm(7, *cells), vmem(8, 128)]
        scratch = [moved, pltpu.VMEM(buffer, F32), pltpu.SemaphoreType.DMA((2 * (count + len(early_planes)),))]
    else:
        outs = [vmem(*buffer)]
        scratch = [moved]
    return call(kernel, name, "v" * len(args), outs, args, scratch=scratch)


def multiply(first, second):
    return jnp.dot(first, second, precision=lax.Precision.HIGHEST, preferred_element_type=F32)


def hartley(length):
    index = np.arange(length)
    angle = 2.0 * np.pi * ((index[:, None] * index[None, :]) % length) / length
    return (np.cos(angle) + np.sin(angle)) / np.sqrt(length)


def filter_tables(depth, count_y, count_z):
    half = count_z // 2
    wave_z = hartley(count_z)
    waves = np.stack([wave_z[:, :half], wave_z[:, half:]]).astype(np.float32)
    waves_back = np.stack([wave_z[:half], wave_z[half:]]).astype(np.float32)
    wave_y = np.kron(np.eye(depth), hartley(count_y)).astype(np.float32)
    wave_ends = np.kron(np.eye(2), hartley(count_y)).astype(np.float32)
    symbol_y = 2.0 - 2.0 * np.cos(2.0 * np.pi * np.arange(count_y) / count_y)
    symbol_z = 2.0 - 2.0 * np.cos(2.0 * np.pi * np.arange(count_z) / count_z)
    weight = float(RADIUS * RADIUS)
    centre = (1.0 + weight * (2.0 + symbol_y[:, None] + symbol_z[None, :])) / weight
    ratio = 2.0 / (centre + np.sqrt(centre * centre - 4.0))
    peak = 1.0 / (weight * (1.0 / ratio - ratio))
    fields = np.stack([ratio, np.log(ratio) * depth, peak]).astype(np.float32)
    fields = np.stack([fields[:, :, :half], fields[:, :, half:]])
    return waves, waves_back, wave_y, wave_ends, fields


def to_modes(own, other, wave_y, wave_ends, fields):
    count, rows, half = own.shape
    depth = count - 2
    full = 2 * rows
    inside = depth * full

    def kernel(own_ref, other_ref, wave_ref, small_ref, field_ref, modes, ends, both):
        core = lax.axis_index("gy")
        for x in range(count):
            both[x * full : x * full + rows] = own_ref[x]
            both[x * full + rows : (x + 1) * full] = other_ref[x]
        modes[0:inside] = multiply(wave_ref[...], both[0:inside])
        modes[inside : inside + 2 * full] = multiply(small_ref[...], both[inside : inside + 2 * full])
        ratio = field_ref[core, 0]
        before, after = modes[inside : inside + full], modes[inside + full : inside + 2 * full]
        head = before
        for x in range(depth):
            head = head * ratio + modes[x * full : (x + 1) * full]
        ends[0] = head * ratio + after
        tail = after
        for x in range(depth - 1, -1, -1):
            tail = tail * ratio + modes[x * full : (x + 1) * full]
        ends[1] = tail * ratio + before

    return call(
        kernel,
        "to_modes",
        "vvvvv",
        [vmem(count * full, half), vmem(2, full, half)],
        (own, other, wave_y, wave_ends, fields),
        scratch=[pltpu.VMEM((count * full, half), F32)],
    )


def join_segments(ends, arrived, carry, fields, reach, after):
    first = carry is None

    def kernel(*refs):
        ends_ref, in_ref, field_ref = refs[:3]
        carry_ref = None if first else refs[3]
        ends_out, carry_out = refs[-2:]
        core = lax.axis_index("gy")
        index = lax.axis_index("gx")
        place = lax.rem(index, reach)
        upper = lax.rem(lax.div(index, reach), 2) == 1
        rate = field_ref[core, 1]
        whole = jnp.exp(rate * float(reach))
        forward = jnp.exp(rate * place.astype(F32))
        backward = jnp.exp(rate * (reach - 1 - place).astype(F32))
        head, tail = ends_ref[0], ends_ref[1]
        head_in, tail_in = in_ref[0], in_ref[1]
        left = pick(upper, forward * head_in, jnp.zeros_like(head))
        right = pick(upper, jnp.zeros_like(head), backward * tail_in)
        carry_out[0] = left if first else carry_ref[0] + left
        carry_out[1] = right if first else carry_ref[1] + right
        ends_out[0] = pick(upper, head + whole * head_in, head_in + whole * head)
        ends_out[1] = pick(upper, tail_in + whole * tail, tail + whole * tail_in)

    args = (ends, arrived, fields) + (() if first else (carry,)) + after
    return call(kernel, "join_segments", "v" * len(args), [vmem(*ends.shape)] * 2, args, micros=0.0)


def from_modes(modes, ends, carry, wave_y, fields, depth, parts, after):
    half = modes.shape[1]
    full = modes.shape[0] // (depth + 2)
    rows = full // 2
    inside = depth * full

    def kernel(modes_ref, ends_ref, carry_ref, wave_ref, field_ref, after_ref, own, other, solved):
        core = lax.axis_index("gy")
        index = lax.axis_index("gx")
        ratio, rate, peak = field_ref[core, 0], field_ref[core, 1], field_ref[core, 2]
        around = 1.0 / (1.0 - jnp.exp(rate * float(parts)))
        left = carry_ref[0] + jnp.exp(rate * index.astype(F32)) * around * ends_ref[0]
        right = carry_ref[1] + jnp.exp(rate * (parts - 1 - index).astype(F32)) * around * ends_ref[1]
        run = left + ratio * modes_ref[inside : inside + full]
        for x in range(depth):
            run = run + modes_ref[x * full : (x + 1) * full]
            solved[x * full : (x + 1) * full] = run
            run = run * ratio
        run = right + ratio * modes_ref[inside + full : inside + 2 * full]
        for x in range(depth - 1, -1, -1):
            solved[x * full : (x + 1) * full] = peak * (solved[x * full : (x + 1) * full] + run)
            run = ratio * (run + modes_ref[x * full : (x + 1) * full])
        back = multiply(wave_ref[...], solved[...])
        for x in range(depth):
            own[x * rows : (x + 1) * rows] = back[x * full : x * full + rows]
            other[x * rows : (x + 1) * rows] = back[x * full + rows : (x + 1) * full]

    flat = (depth * rows, half)
    return call(
        kernel,
        "from_modes",
        "vvvvvv",
        [vmem(*flat)] * 2,
        (modes, ends, carry, wave_y, fields, after),
        scratch=[pltpu.VMEM((inside, half), F32)],
    )


def last_transform(own, other, waves_back, depth):
    flat, half = own.shape
    rows = flat // depth

    def kernel(own_ref, other_ref, wave_ref, out_ref, out, sem):
        core = lax.axis_index("gy")
        result = multiply(own_ref[...], wave_ref[core]) + multiply(other_ref[...], wave_ref[1 - core])
        out[...] = result.reshape(depth, rows, 2 * half)
        copy = pltpu.make_async_copy(out, out_ref, sem.at[0])
        copy.start()
        copy.wait()

    shape = (depth, rows, 2 * half)
    return call(
        kernel,
        "last_transform",
        "vvv",
        [hbm(*shape)],
        (own, other, waves_back),
        scratch=[pltpu.VMEM(shape, F32), pltpu.SemaphoreType.DMA((1,))],
    )


def per_device(fluid_state, heat_state, design, cell_type, boundary, fluid_adjoint, heat_adjoint):
    depth, rows, columns = design.shape
    far = depth - 1
    parts = lax.axis_size("gx")
    waves, waves_back, wave_y, wave_ends, fields = filter_tables(depth, 2 * rows, columns)

    pairs_a = [(i, i ^ 1) for i in range(parts)]
    pairs_b = [(i, (i + 1) % parts if i % 2 else (i - 1) % parts) for i in range(parts)]

    def across(value):
        return lax.ppermute(value, "gy", [(0, 1), (1, 0)])

    def sideways(first, second):
        first = lax.ppermute(first, "gx", pairs_a)
        second = lax.ppermute(second, "gx", pairs_b)
        return first, second

    fluid_state, heat_state, design, cell_type, boundary = (
        in_hbm(value) for value in (fluid_state, heat_state, design, cell_type, boundary)
    )
    adj, hadj = fluid_adjoint, heat_adjoint
    post, heat_zero, aux_zero, porosity, label, chosen, sides, rows_one = first_collision(
        fluid_state, heat_state, design, cell_type, boundary
    )
    rows_one = across(rows_one)
    face_a, face_b = crossing_faces("first_faces", sides, rows_one, 1)
    face_a, face_b = sideways(face_a, face_b)
    post_one, heat_one, aux_one = second_interior(post, rows_one, porosity, label)
    post_one, heat_one, aux_one, rows_heat = second_boundary(
        post, rows_one, face_a, face_b, porosity, label, adj, hadj, post_one, heat_one, aux_one
    )
    rows_heat = across(rows_heat)
    seed_a, seed_b = heat_faces(post_one, hadj, label, rows_heat)
    adj_a, adj_b = adjoint_faces(
        adj, label, rows_heat, aux_zero, heat_zero, porosity, chosen, seed_a
    )
    seed_a, seed_b = sideways(seed_a, seed_b)
    adj_a, adj_b = sideways(adj_a, adj_b)
    fixed = (adj, hadj, post_one, heat_one, aux_one, porosity, label, rows_heat)
    state = second_adjoint(range(2, far - 1), "adjoint_inner", fixed, (), None, 0.0)
    lam, sens_one, lit, rows_two, sides = second_adjoint(
        (0, 1, far - 1, far), "adjoint_outer", fixed, (adj_a, adj_b, seed_a, seed_b), tuple(state), 0.0
    )
    rows_two = across(rows_two)
    face_a, face_b = crossing_faces("costate_faces", sides, rows_two, -1)
    face_a, face_b = sideways(face_a, face_b)
    fixed = (aux_zero, heat_zero, porosity, label)
    own, other = first_sensitivity(lam, rows_two, fixed + (chosen,), sens_one, adj_a, adj_b, waves)
    early = first_adjoint(((1,),), "costate_early", lam, rows_two, fixed, (), None, None)
    fluid_costate, heat_costate, token = first_adjoint(
        ((0, far), range(2, far)), "costate_rest", lam, rows_two, fixed, (face_b, face_a), (1,), early
    )
    other = across(other)
    modes, ends = to_modes(own, other, wave_y, wave_ends, fields)
    carry = None
    reach = 1
    while reach < parts:
        arrived = lax.ppermute(ends, "gx", [(i, i ^ reach) for i in range(parts)])
        ends, carry = join_segments(ends, arrived, carry, fields, reach, (early,) if reach == 1 else ())
        reach = 2 * reach
    own, other = from_modes(modes, ends, carry, wave_y, fields, depth, parts, token)
    other = across(other)
    return (fluid_costate, heat_costate, last_transform(own, other, waves_back, depth))


def solution(mesh):
    return jax.shard_map(
        per_device,
        mesh=mesh,
        in_specs=(
            P(None, ("case", "gx"), "gy", None),
            P(None, ("case", "gx"), "gy", None),
            P(("case", "gx"), "gy", None),
            P(("case", "gx"), "gy", None),
            P(("case", "gx"), "gy", None),
            P(None, ("case", "gx"), "gy", None),
            P(None, ("case", "gx"), "gy", None),
        ),
        out_specs=(
            P(None, ("case", "gx"), "gy", None),
            P(None, ("case", "gx"), "gy", None),
            P(("case", "gx"), "gy", None),
        ),
        check_vma=False,
    )
```

```python
import numpy as np
import jax
import jax.numpy as jnp
from jax import lax
from jax.experimental import pallas as pl
from jax.experimental.pallas import tpu as pltpu
from jax.sharding import PartitionSpec as P

RADIUS = 4

fluid_vel = [
    (0, 0, 0),
    (1, 0, 0),
    (-1, 0, 0),
    (0, 1, 0),
    (0, -1, 0),
    (0, 0, 1),
    (0, 0, -1),
    (1, 1, 0),
    (-1, -1, 0),
    (1, -1, 0),
    (-1, 1, 0),
    (1, 0, 1),
    (-1, 0, -1),
    (1, 0, -1),
    (-1, 0, 1),
    (0, 1, 1),
    (0, -1, -1),
    (0, 1, -1),
    (0, -1, 1),
]
fluid_wts = [1.0 / 3.0] + [1.0 / 18.0] * 6 + [1.0 / 36.0] * 12
inlet_speed = 0.05
inlet_eq = [
    weight
    * (
        1.0
        + 3.0 * inlet_speed * entry[2]
        + 4.5 * (inlet_speed * entry[2]) ** 2
        - 1.5 * inlet_speed**2
    )
    for entry, weight in zip(fluid_vel, fluid_wts)
]

VEL = fluid_vel + fluid_vel[:7]
COUNT = len(VEL)
PLUS = [i for i in range(COUNT) if VEL[i][0] == 1]
MINUS = [i for i in range(COUNT) if VEL[i][0] == -1]
YPLUS = [i for i in range(COUNT) if VEL[i][1] == 1]
YMINUS = [i for i in range(COUNT) if VEL[i][1] == -1]
FPLUS = [i for i in PLUS if i < 19]
FMINUS = [i for i in MINUS if i < 19]
FYPLUS = [i for i in YPLUS if i < 19]
FYMINUS = [i for i in YMINUS if i < 19]

VMEM_BYTES = 24 * 1024 * 1024
EARLY = 3
SEEDS = 40
F32 = jnp.float32


def params():
    return pltpu.CompilerParams(vmem_limit_bytes=VMEM_BYTES)


def cost(micros):
    return pl.CostEstimate(flops=int(micros * 1e9), bytes_accessed=0, transcendentals=0)


def shift_y(value, step, ghost):
    if step == 0:
        return value
    rows = value.shape[0]
    moved = pltpu.roll(value, step % rows, 0)
    place = lax.broadcasted_iota(jnp.int32, value.shape, 0)
    edge = 0 if step > 0 else rows - 1
    return jnp.where(place == edge, jnp.broadcast_to(ghost, value.shape), moved)


def shift_z(value, step):
    if step == 0:
        return value
    return pltpu.roll(value, step % value.shape[1], 1)


def pick(flag, first, second):
    return jnp.where(flag, first, second)


def tiles(rows, columns):
    return [
        (slice(r, r + 8), slice(c, c + 128)) for r in range(0, rows, 8) for c in range(0, columns, 128)
    ]


def porosity_of(design, kind):
    return jnp.where(kind == 2, design, jnp.where(kind == 1, 0.0, 1.0))


def heat_rate_of(porosity):
    return 1.0 / (0.55 + 0.9 * (1.0 - porosity))


def moments(pops, porosity):
    density = pops[0]
    for value in pops[1:]:
        density = density + value
    diff = {i: pops[i] - pops[i + 1] for i in range(1, 19, 2)}
    flux_x = diff[1] + diff[7] + diff[9] + diff[11] + diff[13]
    flux_y = diff[3] + diff[7] - diff[9] + diff[15] + diff[17]
    flux_z = diff[5] + diff[11] - diff[13] + diff[15] - diff[17]
    inverse = (0.1 + porosity) / (density * (0.5 + 0.6 * porosity))
    return density, (flux_x * inverse, flux_y * inverse, flux_z * inverse)


def along(entry, vector):
    total = None
    for part, value in zip(entry, vector):
        if part == 0:
            continue
        if total is None:
            total = value if part == 1 else -value
        else:
            total = total + value if part == 1 else total - value
    return total


def collide_fluid(pops, density, velocity, inlet):
    speed = velocity[0] * velocity[0] + velocity[1] * velocity[1] + velocity[2] * velocity[2]
    scaled = 1.25 * density
    base = scaled - 1.5 * scaled * speed
    result = [jnp.where(inlet, inlet_eq[0], base * (1.0 / 3.0) - 0.25 * pops[0])]
    for i in range(1, 19, 2):
        weight = fluid_wts[i]
        part = along(VEL[i], velocity)
        flow = scaled * part
        even = weight * base + (4.5 * weight) * (flow * part)
        odd = (3.0 * weight) * flow
        result.append(jnp.where(inlet, inlet_eq[i], even + odd - 0.25 * pops[i]))
        result.append(jnp.where(inlet, inlet_eq[i + 1], even - odd - 0.25 * pops[i + 1]))
    return result


def collide_heat(pops, velocity, porosity, inlet):
    temper = pops[0]
    for value in pops[1:]:
        temper = temper + value
    rate = heat_rate_of(porosity)
    keep = 1.0 - rate
    warm = rate * temper
    base = warm + (1.0 - porosity)
    result = [jnp.where(inlet, 0.0, keep * pops[0] + 0.25 * base)]
    for axis in range(3):
        i = 1 + 2 * axis
        odd = 0.5 * (warm * velocity[axis])
        even = 0.125 * base
        result.append(jnp.where(inlet, 0.0, keep * pops[i] + (even + odd)))
        result.append(jnp.where(inlet, 0.0, keep * pops[i + 1] + (even - odd)))
    return result


def collide_adjoint(density, velocity, heat, porosity, inlet, mu, nu):
    ux, uy, uz = velocity
    mu = [jnp.where(inlet, 0.0, value) for value in mu]
    nu = [jnp.where(inlet, 0.0, value) for value in nu]
    even = {i: mu[i] + mu[i + 1] for i in range(1, 19, 2)}
    odd = {i: mu[i] - mu[i + 1] for i in range(1, 19, 2)}
    wa, wb = 1.0 / 18.0, 1.0 / 36.0
    xy_sum, xz_sum, yz_sum = even[7] + even[9], even[11] + even[13], even[15] + even[17]
    m0 = mu[0] * (1.0 / 3.0) + wa * (even[1] + even[3] + even[5]) + wb * (xy_sum + xz_sum + yz_sum)
    m1x = wa * odd[1] + wb * (odd[7] + odd[9] + odd[11] + odd[13])
    m1y = wa * odd[3] + wb * (odd[7] - odd[9] + odd[15] + odd[17])
    m1z = wa * odd[5] + wb * (odd[11] - odd[13] + odd[15] - odd[17])
    mxx = wa * even[1] + wb * (xy_sum + xz_sum)
    myy = wa * even[3] + wb * (xy_sum + yz_sum)
    mzz = wa * even[5] + wb * (xz_sum + yz_sum)
    mxy = wb * (even[7] - even[9])
    mxz = wb * (even[11] - even[13])
    myz = wb * (even[15] - even[17])
    vx = mxx * ux + mxy * uy + mxz * uz
    vy = mxy * ux + myy * uy + myz * uz
    vz = mxz * ux + myz * uy + mzz * uz
    speed = ux * ux + uy * uy + uz * uz
    slope = (
        m0 * (1.0 - 1.5 * speed)
        + 3.0 * (ux * m1x + uy * m1y + uz * m1z)
        + 4.5 * (ux * vx + uy * vy + uz * vz)
    )
    rate = heat_rate_of(porosity)
    keep = 1.0 - rate
    temper = heat[0]
    for value in heat[1:]:
        temper = temper + value
    n0 = 0.25 * nu[0] + 0.125 * (nu[1] + nu[2] + nu[3] + nu[4] + nu[5] + nu[6])
    n1x, n1y, n1z = (0.125 * (nu[i] - nu[i + 1]) for i in (1, 3, 5))
    warm = 4.0 * rate * temper
    scaled = 3.75 * density
    bar_x = scaled * (m1x - m0 * ux + 3.0 * vx) + warm * n1x
    bar_y = scaled * (m1y - m0 * uy + 3.0 * vy) + warm * n1y
    bar_z = scaled * (m1z - m0 * uz + 3.0 * vz) + warm * n1z
    work = bar_x * ux + bar_y * uy + bar_z * uz
    ramp = 0.1 + porosity
    drag = 0.5 + 0.6 * porosity
    over = 1.0 / (density * drag)
    inverse = ramp * over
    b = (bar_x * inverse, bar_y * inverse, bar_z * inverse)
    a = 1.25 * slope - work * (drag * over)
    lam = [a - 0.25 * mu[0]]
    for i in range(1, 19, 2):
        part = along(VEL[i], b)
        lam.append((a + part) - 0.25 * mu[i])
        lam.append((a - part) - 0.25 * mu[i + 1])
    pull = n0 + 4.0 * (ux * n1x + uy * n1y + uz * n1z)
    a_heat = rate * pull
    lam_heat = [keep * value + a_heat for value in nu]
    dot = nu[0] * heat[0]
    for first, second in zip(nu[1:], heat[1:]):
        dot = dot + first * second
    sens = work * (0.44 / (ramp * drag)) - n0 + (0.9 * rate * rate) * (temper * pull - dot)
    return lam, lam_heat, sens


IN_VMEM = pl.BlockSpec(memory_space=pltpu.VMEM)
IN_HBM = pl.BlockSpec(memory_space=pltpu.HBM)


def vmem(*shape):
    return pltpu.VMEM(shape, F32)


def hbm(*shape):
    return pltpu.HBM(shape, F32)


def in_hbm(value):
    return pltpu.with_memory_space_constraint(value, pltpu.HBM)


def call(kernel, name, specs, outs, args, scratch=(), aliases=None, micros=0.0):
    spec_of = {"v": IN_VMEM, "h": IN_HBM}
    single = len(outs) == 1
    args = [
        pltpu.with_memory_space_constraint(value, pltpu.VMEM) if letter == "v" else value
        for letter, value in zip(specs, args)
    ]
    out_specs = [IN_HBM if out.memory_space == pltpu.HBM else IN_VMEM for out in outs]
    return pl.pallas_call(
        kernel,
        in_specs=[spec_of[letter] for letter in specs],
        out_specs=out_specs[0] if single else out_specs,
        out_shape=outs[0] if single else outs,
        scratch_shapes=list(scratch),
        input_output_aliases=aliases or {},
        compiler_params=params(),
        cost_estimate=cost(micros),
        name=name,
    )(*args)


def row_slot(i):
    return YPLUS.index(i) if VEL[i][1] > 0 else 6 + YMINUS.index(i)


def adjoint_slot(i):
    return 5 + FYPLUS.index(i) if VEL[i][1] > 0 else 10 + FYMINUS.index(i)


def for_planes(planes, body):
    if isinstance(planes, tuple):
        for x in planes:
            body(x)
    else:

        def step(x, carry):
            body(x)
            return carry

        lax.fori_loop(planes[0], planes[-1] + 1, step, 0)


def neighbour(x, step, far):
    plane = x + step
    if isinstance(x, int) and (plane < 0 or plane > far):
        return None
    return plane


def moved_population(source, i, x, direction, slot_of, rows_ref, low, high, far):
    step = tuple(direction * part for part in VEL[i])
    plane = neighbour(x, -step[0], far)
    if plane is None:
        value = low() if step[0] == 1 else high()
    else:
        value = source[i, plane]
        if step[1]:
            value = shift_y(value, step[1], rows_ref[slot_of(i), pl.ds(plane, 1), :])
    return shift_z(value, step[2])


def corner_rows(direction):
    return ((7, -1), (9, -1), (8, 0), (10, 0)) if direction == 1 else ((7, 0), (9, 0), (8, -1), (10, -1))


def collide_plane(x, fluid, heat, post, aux, porosity, label):
    _, _, rows, columns = post.shape
    for r, c in tiles(rows, columns):
        phi = porosity[x, r, c]
        inlet = label[x, r, c] == 1
        pops = [fluid[i, x, r, c] for i in range(19)]
        density, velocity = moments(pops, phi)
        for i, value in enumerate((density,) + velocity):
            aux[i, x, r, c] = value
        warm = [heat[i, x, r, c] for i in range(7)]
        result = collide_fluid(pops, density, velocity, inlet) + collide_heat(warm, velocity, phi, inlet)
        for i, value in enumerate(result):
            post[i, x, r, c] = value


def first_boundary(fluid, heat, design, kind, label):
    cells = design.shape
    depth, rows, columns = cells
    far = depth - 1
    last = rows - 1

    def kernel(fluid_in, heat_in, design_in, kind_in, label_in, post, heat, aux, porosity, label, chosen,
               sides, corner, design, kind, sem):
        fields = (
            pltpu.make_async_copy(design_in, design, sem.at[0]),
            pltpu.make_async_copy(kind_in, kind, sem.at[1]),
            pltpu.make_async_copy(label_in, label, sem.at[2]),
        )
        loads = []
        for n, x in enumerate((0, far)):
            loads.append(pltpu.make_async_copy(fluid_in.at[:, x], post.at[0:19, x], sem.at[3 + 2 * n]))
            loads.append(pltpu.make_async_copy(heat_in.at[:, x], heat.at[:, x], sem.at[4 + 2 * n]))
        for copy in fields + tuple(loads):
            copy.start()
        for copy in fields:
            copy.wait()

        def prepare(x, carry):
            kinds = kind[x]
            porosity[x] = porosity_of(design[x], kinds)
            chosen[x] = jnp.where(kinds == 2, 1.0, 0.0)
            return carry

        lax.fori_loop(0, depth, prepare, 0)
        for copy in loads:
            copy.wait()
        collide_plane(0, post, heat, post, aux, porosity, label)
        collide_plane(far, post, heat, post, aux, porosity, label)
        for slot in range(6):
            sides[slot] = post[PLUS[slot], far]
            sides[6 + slot] = post[MINUS[slot], 0]
        corner[...] = jnp.zeros((8, columns), F32)
        for slot, (i, x) in enumerate(corner_rows(1)):
            y = last if VEL[i][1] > 0 else 0
            corner[slot : slot + 1, :] = post[i, x % depth, y : y + 1, :]

    return call(
        kernel,
        "first_boundary",
        "hhhhh",
        [
            vmem(COUNT, *cells),
            vmem(7, *cells),
            vmem(4, *cells),
            vmem(*cells),
            pltpu.VMEM(cells, jnp.int32),
            vmem(*cells),
            vmem(12, rows, columns),
            vmem(8, columns),
        ],
        (fluid, heat, design, kind, label),
        scratch=[pltpu.VMEM(cells, F32), pltpu.VMEM(cells, jnp.int32), pltpu.SemaphoreType.DMA((7,))],
    )


def first_interior(fluid, heat, post, aux, porosity, label, after):
    cells = label.shape
    depth, rows, columns = cells
    far = depth - 1
    last = rows - 1

    def kernel(fluid, heat, post_in, aux_in, porosity, label, after_ref, post, aux, msg):
        for_planes(range(1, far), lambda x: collide_plane(x, fluid, heat, post, aux, porosity, label))

        def rows_of(x, carry):
            here = pl.ds(x, 1)
            for i in YPLUS:
                msg[row_slot(i), here, :] = post[i, x, last : last + 1, :]
            for i in YMINUS:
                msg[row_slot(i), here, :] = post[i, x, 0:1, :]
            return carry

        lax.fori_loop(0, depth, rows_of, 0)

    return call(
        kernel,
        "first_interior",
        "vvvvvvv",
        [vmem(COUNT, *cells), vmem(4, *cells), vmem(12, depth, columns)],
        (fluid, heat, post, aux, porosity, label, after),
        aliases={2: 0, 3: 1},
        micros=1.0,
    )


def source_weights(aux, heat, porosity, label, chosen, x, k):
    density, ux, uy, uz = (aux[i, x] for i in range(4))
    phi = porosity[x]
    valid = jnp.logical_and(label[x] != 1, chosen[x] > 0.0)
    over = 0.44 / ((0.1 + phi) * (0.5 + 0.6 * phi))
    rate = heat_rate_of(phi)
    temper = heat[0, x]
    for i in range(1, 7):
        temper = temper + heat[i, x]
    part = along(VEL[k], (ux, uy, uz))
    weight = over * (0.5 * rate * temper) * part - 0.125
    weight = weight + (0.9 * rate * rate) * (temper * (0.125 + 0.5 * part) - heat[k, x])
    scale = jnp.where(valid, 3.75 * over * density, 0.0)
    return jnp.where(valid, weight, 0.0), scale, ux, uy, uz


def crossing_sides(sides_ref, row_of, direction, slot):
    i, j = PLUS[slot], MINUS[slot]
    plus, minus = sides_ref[slot], sides_ref[6 + slot]
    if VEL[i][1]:
        plus = shift_y(plus, direction * VEL[i][1], row_of(i))
        minus = shift_y(minus, direction * VEL[j][1], row_of(j))
    return (plus, minus) if direction == 1 else (minus, plus)


def first_faces(sides, rows_in, label, aux, heat, porosity, chosen):
    _, rows, columns = sides.shape
    far = label.shape[0] - 1

    def kernel(sides_ref, rows_ref, label, aux, heat, porosity, chosen, a_ref, b_ref, token):
        token[...] = jnp.zeros((8, 128), F32)
        even = lax.rem(lax.axis_index("gx"), 2) == 0

        def row_of(i):
            slot = [entry[0] for entry in corner_rows(1)].index(i)
            return rows_ref[slot : slot + 1, :]

        for slot in range(6):
            high, low = crossing_sides(sides_ref, row_of, 1, slot)
            a_ref[slot] = pick(even, high, low)
            b_ref[slot] = pick(even, low, high)
        highs = source_weights(aux, heat, porosity, label, chosen, far, 1)
        lows = source_weights(aux, heat, porosity, label, chosen, 0, 2)
        for slot in range(EARLY):
            a_ref[6 + slot] = pick(even, highs[slot], lows[slot])
            b_ref[6 + slot] = pick(even, lows[slot], highs[slot])

    return call(
        kernel,
        "first_faces",
        "v" * 7,
        [vmem(6 + EARLY, rows, columns)] * 2 + [vmem(8, 128)],
        (sides, rows_in, label, aux, heat, porosity, chosen),
    )


def costate_faces(sides, rows_in):
    _, rows, columns = sides.shape

    def kernel(sides_ref, rows_ref, a_ref, b_ref):
        even = lax.rem(lax.axis_index("gx"), 2) == 0
        far = rows_ref.shape[1] - 1

        def row_of(i):
            x = 0 if VEL[i][0] > 0 else far
            return rows_ref[row_slot(i), x : x + 1, :]

        for slot in range(6):
            high, low = crossing_sides(sides_ref, row_of, -1, slot)
            a_ref[slot] = pick(even, high, low)
            b_ref[slot] = pick(even, low, high)

    return call(kernel, "costate_faces", "vv", [vmem(6, rows, columns)] * 2, (sides, rows_in))


def second_planes(planes, source, rows_ref, low, high, porosity_ref, label_ref, post, heat, aux, moved):
    _, depth, rows, columns = source.shape
    far = depth - 1

    def body(x):
        for i in range(COUNT):
            value = moved_population(
                source, i, x, 1, row_slot, rows_ref, lambda: low(PLUS.index(i)), lambda: high(MINUS.index(i)), far
            )
            if i < 19:
                moved[i] = value
            else:
                heat[i - 19, x] = value
        for r, c in tiles(rows, columns):
            porosity = porosity_ref[x, r, c]
            inlet = label_ref[x, r, c] == 1
            pops = [moved[i, r, c] for i in range(19)]
            density, velocity = moments(pops, porosity)
            for i, value in enumerate((density,) + velocity):
                aux[i, x, r, c] = value
            warm = [heat[i, x, r, c] for i in range(7)]
            for i, value in enumerate(collide_heat(warm, velocity, porosity, inlet)):
                post[i, x, r, c] = value

    for_planes(planes, body)


def second_interior(source, rows_in, porosity, label):
    cells = label.shape
    depth, rows, columns = cells
    far = depth - 1

    def kernel(source, rows_ref, porosity, label, post, heat, aux, moved):
        second_planes(range(1, far), source, rows_ref, None, None, porosity, label, post, heat, aux, moved)

    return call(
        kernel,
        "second_interior",
        "vvvv",
        [vmem(7, *cells), vmem(7, *cells), vmem(4, *cells)],
        (source, rows_in, porosity, label),
        scratch=[pltpu.VMEM((19, rows, columns), F32)],
        micros=0.0,
    )


def second_boundary(source, rows_in, face_a, face_b, porosity, label, adjoint, heat_adjoint, post, heat, aux):
    cells = label.shape
    depth, rows, columns = cells
    far = depth - 1
    last = rows - 1

    def kernel(source, rows_ref, a_ref, b_ref, porosity, label, adj, hadj, post_in, heat_in, aux_in,
               post, heat, aux, msg, moved):
        even = lax.rem(lax.axis_index("gx"), 2) == 0

        def low(slot):
            return pick(even, b_ref[slot], a_ref[slot])

        def high(slot):
            return pick(even, a_ref[slot], b_ref[slot])

        second_planes((0, far), source, rows_ref, low, high, porosity, label, post, heat, aux, moved)

        def rows_of(x, carry):
            here = pl.ds(x, 1)
            msg[0, here, :] = post[3, x, last : last + 1, :]
            msg[1, here, :] = post[4, x, 0:1, :]
            for i in FYPLUS:
                msg[adjoint_slot(i), here, :] = adj[i, x, 0:1, :]
            for i in FYMINUS:
                msg[adjoint_slot(i), here, :] = adj[i, x, last : last + 1, :]
            msg[15, here, :] = jnp.where(label[x, 0:1, :] == 2, 1.0, 0.0)
            msg[16, here, :] = jnp.where(label[x, last : last + 1, :] == 2, 1.0, 0.0)
            for slot, y in ((0, 0), (1, last)):
                row = slice(y, y + 1)
                total = post[4, x, 1:2, :] if y == 0 else post[3, x, last - 1 : last, :]
                total = total + post[0, x, row, :]
                total = total + shift_z(post[5, x, row, :], 1) + shift_z(post[6, x, row, :], -1)
                left = post[1, jnp.maximum(x - 1, 0), row, :]
                right = post[2, jnp.minimum(x + 1, far), row, :]
                total = total + pick(x == 0, jnp.zeros_like(left), left) + pick(x == far, jnp.zeros_like(right), right)
                msg[2 + slot, here, :] = hadj[3 + slot, x, row, :] + jnp.where(label[x, row, :] == 2, total, 0.0)
            return carry

        lax.fori_loop(0, depth, rows_of, 0)
        msg[4] = jnp.zeros((depth, columns), F32)
        msg[4, 0:1, :] = post[1, far, 0:1, :]
        msg[4, 1:2, :] = post[1, far, last : last + 1, :]
        msg[4, 2:3, :] = post[2, 0, 0:1, :]
        msg[4, 3:4, :] = post[2, 0, last : last + 1, :]

    return call(
        kernel,
        "second_boundary",
        "vvvvvvvvvvv",
        [vmem(7, *cells), vmem(7, *cells), vmem(4, *cells), vmem(17, depth, columns)],
        (source, rows_in, face_a, face_b, porosity, label, adjoint, heat_adjoint, post, heat, aux),
        scratch=[pltpu.VMEM((19, rows, columns), F32)],
        aliases={8: 0, 9: 1, 10: 2},
        micros=0.0,
    )


def plane_of(ref, slot):
    return ref[SEEDS + 16 * slot : SEEDS + 16 * (slot + 1)]


def second_faces(post, heat_adjoint, adjoint, label, rows_in, aux, heat, porosity, chosen):
    depth, rows, columns = label.shape
    far = depth - 1

    def kernel(post, hadj, adj, label, rows_ref, aux, heat, porosity, chosen, a_ref, b_ref):
        even = lax.rem(lax.axis_index("gx"), 2) == 0

        def partial(x, other):
            total = post[0, x] + other
            total = total + shift_y(post[3, x], 1, rows_ref[0, x : x + 1, :])
            total = total + shift_y(post[4, x], -1, rows_ref[1, x : x + 1, :])
            return total + shift_z(post[5, x], 1) + shift_z(post[6, x], -1)

        def put(start, high, low):
            where = slice(start, start + high.shape[0])
            a_ref[where] = pick(even, high, low)
            b_ref[where] = pick(even, low, high)

        put(0, post[1, far], post[2, 0])
        high_seed = hadj[2, far] + jnp.where(label[far] == 2, partial(far, post[1, far - 1]), 0.0)
        low_seed = hadj[1, 0] + jnp.where(label[0] == 2, partial(0, post[2, 1]), 0.0)
        put(rows, high_seed, low_seed)
        place = lax.broadcasted_iota(jnp.int32, (8, columns), 0)

        def spread(slot):
            return jnp.broadcast_to(rows_ref[4, slot : slot + 1, :], (8, columns))

        put(2 * rows, jnp.where(place == 0, spread(1), spread(0)), jnp.where(place == 0, spread(3), spread(2)))
        for slot in range(5):
            i, j = FPLUS[slot], FMINUS[slot]
            low, high = adj[i, 0], adj[j, far]
            if VEL[i][1]:
                low = shift_y(low, -VEL[i][1], rows_ref[adjoint_slot(i), 0:1, :])
                high = shift_y(high, -VEL[j][1], rows_ref[adjoint_slot(j), far : far + 1, :])
            put(SEEDS + 16 * slot, high, low)
        put(SEEDS + 80, jnp.where(label[far] == 2, 1.0, 0.0), jnp.where(label[0] == 2, 1.0, 0.0))
        highs = source_weights(aux, heat, porosity, label, chosen, far, 1)
        lows = source_weights(aux, heat, porosity, label, chosen, 0, 2)
        for slot, (high, low) in enumerate(zip(highs[EARLY:], lows[EARLY:])):
            put(SEEDS + 16 * (6 + slot), high, low)

    shape = (SEEDS + 16 * (11 - EARLY), columns)
    return call(
        kernel,
        "second_faces",
        "v" * 9,
        [vmem(*shape)] * 2,
        (post, heat_adjoint, adjoint, label, rows_in, aux, heat, porosity, chosen),
    )


def second_adjoint(planes, name, fixed, arrived, state, micros):
    adj, hadj, post, heat, aux, porosity, label, rows_in = fixed
    cells = label.shape
    depth, rows, columns = cells
    far = depth - 1
    last = rows - 1
    first = state is None
    boundary = isinstance(planes, tuple)
    lit_planes = range(planes[0] - 1, planes[-1] + 2) if first else ((0, far) if boundary else ())

    def kernel(*refs):
        refs = list(refs)
        adj, hadj, post, heat, aux, porosity, label, rows_ref = refs[:8]
        refs = refs[8:]
        if boundary:
            sa, sb = refs[:2]
        refs = refs[len(arrived) :]
        if not first:
            refs = refs[3:]
        lam, sens, lit = refs[:3]
        msg = refs[3] if boundary else None
        sides = refs[4] if boundary else None
        moved = refs[-1]
        even = lax.rem(lax.axis_index("gx"), 2) == 0
        tail = 2 * rows

        def from_left(where):
            return pick(even, sb[where], sa[where])

        def from_right(where):
            return pick(even, sa[where], sb[where])

        def light(x):
            here = pl.ds(x, 1)
            before, after = neighbour(x, -1, far), neighbour(x, 1, far)
            total = post[0, x]
            total = total + (from_left(slice(0, rows)) if before is None else post[1, before])
            total = total + (from_right(slice(0, rows)) if after is None else post[2, after])
            total = total + shift_y(post[3, x], 1, rows_ref[0, here, :])
            total = total + shift_y(post[4, x], -1, rows_ref[1, here, :])
            total = total + shift_z(post[5, x], 1) + shift_z(post[6, x], -1)
            lit[x] = jnp.where(label[x] == 2, total, 0.0)

        if lit_planes:
            for_planes(lit_planes, light)

        def body(x):
            here = pl.ds(x, 1)
            before, after = neighbour(x, -1, far), neighbour(x, 1, far)
            glow = lit[x]
            moved[19] = hadj[0, x] + glow
            if after is None:
                moved[20] = from_right(slice(rows, tail)) + pick(even, plane_of(sa, 5), plane_of(sb, 5)) * post[1, far]
            else:
                moved[20] = hadj[1, after] + lit[after]
            if before is None:
                moved[21] = from_left(slice(rows, tail)) + pick(even, plane_of(sb, 5), plane_of(sa, 5)) * post[2, 0]
            else:
                moved[21] = hadj[2, before] + lit[before]
            above = post[3, x, last : last + 1, :]
            below = post[4, x, 0:1, :]
            if before is None:
                above = above + from_left(slice(tail + 1, tail + 2))
                below = below + from_left(slice(tail, tail + 1))
            if after is None:
                above = above + from_right(slice(tail + 1, tail + 2))
                below = below + from_right(slice(tail, tail + 1))
            moved[22] = shift_y(hadj[3, x] + glow, -1, rows_ref[2, here, :] + rows_ref[15, here, :] * above)
            moved[23] = shift_y(hadj[4, x] + glow, 1, rows_ref[3, here, :] + rows_ref[16, here, :] * below)
            moved[24] = shift_z(hadj[5, x] + glow, -1)
            moved[25] = shift_z(hadj[6, x] + glow, 1)
            for i in range(19):
                moved[i] = moved_population(
                    adj,
                    i,
                    x,
                    -1,
                    adjoint_slot,
                    rows_ref,
                    lambda: pick(even, plane_of(sb, FMINUS.index(i)), plane_of(sa, FMINUS.index(i))),
                    lambda: pick(even, plane_of(sa, FPLUS.index(i)), plane_of(sb, FPLUS.index(i))),
                    far,
                )
            for r, c in tiles(rows, columns):
                inlet = label[x, r, c] == 1
                density, ux, uy, uz = (aux[i, x, r, c] for i in range(4))
                warm = [heat[i, x, r, c] for i in range(7)]
                mu = [moved[i, r, c] for i in range(19)]
                nu = [moved[19 + i, r, c] for i in range(7)]
                result, result_heat, part = collide_adjoint(
                    density, (ux, uy, uz), warm, porosity[x, r, c], inlet, mu, nu
                )
                for i, value in enumerate(result + result_heat):
                    lam[i, x, r, c] = value
                sens[x, r, c] = part

        for_planes(planes, body)
        if boundary:
            for slot in range(6):
                sides[slot] = lam[PLUS[slot], 0]
                sides[6 + slot] = lam[MINUS[slot], far]

            def rows_of(x, carry):
                here = pl.ds(x, 1)
                for i in YPLUS:
                    msg[row_slot(i), here, :] = lam[i, x, 0:1, :]
                for i in YMINUS:
                    msg[row_slot(i), here, :] = lam[i, x, last : last + 1, :]
                return carry

            lax.fori_loop(0, depth, rows_of, 0)

    outs = [vmem(COUNT, *cells), vmem(*cells), vmem(*cells)]
    if boundary:
        outs += [vmem(12, depth, columns), vmem(12, rows, columns)]
    args = fixed + arrived + (() if first else state)
    base = len(args) - 3
    return call(
        kernel,
        name,
        "v" * len(args),
        outs,
        args,
        scratch=[pltpu.VMEM((COUNT, rows, columns), F32)],
        aliases=None if first else {base: 0, base + 1: 1, base + 2: 2},
        micros=micros,
    )


def arriving(lam, rows_ref, moved, x, far, low, high):
    for i in range(COUNT):
        moved[i] = moved_population(
            lam, i, x, -1, row_slot, rows_ref, lambda: low(MINUS.index(i)), lambda: high(PLUS.index(i)), far
        )


def first_sensitivity(lam, rows_in, fixed, sens_one, weights_a, weights_b, rate_a, rate_b, waves):
    aux, heat, porosity, label, chosen = fixed
    depth, rows, columns = label.shape
    far = depth - 1
    half = columns // 2
    count = depth + 2

    def kernel(lam, rows_ref, aux, heat, porosity, label, chosen, sens_ref, a_ref, b_ref, ra_ref, rb_ref, waves_ref,
               own, other, moved, total):
        even = lax.rem(lax.axis_index("gx"), 2) == 0
        core = lax.axis_index("gy")

        def nothing(slot):
            return jnp.zeros((rows, columns), F32)

        def body(x):
            arriving(lam, rows_ref, moved, x, far, nothing, nothing)
            for r, c in tiles(rows, columns):
                inlet = label[x, r, c] == 1
                density, ux, uy, uz = (aux[i, x, r, c] for i in range(4))
                warm = [heat[i, x, r, c] for i in range(7)]
                mu = [moved[i, r, c] for i in range(19)]
                nu = [moved[19 + i, r, c] for i in range(7)]
                _, _, part = collide_adjoint(density, (ux, uy, uz), warm, porosity[x, r, c], inlet, mu, nu)
                total[x, r, c] = jnp.where(chosen[x, r, c] > 0.0, part + sens_ref[x, r, c], 0.0)

        for_planes((0, far), body)
        for_planes(range(1, far), body)
        def weights(slot, reverse):
            if slot < EARLY:
                of_a, of_b = ra_ref[6 + slot], rb_ref[6 + slot]
            else:
                of_a, of_b = plane_of(a_ref, 6 + slot - EARLY), plane_of(b_ref, 6 + slot - EARLY)
            return pick(even, of_b, of_a) if reverse else pick(even, of_a, of_b)

        for place, x, members, reverse in ((depth, 0, PLUS, True), (depth + 1, far, MINUS, False)):
            rate, scale, *vector = (weights(slot, reverse) for slot in range(5))
            speed = vector[0] * vector[0] + vector[1] * vector[1] + vector[2] * vector[2]
            result = jnp.zeros((rows, columns), F32)
            for i in members:
                value = lam[i, x]
                if VEL[i][1]:
                    value = shift_y(value, -VEL[i][1], rows_ref[row_slot(i), x : x + 1, :])
                value = shift_z(value, -VEL[i][2])
                if i < 19:
                    part = along(VEL[i], vector)
                    result = result + (fluid_wts[i] * scale) * (part - speed + 3.0 * part * part) * value
                else:
                    result = result + rate * value
            total[place] = result
        flat = total[...].reshape(count * rows, columns)
        own[...] = multiply(flat, waves_ref[core]).reshape(count, rows, half)
        other[...] = multiply(flat, waves_ref[1 - core]).reshape(count, rows, half)

    args = (lam, rows_in) + fixed + (sens_one, weights_a, weights_b, rate_a, rate_b, waves)
    return call(
        kernel,
        "first_sensitivity",
        "v" * len(args),
        [vmem(count, rows, half)] * 2,
        args,
        scratch=[pltpu.VMEM((COUNT, rows, columns), F32), pltpu.VMEM((count, rows, columns), F32)],
    )


def first_adjoint(groups, name, lam, rows_in, fixed, arrived, early_planes, early):
    aux, heat, porosity, label = fixed
    cells = label.shape
    depth, rows, columns = cells
    far = depth - 1
    planes = [x for group in groups for x in group]
    count = len(planes)
    last = early is not None

    def kernel(*refs):
        refs = list(refs)
        lam, rows_ref, aux, heat, porosity, label = refs[:6]
        refs = refs[6:]
        if last:
            b_ref, a_ref, early_ref, fluid_out, heat_out, token, moved, out, sem = refs
            token[...] = jnp.zeros((8, 128), F32)
        else:
            out, moved = refs
        even = lax.rem(lax.axis_index("gx"), 2) == 0

        def place(x):
            return planes.index(x) if isinstance(x, int) else x - groups[-1][0] + count - len(groups[-1])

        def writes(source, n, x, slot):
            return (
                pltpu.make_async_copy(source.at[0:19, n], fluid_out.at[:, x], sem.at[2 * slot]),
                pltpu.make_async_copy(source.at[19:26, n], heat_out.at[:, x], sem.at[2 * slot + 1]),
            )

        def low(slot):
            return pick(even, b_ref[slot], a_ref[slot])

        def high(slot):
            return pick(even, a_ref[slot], b_ref[slot])

        def body(x):
            n = place(x)
            arriving(lam, rows_ref, moved, x, far, low, high)
            for r, c in tiles(rows, columns):
                inlet = label[x, r, c] == 1
                density, ux, uy, uz = (aux[i, x, r, c] for i in range(4))
                warm = [heat[i, x, r, c] for i in range(7)]
                mu = [moved[i, r, c] for i in range(19)]
                nu = [moved[19 + i, r, c] for i in range(7)]
                result, result_heat, _ = collide_adjoint(density, (ux, uy, uz), warm, porosity[x, r, c], inlet, mu, nu)
                for i, value in enumerate(result + result_heat):
                    out[i, n, r, c] = value
            if last:
                for copy in writes(out, n, x, n):
                    copy.start()

        early_copies = []
        if last:
            for n, x in enumerate(early_planes):
                early_copies += writes(early_ref, n, x, count + n)
        for copy in early_copies:
            copy.start()
        for group in groups:
            for_planes(group, body)
        if last:

            def finish(x):
                for copy in writes(out, place(x), x, place(x)):
                    copy.wait()

            for group in groups:
                for_planes(group, finish)
        for copy in early_copies:
            copy.wait()

    buffer = (COUNT, count, rows, columns)
    moved = pltpu.VMEM((COUNT, rows, columns), F32)
    args = (lam, rows_in) + fixed + arrived + ((early,) if last else ())
    if last:
        outs = [hbm(19, *cells), hbm(7, *cells), vmem(8, 128)]
        scratch = [moved, pltpu.VMEM(buffer, F32), pltpu.SemaphoreType.DMA((2 * (count + len(early_planes)),))]
    else:
        outs = [vmem(*buffer)]
        scratch = [moved]
    return call(kernel, name, "v" * len(args), outs, args, scratch=scratch)


def multiply(first, second):
    return jnp.dot(first, second, precision=lax.Precision.HIGHEST, preferred_element_type=F32)


def hartley(length):
    index = np.arange(length)
    angle = 2.0 * np.pi * ((index[:, None] * index[None, :]) % length) / length
    return (np.cos(angle) + np.sin(angle)) / np.sqrt(length)


def filter_tables(depth, count_y, count_z):
    half = count_z // 2
    wave_z = hartley(count_z)
    waves = np.stack([wave_z[:, :half], wave_z[:, half:]]).astype(np.float32)
    waves_back = np.stack([wave_z[:half], wave_z[half:]]).astype(np.float32)
    wave_y = np.kron(np.eye(depth), hartley(count_y)).astype(np.float32)
    wave_ends = np.kron(np.eye(2), hartley(count_y)).astype(np.float32)
    symbol_y = 2.0 - 2.0 * np.cos(2.0 * np.pi * np.arange(count_y) / count_y)
    symbol_z = 2.0 - 2.0 * np.cos(2.0 * np.pi * np.arange(count_z) / count_z)
    weight = float(RADIUS * RADIUS)
    centre = (1.0 + weight * (2.0 + symbol_y[:, None] + symbol_z[None, :])) / weight
    ratio = 2.0 / (centre + np.sqrt(centre * centre - 4.0))
    peak = 1.0 / (weight * (1.0 / ratio - ratio))
    fields = np.stack([ratio, np.log(ratio) * depth, peak]).astype(np.float32)
    fields = np.stack([fields[:, :, :half], fields[:, :, half:]])
    return waves, waves_back, wave_y, wave_ends, fields


def to_modes(own, other, wave_y, wave_ends, fields):
    count, rows, half = own.shape
    depth = count - 2
    full = 2 * rows
    inside = depth * full

    def kernel(own_ref, other_ref, wave_ref, small_ref, field_ref, modes, ends, both):
        core = lax.axis_index("gy")
        for x in range(count):
            both[x * full : x * full + rows] = own_ref[x]
            both[x * full + rows : (x + 1) * full] = other_ref[x]
        modes[0:inside] = multiply(wave_ref[...], both[0:inside])
        modes[inside : inside + 2 * full] = multiply(small_ref[...], both[inside : inside + 2 * full])
        ratio = field_ref[core, 0]
        before, after = modes[inside : inside + full], modes[inside + full : inside + 2 * full]
        head = before
        for x in range(depth):
            head = head * ratio + modes[x * full : (x + 1) * full]
        ends[0] = head * ratio + after
        tail = after
        for x in range(depth - 1, -1, -1):
            tail = tail * ratio + modes[x * full : (x + 1) * full]
        ends[1] = tail * ratio + before

    return call(
        kernel,
        "to_modes",
        "vvvvv",
        [vmem(count * full, half), vmem(2, full, half)],
        (own, other, wave_y, wave_ends, fields),
        scratch=[pltpu.VMEM((count * full, half), F32)],
    )


def join_segments(ends, arrived, carry, fields, reach, after):
    first = carry is None

    def kernel(*refs):
        ends_ref, in_ref, field_ref = refs[:3]
        carry_ref = None if first else refs[3]
        ends_out, carry_out = refs[-2:]
        core = lax.axis_index("gy")
        index = lax.axis_index("gx")
        place = lax.rem(index, reach)
        upper = lax.rem(lax.div(index, reach), 2) == 1
        rate = field_ref[core, 1]
        whole = jnp.exp(rate * float(reach))
        forward = jnp.exp(rate * place.astype(F32))
        backward = jnp.exp(rate * (reach - 1 - place).astype(F32))
        head, tail = ends_ref[0], ends_ref[1]
        head_in, tail_in = in_ref[0], in_ref[1]
        left = pick(upper, forward * head_in, jnp.zeros_like(head))
        right = pick(upper, jnp.zeros_like(head), backward * tail_in)
        carry_out[0] = left if first else carry_ref[0] + left
        carry_out[1] = right if first else carry_ref[1] + right
        ends_out[0] = pick(upper, head + whole * head_in, head_in + whole * head)
        ends_out[1] = pick(upper, tail_in + whole * tail, tail + whole * tail_in)

    args = (ends, arrived, fields) + (() if first else (carry,)) + after
    return call(kernel, "join_segments", "v" * len(args), [vmem(*ends.shape)] * 2, args, micros=0.0)


def from_modes(modes, ends, carry, wave_y, fields, depth, parts, after):
    half = modes.shape[1]
    full = modes.shape[0] // (depth + 2)
    rows = full // 2
    inside = depth * full

    def kernel(modes_ref, ends_ref, carry_ref, wave_ref, field_ref, after_ref, own, other, solved):
        core = lax.axis_index("gy")
        index = lax.axis_index("gx")
        ratio, rate, peak = field_ref[core, 0], field_ref[core, 1], field_ref[core, 2]
        around = 1.0 / (1.0 - jnp.exp(rate * float(parts)))
        left = carry_ref[0] + jnp.exp(rate * index.astype(F32)) * around * ends_ref[0]
        right = carry_ref[1] + jnp.exp(rate * (parts - 1 - index).astype(F32)) * around * ends_ref[1]
        run = left + ratio * modes_ref[inside : inside + full]
        for x in range(depth):
            run = run + modes_ref[x * full : (x + 1) * full]
            solved[x * full : (x + 1) * full] = run
            run = run * ratio
        run = right + ratio * modes_ref[inside + full : inside + 2 * full]
        for x in range(depth - 1, -1, -1):
            solved[x * full : (x + 1) * full] = peak * (solved[x * full : (x + 1) * full] + run)
            run = ratio * (run + modes_ref[x * full : (x + 1) * full])
        back = multiply(wave_ref[...], solved[...])
        for x in range(depth):
            own[x * rows : (x + 1) * rows] = back[x * full : x * full + rows]
            other[x * rows : (x + 1) * rows] = back[x * full + rows : (x + 1) * full]

    flat = (depth * rows, half)
    return call(
        kernel,
        "from_modes",
        "vvvvvv",
        [vmem(*flat)] * 2,
        (modes, ends, carry, wave_y, fields, after),
        scratch=[pltpu.VMEM((inside, half), F32)],
    )


def last_transform(own, other, waves_back, depth):
    flat, half = own.shape
    rows = flat // depth

    def kernel(own_ref, other_ref, wave_ref, out_ref, out, sem):
        core = lax.axis_index("gy")
        result = multiply(own_ref[...], wave_ref[core]) + multiply(other_ref[...], wave_ref[1 - core])
        out[...] = result.reshape(depth, rows, 2 * half)
        copy = pltpu.make_async_copy(out, out_ref, sem.at[0])
        copy.start()
        copy.wait()

    shape = (depth, rows, 2 * half)
    return call(
        kernel,
        "last_transform",
        "vvv",
        [hbm(*shape)],
        (own, other, waves_back),
        scratch=[pltpu.VMEM(shape, F32), pltpu.SemaphoreType.DMA((1,))],
    )


def per_device(fluid_state, heat_state, design, cell_type, boundary, fluid_adjoint, heat_adjoint):
    depth, rows, columns = design.shape
    far = depth - 1
    parts = lax.axis_size("gx")
    waves, waves_back, wave_y, wave_ends, fields = filter_tables(depth, 2 * rows, columns)

    pairs_a = [(i, i ^ 1) for i in range(parts)]
    pairs_b = [(i, (i + 1) % parts if i % 2 else (i - 1) % parts) for i in range(parts)]

    def across(value):
        return lax.ppermute(value, "gy", [(0, 1), (1, 0)])

    def sideways(first, second):
        first = lax.ppermute(first, "gx", pairs_a)
        second = lax.ppermute(second, "gx", pairs_b)
        return first, second

    adj, hadj = fluid_adjoint, heat_adjoint
    post, heat_edge, aux_edge, porosity, label, chosen, sides, corner = first_boundary(
        *(in_hbm(value) for value in (fluid_state, heat_state, design, cell_type, boundary))
    )
    face_a, face_b, token = first_faces(sides, across(corner), label, aux_edge, heat_edge, porosity, chosen)
    face_a, face_b = sideways(face_a, face_b)
    rate_a, rate_b = face_a, face_b
    heat_zero = heat_state
    post, aux_zero, rows_one = first_interior(
        fluid_state, heat_zero, post, aux_edge, porosity, label, token
    )
    rows_one = across(rows_one)
    post_one, heat_one, aux_one = second_interior(post, rows_one, porosity, label)
    post_one, heat_one, aux_one, rows_heat = second_boundary(
        post, rows_one, face_a, face_b, porosity, label, adj, hadj, post_one, heat_one, aux_one
    )
    rows_heat = across(rows_heat)
    seed_a, seed_b = second_faces(post_one, hadj, adj, label, rows_heat, aux_zero, heat_zero, porosity, chosen)
    seed_a, seed_b = sideways(seed_a, seed_b)
    fixed = (adj, hadj, post_one, heat_one, aux_one, porosity, label, rows_heat)
    state = second_adjoint(range(2, far - 1), "adjoint_inner", fixed, (), None, 0.0)
    lam, sens_one, lit, rows_two, sides = second_adjoint(
        (0, 1, far - 1, far), "adjoint_outer", fixed, (seed_a, seed_b), tuple(state), 0.0
    )
    rows_two = across(rows_two)
    face_a, face_b = costate_faces(sides, rows_two)
    face_a, face_b = sideways(face_a, face_b)
    fixed = (aux_zero, heat_zero, porosity, label)
    own, other = first_sensitivity(lam, rows_two, fixed + (chosen,), sens_one, seed_a, seed_b, rate_a, rate_b, waves)
    early = first_adjoint(((1,),), "costate_early", lam, rows_two, fixed, (), None, None)
    fluid_costate, heat_costate, token = first_adjoint(
        ((0, far), range(2, far)), "costate_rest", lam, rows_two, fixed, (face_b, face_a), (1,), early
    )
    other = across(other)
    modes, ends = to_modes(own, other, wave_y, wave_ends, fields)
    carry = None
    reach = 1
    while reach < parts:
        arrived = lax.ppermute(ends, "gx", [(i, i ^ reach) for i in range(parts)])
        ends, carry = join_segments(ends, arrived, carry, fields, reach, (early,) if reach == 1 else ())
        reach = 2 * reach
    own, other = from_modes(modes, ends, carry, wave_y, fields, depth, parts, token)
    other = across(other)
    return (fluid_costate, heat_costate, last_transform(own, other, waves_back, depth))


def solution(mesh):
    return jax.shard_map(
        per_device,
        mesh=mesh,
        in_specs=(
            P(None, ("case", "gx"), "gy", None),
            P(None, ("case", "gx"), "gy", None),
            P(("case", "gx"), "gy", None),
            P(("case", "gx"), "gy", None),
            P(("case", "gx"), "gy", None),
            P(None, ("case", "gx"), "gy", None),
            P(None, ("case", "gx"), "gy", None),
        ),
        out_specs=(
            P(None, ("case", "gx"), "gy", None),
            P(None, ("case", "gx"), "gy", None),
            P(("case", "gx"), "gy", None),
        ),
        check_vma=False,
    )
```

```python
import numpy as np
import jax
import jax.numpy as jnp
from jax import lax
from jax.experimental import pallas as pl
from jax.experimental.pallas import tpu as pltpu
from jax.sharding import PartitionSpec as P

RADIUS = 4

fluid_vel = [
    (0, 0, 0),
    (1, 0, 0),
    (-1, 0, 0),
    (0, 1, 0),
    (0, -1, 0),
    (0, 0, 1),
    (0, 0, -1),
    (1, 1, 0),
    (-1, -1, 0),
    (1, -1, 0),
    (-1, 1, 0),
    (1, 0, 1),
    (-1, 0, -1),
    (1, 0, -1),
    (-1, 0, 1),
    (0, 1, 1),
    (0, -1, -1),
    (0, 1, -1),
    (0, -1, 1),
]
fluid_wts = [1.0 / 3.0] + [1.0 / 18.0] * 6 + [1.0 / 36.0] * 12
inlet_speed = 0.05
inlet_eq = [
    weight
    * (
        1.0
        + 3.0 * inlet_speed * entry[2]
        + 4.5 * (inlet_speed * entry[2]) ** 2
        - 1.5 * inlet_speed**2
    )
    for entry, weight in zip(fluid_vel, fluid_wts)
]

VEL = fluid_vel + fluid_vel[:7]
COUNT = len(VEL)
PLUS = [i for i in range(COUNT) if VEL[i][0] == 1]
MINUS = [i for i in range(COUNT) if VEL[i][0] == -1]
YPLUS = [i for i in range(COUNT) if VEL[i][1] == 1]
YMINUS = [i for i in range(COUNT) if VEL[i][1] == -1]
FPLUS = [i for i in PLUS if i < 19]
FMINUS = [i for i in MINUS if i < 19]
FYPLUS = [i for i in YPLUS if i < 19]
FYMINUS = [i for i in YMINUS if i < 19]

VMEM_BYTES = 24 * 1024 * 1024
EARLY = 3
SEEDS = 40
F32 = jnp.float32


def params():
    return pltpu.CompilerParams(vmem_limit_bytes=VMEM_BYTES)


def cost(micros):
    return pl.CostEstimate(flops=int(micros * 1e9), bytes_accessed=0, transcendentals=0)


def shift_y(value, step, ghost):
    if step == 0:
        return value
    rows = value.shape[0]
    moved = pltpu.roll(value, step % rows, 0)
    place = lax.broadcasted_iota(jnp.int32, value.shape, 0)
    edge = 0 if step > 0 else rows - 1
    return jnp.where(place == edge, jnp.broadcast_to(ghost, value.shape), moved)


def shift_z(value, step):
    if step == 0:
        return value
    return pltpu.roll(value, step % value.shape[1], 1)


def pick(flag, first, second):
    return jnp.where(flag, first, second)


def tiles(rows, columns):
    return [
        (slice(r, r + 8), slice(c, c + 128)) for r in range(0, rows, 8) for c in range(0, columns, 128)
    ]


def porosity_of(design, kind):
    return jnp.where(kind == 2, design, jnp.where(kind == 1, 0.0, 1.0))


def heat_rate_of(porosity):
    return 1.0 / (0.55 + 0.9 * (1.0 - porosity))


def moments(pops, porosity):
    density = pops[0]
    for value in pops[1:]:
        density = density + value
    diff = {i: pops[i] - pops[i + 1] for i in range(1, 19, 2)}
    flux_x = diff[1] + diff[7] + diff[9] + diff[11] + diff[13]
    flux_y = diff[3] + diff[7] - diff[9] + diff[15] + diff[17]
    flux_z = diff[5] + diff[11] - diff[13] + diff[15] - diff[17]
    inverse = (0.1 + porosity) / (density * (0.5 + 0.6 * porosity))
    return density, (flux_x * inverse, flux_y * inverse, flux_z * inverse)


def along(entry, vector):
    total = None
    for part, value in zip(entry, vector):
        if part == 0:
            continue
        if total is None:
            total = value if part == 1 else -value
        else:
            total = total + value if part == 1 else total - value
    return total


def collide_fluid(pops, density, velocity, inlet):
    speed = velocity[0] * velocity[0] + velocity[1] * velocity[1] + velocity[2] * velocity[2]
    scaled = 1.25 * density
    base = scaled - 1.5 * scaled * speed
    result = [jnp.where(inlet, inlet_eq[0], base * (1.0 / 3.0) - 0.25 * pops[0])]
    for i in range(1, 19, 2):
        weight = fluid_wts[i]
        part = along(VEL[i], velocity)
        flow = scaled * part
        even = weight * base + (4.5 * weight) * (flow * part)
        odd = (3.0 * weight) * flow
        result.append(jnp.where(inlet, inlet_eq[i], even + odd - 0.25 * pops[i]))
        result.append(jnp.where(inlet, inlet_eq[i + 1], even - odd - 0.25 * pops[i + 1]))
    return result


def collide_heat(pops, velocity, porosity, inlet):
    temper = pops[0]
    for value in pops[1:]:
        temper = temper + value
    rate = heat_rate_of(porosity)
    keep = 1.0 - rate
    warm = rate * temper
    base = warm + (1.0 - porosity)
    result = [jnp.where(inlet, 0.0, keep * pops[0] + 0.25 * base)]
    for axis in range(3):
        i = 1 + 2 * axis
        odd = 0.5 * (warm * velocity[axis])
        even = 0.125 * base
        result.append(jnp.where(inlet, 0.0, keep * pops[i] + (even + odd)))
        result.append(jnp.where(inlet, 0.0, keep * pops[i + 1] + (even - odd)))
    return result


def collide_adjoint(density, velocity, heat, porosity, inlet, mu, nu):
    ux, uy, uz = velocity
    mu = [jnp.where(inlet, 0.0, value) for value in mu]
    nu = [jnp.where(inlet, 0.0, value) for value in nu]
    even = {i: mu[i] + mu[i + 1] for i in range(1, 19, 2)}
    odd = {i: mu[i] - mu[i + 1] for i in range(1, 19, 2)}
    wa, wb = 1.0 / 18.0, 1.0 / 36.0
    xy_sum, xz_sum, yz_sum = even[7] + even[9], even[11] + even[13], even[15] + even[17]
    m0 = mu[0] * (1.0 / 3.0) + wa * (even[1] + even[3] + even[5]) + wb * (xy_sum + xz_sum + yz_sum)
    m1x = wa * odd[1] + wb * (odd[7] + odd[9] + odd[11] + odd[13])
    m1y = wa * odd[3] + wb * (odd[7] - odd[9] + odd[15] + odd[17])
    m1z = wa * odd[5] + wb * (odd[11] - odd[13] + odd[15] - odd[17])
    mxx = wa * even[1] + wb * (xy_sum + xz_sum)
    myy = wa * even[3] + wb * (xy_sum + yz_sum)
    mzz = wa * even[5] + wb * (xz_sum + yz_sum)
    mxy = wb * (even[7] - even[9])
    mxz = wb * (even[11] - even[13])
    myz = wb * (even[15] - even[17])
    vx = mxx * ux + mxy * uy + mxz * uz
    vy = mxy * ux + myy * uy + myz * uz
    vz = mxz * ux + myz * uy + mzz * uz
    speed = ux * ux + uy * uy + uz * uz
    slope = (
        m0 * (1.0 - 1.5 * speed)
        + 3.0 * (ux * m1x + uy * m1y + uz * m1z)
        + 4.5 * (ux * vx + uy * vy + uz * vz)
    )
    rate = heat_rate_of(porosity)
    keep = 1.0 - rate
    temper = heat[0]
    for value in heat[1:]:
        temper = temper + value
    n0 = 0.25 * nu[0] + 0.125 * (nu[1] + nu[2] + nu[3] + nu[4] + nu[5] + nu[6])
    n1x, n1y, n1z = (0.125 * (nu[i] - nu[i + 1]) for i in (1, 3, 5))
    warm = 4.0 * rate * temper
    scaled = 3.75 * density
    bar_x = scaled * (m1x - m0 * ux + 3.0 * vx) + warm * n1x
    bar_y = scaled * (m1y - m0 * uy + 3.0 * vy) + warm * n1y
    bar_z = scaled * (m1z - m0 * uz + 3.0 * vz) + warm * n1z
    work = bar_x * ux + bar_y * uy + bar_z * uz
    ramp = 0.1 + porosity
    drag = 0.5 + 0.6 * porosity
    over = 1.0 / (density * drag)
    inverse = ramp * over
    b = (bar_x * inverse, bar_y * inverse, bar_z * inverse)
    a = 1.25 * slope - work * (drag * over)
    lam = [a - 0.25 * mu[0]]
    for i in range(1, 19, 2):
        part = along(VEL[i], b)
        lam.append((a + part) - 0.25 * mu[i])
        lam.append((a - part) - 0.25 * mu[i + 1])
    pull = n0 + 4.0 * (ux * n1x + uy * n1y + uz * n1z)
    a_heat = rate * pull
    lam_heat = [keep * value + a_heat for value in nu]
    dot = nu[0] * heat[0]
    for first, second in zip(nu[1:], heat[1:]):
        dot = dot + first * second
    sens = work * (0.44 / (ramp * drag)) - n0 + (0.9 * rate * rate) * (temper * pull - dot)
    return lam, lam_heat, sens


IN_VMEM = pl.BlockSpec(memory_space=pltpu.VMEM)
IN_HBM = pl.BlockSpec(memory_space=pltpu.HBM)


def vmem(*shape):
    return pltpu.VMEM(shape, F32)


def hbm(*shape):
    return pltpu.HBM(shape, F32)


def in_hbm(value):
    return pltpu.with_memory_space_constraint(value, pltpu.HBM)


def call(kernel, name, specs, outs, args, scratch=(), aliases=None, micros=0.0):
    spec_of = {"v": IN_VMEM, "h": IN_HBM}
    single = len(outs) == 1
    args = [
        pltpu.with_memory_space_constraint(value, pltpu.VMEM) if letter == "v" else value
        for letter, value in zip(specs, args)
    ]
    out_specs = [IN_HBM if out.memory_space == pltpu.HBM else IN_VMEM for out in outs]
    return pl.pallas_call(
        kernel,
        in_specs=[spec_of[letter] for letter in specs],
        out_specs=out_specs[0] if single else out_specs,
        out_shape=outs[0] if single else outs,
        scratch_shapes=list(scratch),
        input_output_aliases=aliases or {},
        compiler_params=params(),
        cost_estimate=cost(micros),
        name=name,
    )(*args)


def row_slot(i):
    return YPLUS.index(i) if VEL[i][1] > 0 else 6 + YMINUS.index(i)


def adjoint_slot(i):
    return 5 + FYPLUS.index(i) if VEL[i][1] > 0 else 10 + FYMINUS.index(i)


def for_planes(planes, body):
    if isinstance(planes, tuple):
        for x in planes:
            body(x)
    else:

        def step(x, carry):
            body(x)
            return carry

        lax.fori_loop(planes[0], planes[-1] + 1, step, 0)


def neighbour(x, step, far):
    plane = x + step
    if isinstance(x, int) and (plane < 0 or plane > far):
        return None
    return plane


def moved_population(source, i, x, direction, slot_of, rows_ref, low, high, far):
    step = tuple(direction * part for part in VEL[i])
    plane = neighbour(x, -step[0], far)
    if plane is None:
        value = low() if step[0] == 1 else high()
    else:
        value = source[i, plane]
        if step[1]:
            value = shift_y(value, step[1], rows_ref[slot_of(i), pl.ds(plane, 1), :])
    return shift_z(value, step[2])


def corner_rows(direction):
    return ((7, -1), (9, -1), (8, 0), (10, 0)) if direction == 1 else ((7, 0), (9, 0), (8, -1), (10, -1))


def collide_plane(x, fluid, heat, post, aux, porosity, label):
    _, _, rows, columns = post.shape
    for r, c in tiles(rows, columns):
        phi = porosity[x, r, c]
        inlet = label[x, r, c] == 1
        pops = [fluid[i, x, r, c] for i in range(19)]
        density, velocity = moments(pops, phi)
        for i, value in enumerate((density,) + velocity):
            aux[i, x, r, c] = value
        warm = [heat[i, x, r, c] for i in range(7)]
        result = collide_fluid(pops, density, velocity, inlet) + collide_heat(warm, velocity, phi, inlet)
        for i, value in enumerate(result):
            post[i, x, r, c] = value


def first_boundary(fluid, heat, design, kind, label):
    cells = design.shape
    depth, rows, columns = cells
    far = depth - 1
    last = rows - 1

    def kernel(fluid_in, heat_in, design_in, kind_in, label_in, post, heat, aux, porosity, label, chosen,
               sides, corner, design, kind, sem):
        fields = (
            pltpu.make_async_copy(design_in, design, sem.at[0]),
            pltpu.make_async_copy(kind_in, kind, sem.at[1]),
            pltpu.make_async_copy(label_in, label, sem.at[2]),
        )
        loads = []
        for n, x in enumerate((0, far)):
            loads.append(pltpu.make_async_copy(fluid_in.at[:, x], post.at[0:19, x], sem.at[3 + 2 * n]))
            loads.append(pltpu.make_async_copy(heat_in.at[:, x], heat.at[:, x], sem.at[4 + 2 * n]))
        for copy in fields + tuple(loads):
            copy.start()
        for copy in fields:
            copy.wait()

        def prepare(x, carry):
            kinds = kind[x]
            porosity[x] = porosity_of(design[x], kinds)
            chosen[x] = jnp.where(kinds == 2, 1.0, 0.0)
            return carry

        lax.fori_loop(0, depth, prepare, 0)
        for copy in loads:
            copy.wait()
        collide_plane(0, post, heat, post, aux, porosity, label)
        collide_plane(far, post, heat, post, aux, porosity, label)
        for slot in range(6):
            sides[slot] = post[PLUS[slot], far]
            sides[6 + slot] = post[MINUS[slot], 0]
        corner[...] = jnp.zeros((8, columns), F32)
        for slot, (i, x) in enumerate(corner_rows(1)):
            y = last if VEL[i][1] > 0 else 0
            corner[slot : slot + 1, :] = post[i, x % depth, y : y + 1, :]

    return call(
        kernel,
        "first_boundary",
        "hhhhh",
        [
            vmem(COUNT, *cells),
            vmem(7, *cells),
            vmem(4, *cells),
            vmem(*cells),
            pltpu.VMEM(cells, jnp.int32),
            vmem(*cells),
            vmem(12, rows, columns),
            vmem(8, columns),
        ],
        (fluid, heat, design, kind, label),
        scratch=[pltpu.VMEM(cells, F32), pltpu.VMEM(cells, jnp.int32), pltpu.SemaphoreType.DMA((7,))],
    )


def first_interior(fluid, heat, post, aux, porosity, label, after):
    cells = label.shape
    depth, rows, columns = cells
    far = depth - 1
    last = rows - 1

    def kernel(fluid, heat, post_in, aux_in, porosity, label, after_ref, post, aux, msg):
        for_planes(range(1, far), lambda x: collide_plane(x, fluid, heat, post, aux, porosity, label))

        def rows_of(x, carry):
            here = pl.ds(x, 1)
            for i in YPLUS:
                msg[row_slot(i), here, :] = post[i, x, last : last + 1, :]
            for i in YMINUS:
                msg[row_slot(i), here, :] = post[i, x, 0:1, :]
            return carry

        lax.fori_loop(0, depth, rows_of, 0)

    return call(
        kernel,
        "first_interior",
        "vvvvvvv",
        [vmem(COUNT, *cells), vmem(4, *cells), vmem(12, depth, columns)],
        (fluid, heat, post, aux, porosity, label, after),
        aliases={2: 0, 3: 1},
        micros=1.0,
    )


def source_weights(aux, heat, porosity, label, chosen, x, k):
    density, ux, uy, uz = (aux[i, x] for i in range(4))
    phi = porosity[x]
    valid = jnp.logical_and(label[x] != 1, chosen[x] > 0.0)
    over = 0.44 / ((0.1 + phi) * (0.5 + 0.6 * phi))
    rate = heat_rate_of(phi)
    temper = heat[0, x]
    for i in range(1, 7):
        temper = temper + heat[i, x]
    part = along(VEL[k], (ux, uy, uz))
    weight = over * (0.5 * rate * temper) * part - 0.125
    weight = weight + (0.9 * rate * rate) * (temper * (0.125 + 0.5 * part) - heat[k, x])
    scale = jnp.where(valid, 3.75 * over * density, 0.0)
    return jnp.where(valid, weight, 0.0), scale, ux, uy, uz


def crossing_sides(sides_ref, row_of, direction, slot):
    i, j = PLUS[slot], MINUS[slot]
    plus, minus = sides_ref[slot], sides_ref[6 + slot]
    if VEL[i][1]:
        plus = shift_y(plus, direction * VEL[i][1], row_of(i))
        minus = shift_y(minus, direction * VEL[j][1], row_of(j))
    return (plus, minus) if direction == 1 else (minus, plus)


def first_faces(sides, rows_in, label, aux, heat, porosity, chosen):
    _, rows, columns = sides.shape
    far = label.shape[0] - 1

    def kernel(sides_ref, rows_ref, label, aux, heat, porosity, chosen, a_ref, b_ref, token):
        token[...] = jnp.zeros((8, 128), F32)
        even = lax.rem(lax.axis_index("gx"), 2) == 0

        def row_of(i):
            slot = [entry[0] for entry in corner_rows(1)].index(i)
            return rows_ref[slot : slot + 1, :]

        for slot in range(6):
            high, low = crossing_sides(sides_ref, row_of, 1, slot)
            a_ref[slot] = pick(even, high, low)
            b_ref[slot] = pick(even, low, high)
        highs = source_weights(aux, heat, porosity, label, chosen, far, 1)
        lows = source_weights(aux, heat, porosity, label, chosen, 0, 2)
        for slot in range(EARLY):
            a_ref[6 + slot] = pick(even, highs[slot], lows[slot])
            b_ref[6 + slot] = pick(even, lows[slot], highs[slot])

    return call(
        kernel,
        "first_faces",
        "v" * 7,
        [vmem(6 + EARLY, rows, columns)] * 2 + [vmem(8, 128)],
        (sides, rows_in, label, aux, heat, porosity, chosen),
    )


def costate_faces(sides, rows_in):
    _, rows, columns = sides.shape

    def kernel(sides_ref, rows_ref, a_ref, b_ref):
        even = lax.rem(lax.axis_index("gx"), 2) == 0
        far = rows_ref.shape[1] - 1

        def row_of(i):
            x = 0 if VEL[i][0] > 0 else far
            return rows_ref[row_slot(i), x : x + 1, :]

        for slot in range(6):
            high, low = crossing_sides(sides_ref, row_of, -1, slot)
            a_ref[slot] = pick(even, high, low)
            b_ref[slot] = pick(even, low, high)

    return call(kernel, "costate_faces", "vv", [vmem(6, rows, columns)] * 2, (sides, rows_in))


def second_planes(planes, source, rows_ref, low, high, porosity_ref, label_ref, post, heat, aux, moved):
    _, depth, rows, columns = source.shape
    far = depth - 1

    def body(x):
        for i in range(COUNT):
            value = moved_population(
                source, i, x, 1, row_slot, rows_ref, lambda: low(PLUS.index(i)), lambda: high(MINUS.index(i)), far
            )
            if i < 19:
                moved[i] = value
            else:
                heat[i - 19, x] = value
        for r, c in tiles(rows, columns):
            porosity = porosity_ref[x, r, c]
            inlet = label_ref[x, r, c] == 1
            pops = [moved[i, r, c] for i in range(19)]
            density, velocity = moments(pops, porosity)
            for i, value in enumerate((density,) + velocity):
                aux[i, x, r, c] = value
            warm = [heat[i, x, r, c] for i in range(7)]
            for i, value in enumerate(collide_heat(warm, velocity, porosity, inlet)):
                post[i, x, r, c] = value

    for_planes(planes, body)


def input_rows(x, adj, label, msg):
    here = pl.ds(x, 1)
    last = label.shape[1] - 1
    for i in FYPLUS:
        msg[adjoint_slot(i), here, :] = adj[i, x, 0:1, :]
    for i in FYMINUS:
        msg[adjoint_slot(i), here, :] = adj[i, x, last : last + 1, :]
    msg[15, here, :] = jnp.where(label[x, 0:1, :] == 2, 1.0, 0.0)
    msg[16, here, :] = jnp.where(label[x, last : last + 1, :] == 2, 1.0, 0.0)


def heat_rows(x, post, hadj, label, msg):
    here = pl.ds(x, 1)
    far, last = label.shape[0] - 1, label.shape[1] - 1
    msg[0, here, :] = post[3, x, last : last + 1, :]
    msg[1, here, :] = post[4, x, 0:1, :]
    before, after = neighbour(x, -1, far), neighbour(x, 1, far)
    for slot, y in ((0, 0), (1, last)):
        row = slice(y, y + 1)
        total = post[4, x, 1:2, :] if y == 0 else post[3, x, last - 1 : last, :]
        total = total + post[0, x, row, :]
        total = total + shift_z(post[5, x, row, :], 1) + shift_z(post[6, x, row, :], -1)
        if before is not None:
            total = total + post[1, before, row, :]
        if after is not None:
            total = total + post[2, after, row, :]
        msg[2 + slot, here, :] = hadj[3 + slot, x, row, :] + jnp.where(label[x, row, :] == 2, total, 0.0)


def second_interior(source, rows_in, porosity, label, adjoint, heat_adjoint):
    cells = label.shape
    depth, rows, columns = cells
    far = depth - 1

    def kernel(source, rows_ref, porosity, label, adj, hadj, post, heat, aux, msg, moved):
        second_planes(range(1, far), source, rows_ref, None, None, porosity, label, post, heat, aux, moved)
        for_planes(range(0, depth), lambda x: input_rows(x, adj, label, msg))
        for_planes(range(2, far - 1), lambda x: heat_rows(x, post, hadj, label, msg))

    return call(
        kernel,
        "second_interior",
        "vvvvvv",
        [vmem(7, *cells), vmem(7, *cells), vmem(4, *cells), vmem(17, depth, columns)],
        (source, rows_in, porosity, label, adjoint, heat_adjoint),
        scratch=[pltpu.VMEM((19, rows, columns), F32)],
        micros=0.0,
    )


def second_boundary(source, rows_in, face_a, face_b, porosity, label, heat_adjoint, post, heat, aux, msg):
    cells = label.shape
    depth, rows, columns = cells
    far = depth - 1
    last = rows - 1

    def kernel(source, rows_ref, a_ref, b_ref, porosity, label, hadj, post_in, heat_in, aux_in, msg_in,
               post, heat, aux, msg, moved):
        even = lax.rem(lax.axis_index("gx"), 2) == 0

        def low(slot):
            return pick(even, b_ref[slot], a_ref[slot])

        def high(slot):
            return pick(even, a_ref[slot], b_ref[slot])

        second_planes((0, far), source, rows_ref, low, high, porosity, label, post, heat, aux, moved)

        for x in (0, 1, far - 1, far):
            heat_rows(x, post, hadj, label, msg)
        msg[4] = jnp.zeros((depth, columns), F32)
        msg[4, 0:1, :] = post[1, far, 0:1, :]
        msg[4, 1:2, :] = post[1, far, last : last + 1, :]
        msg[4, 2:3, :] = post[2, 0, 0:1, :]
        msg[4, 3:4, :] = post[2, 0, last : last + 1, :]

    return call(
        kernel,
        "second_boundary",
        "vvvvvvvvvvv",
        [vmem(7, *cells), vmem(7, *cells), vmem(4, *cells), vmem(17, depth, columns)],
        (source, rows_in, face_a, face_b, porosity, label, heat_adjoint, post, heat, aux, msg),
        scratch=[pltpu.VMEM((19, rows, columns), F32)],
        aliases={7: 0, 8: 1, 9: 2, 10: 3},
        micros=0.0,
    )


def plane_of(ref, slot):
    return ref[SEEDS + 16 * slot : SEEDS + 16 * (slot + 1)]


def second_faces(post, heat_adjoint, adjoint, label, rows_in, aux, heat, porosity, chosen):
    depth, rows, columns = label.shape
    far = depth - 1

    def kernel(post, hadj, adj, label, rows_ref, aux, heat, porosity, chosen, a_ref, b_ref):
        even = lax.rem(lax.axis_index("gx"), 2) == 0

        def partial(x, other):
            total = post[0, x] + other
            total = total + shift_y(post[3, x], 1, rows_ref[0, x : x + 1, :])
            total = total + shift_y(post[4, x], -1, rows_ref[1, x : x + 1, :])
            return total + shift_z(post[5, x], 1) + shift_z(post[6, x], -1)

        def put(start, high, low):
            where = slice(start, start + high.shape[0])
            a_ref[where] = pick(even, high, low)
            b_ref[where] = pick(even, low, high)

        put(0, post[1, far], post[2, 0])
        high_seed = hadj[2, far] + jnp.where(label[far] == 2, partial(far, post[1, far - 1]), 0.0)
        low_seed = hadj[1, 0] + jnp.where(label[0] == 2, partial(0, post[2, 1]), 0.0)
        put(rows, high_seed, low_seed)
        place = lax.broadcasted_iota(jnp.int32, (8, columns), 0)

        def spread(slot):
            return jnp.broadcast_to(rows_ref[4, slot : slot + 1, :], (8, columns))

        put(2 * rows, jnp.where(place == 0, spread(1), spread(0)), jnp.where(place == 0, spread(3), spread(2)))
        for slot in range(5):
            i, j = FPLUS[slot], FMINUS[slot]
            low, high = adj[i, 0], adj[j, far]
            if VEL[i][1]:
                low = shift_y(low, -VEL[i][1], rows_ref[adjoint_slot(i), 0:1, :])
                high = shift_y(high, -VEL[j][1], rows_ref[adjoint_slot(j), far : far + 1, :])
            put(SEEDS + 16 * slot, high, low)
        put(SEEDS + 80, jnp.where(label[far] == 2, 1.0, 0.0), jnp.where(label[0] == 2, 1.0, 0.0))
        highs = source_weights(aux, heat, porosity, label, chosen, far, 1)
        lows = source_weights(aux, heat, porosity, label, chosen, 0, 2)
        for slot, (high, low) in enumerate(zip(highs[EARLY:], lows[EARLY:])):
            put(SEEDS + 16 * (6 + slot), high, low)

    shape = (SEEDS + 16 * (11 - EARLY), columns)
    return call(
        kernel,
        "second_faces",
        "v" * 9,
        [vmem(*shape)] * 2,
        (post, heat_adjoint, adjoint, label, rows_in, aux, heat, porosity, chosen),
    )


def costate_rows(x, lam, msg):
    here = pl.ds(x, 1)
    last = lam.shape[2] - 1
    for i in YPLUS:
        msg[row_slot(i), here, :] = lam[i, x, 0:1, :]
    for i in YMINUS:
        msg[row_slot(i), here, :] = lam[i, x, last : last + 1, :]


def second_adjoint(planes, name, fixed, arrived, state, micros):
    adj, hadj, post, heat, aux, porosity, label, rows_in = fixed
    cells = label.shape
    depth, rows, columns = cells
    far = depth - 1
    last = rows - 1
    first = state is None
    boundary = isinstance(planes, tuple)
    lit_planes = range(planes[0] - 1, planes[-1] + 2) if first else ((0, far) if boundary else ())

    def kernel(*refs):
        refs = list(refs)
        adj, hadj, post, heat, aux, porosity, label, rows_ref = refs[:8]
        refs = refs[8:]
        if boundary:
            sa, sb = refs[:2]
        refs = refs[len(arrived) :]
        if not first:
            refs = refs[4:]
        lam, sens, lit, msg = refs[:4]
        sides = refs[4] if boundary else None
        moved = refs[-1]
        even = lax.rem(lax.axis_index("gx"), 2) == 0
        tail = 2 * rows

        def from_left(where):
            return pick(even, sb[where], sa[where])

        def from_right(where):
            return pick(even, sa[where], sb[where])

        def light(x):
            here = pl.ds(x, 1)
            before, after = neighbour(x, -1, far), neighbour(x, 1, far)
            total = post[0, x]
            total = total + (from_left(slice(0, rows)) if before is None else post[1, before])
            total = total + (from_right(slice(0, rows)) if after is None else post[2, after])
            total = total + shift_y(post[3, x], 1, rows_ref[0, here, :])
            total = total + shift_y(post[4, x], -1, rows_ref[1, here, :])
            total = total + shift_z(post[5, x], 1) + shift_z(post[6, x], -1)
            lit[x] = jnp.where(label[x] == 2, total, 0.0)

        if lit_planes:
            for_planes(lit_planes, light)

        def body(x):
            here = pl.ds(x, 1)
            before, after = neighbour(x, -1, far), neighbour(x, 1, far)
            glow = lit[x]
            moved[19] = hadj[0, x] + glow
            if after is None:
                moved[20] = from_right(slice(rows, tail)) + pick(even, plane_of(sa, 5), plane_of(sb, 5)) * post[1, far]
            else:
                moved[20] = hadj[1, after] + lit[after]
            if before is None:
                moved[21] = from_left(slice(rows, tail)) + pick(even, plane_of(sb, 5), plane_of(sa, 5)) * post[2, 0]
            else:
                moved[21] = hadj[2, before] + lit[before]
            above = post[3, x, last : last + 1, :]
            below = post[4, x, 0:1, :]
            if before is None:
                above = above + from_left(slice(tail + 1, tail + 2))
                below = below + from_left(slice(tail, tail + 1))
            if after is None:
                above = above + from_right(slice(tail + 1, tail + 2))
                below = below + from_right(slice(tail, tail + 1))
            moved[22] = shift_y(hadj[3, x] + glow, -1, rows_ref[2, here, :] + rows_ref[15, here, :] * above)
            moved[23] = shift_y(hadj[4, x] + glow, 1, rows_ref[3, here, :] + rows_ref[16, here, :] * below)
            moved[24] = shift_z(hadj[5, x] + glow, -1)
            moved[25] = shift_z(hadj[6, x] + glow, 1)
            for i in range(19):
                moved[i] = moved_population(
                    adj,
                    i,
                    x,
                    -1,
                    adjoint_slot,
                    rows_ref,
                    lambda: pick(even, plane_of(sb, FMINUS.index(i)), plane_of(sa, FMINUS.index(i))),
                    lambda: pick(even, plane_of(sa, FPLUS.index(i)), plane_of(sb, FPLUS.index(i))),
                    far,
                )
            for r, c in tiles(rows, columns):
                inlet = label[x, r, c] == 1
                density, ux, uy, uz = (aux[i, x, r, c] for i in range(4))
                warm = [heat[i, x, r, c] for i in range(7)]
                mu = [moved[i, r, c] for i in range(19)]
                nu = [moved[19 + i, r, c] for i in range(7)]
                result, result_heat, part = collide_adjoint(
                    density, (ux, uy, uz), warm, porosity[x, r, c], inlet, mu, nu
                )
                for i, value in enumerate(result + result_heat):
                    lam[i, x, r, c] = value
                sens[x, r, c] = part

        for_planes(planes, body)
        if boundary:
            for slot in range(6):
                sides[slot] = lam[PLUS[slot], 0]
                sides[6 + slot] = lam[MINUS[slot], far]
        for_planes(planes, lambda x: costate_rows(x, lam, msg))

    outs = [vmem(COUNT, *cells), vmem(*cells), vmem(*cells), vmem(12, depth, columns)]
    if boundary:
        outs.append(vmem(12, rows, columns))
    args = fixed + arrived + (() if first else state)
    base = len(args) - 4
    return call(
        kernel,
        name,
        "v" * len(args),
        outs,
        args,
        scratch=[pltpu.VMEM((COUNT, rows, columns), F32)],
        aliases=None if first else {base + n: n for n in range(4)},
        micros=micros,
    )


def arriving(lam, rows_ref, moved, x, far, low, high):
    for i in range(COUNT):
        moved[i] = moved_population(
            lam, i, x, -1, row_slot, rows_ref, lambda: low(MINUS.index(i)), lambda: high(PLUS.index(i)), far
        )


def first_sensitivity(lam, rows_in, fixed, sens_one, weights_a, weights_b, rate_a, rate_b, waves):
    aux, heat, porosity, label, chosen = fixed
    depth, rows, columns = label.shape
    far = depth - 1
    half = columns // 2
    count = depth + 2

    def kernel(lam, rows_ref, aux, heat, porosity, label, chosen, sens_ref, a_ref, b_ref, ra_ref, rb_ref, waves_ref,
               own, other, moved, total):
        even = lax.rem(lax.axis_index("gx"), 2) == 0
        core = lax.axis_index("gy")

        def nothing(slot):
            return jnp.zeros((rows, columns), F32)

        def body(x):
            arriving(lam, rows_ref, moved, x, far, nothing, nothing)
            for r, c in tiles(rows, columns):
                inlet = label[x, r, c] == 1
                density, ux, uy, uz = (aux[i, x, r, c] for i in range(4))
                warm = [heat[i, x, r, c] for i in range(7)]
                mu = [moved[i, r, c] for i in range(19)]
                nu = [moved[19 + i, r, c] for i in range(7)]
                _, _, part = collide_adjoint(density, (ux, uy, uz), warm, porosity[x, r, c], inlet, mu, nu)
                total[x, r, c] = jnp.where(chosen[x, r, c] > 0.0, part + sens_ref[x, r, c], 0.0)

        for_planes((0, far), body)
        for_planes(range(1, far), body)
        def weights(slot, reverse):
            if slot < EARLY:
                of_a, of_b = ra_ref[6 + slot], rb_ref[6 + slot]
            else:
                of_a, of_b = plane_of(a_ref, 6 + slot - EARLY), plane_of(b_ref, 6 + slot - EARLY)
            return pick(even, of_b, of_a) if reverse else pick(even, of_a, of_b)

        for place, x, members, reverse in ((depth, 0, PLUS, True), (depth + 1, far, MINUS, False)):
            rate, scale, *vector = (weights(slot, reverse) for slot in range(5))
            speed = vector[0] * vector[0] + vector[1] * vector[1] + vector[2] * vector[2]
            result = jnp.zeros((rows, columns), F32)
            for i in members:
                value = lam[i, x]
                if VEL[i][1]:
                    value = shift_y(value, -VEL[i][1], rows_ref[row_slot(i), x : x + 1, :])
                value = shift_z(value, -VEL[i][2])
                if i < 19:
                    part = along(VEL[i], vector)
                    result = result + (fluid_wts[i] * scale) * (part - speed + 3.0 * part * part) * value
                else:
                    result = result + rate * value
            total[place] = result
        flat = total[...].reshape(count * rows, columns)
        own[...] = multiply(flat, waves_ref[core]).reshape(count, rows, half)
        other[...] = multiply(flat, waves_ref[1 - core]).reshape(count, rows, half)

    args = (lam, rows_in) + fixed + (sens_one, weights_a, weights_b, rate_a, rate_b, waves)
    return call(
        kernel,
        "first_sensitivity",
        "v" * len(args),
        [vmem(count, rows, half)] * 2,
        args,
        scratch=[pltpu.VMEM((COUNT, rows, columns), F32), pltpu.VMEM((count, rows, columns), F32)],
    )


def first_adjoint(groups, name, lam, rows_in, fixed, arrived, early_planes, early):
    aux, heat, porosity, label = fixed
    cells = label.shape
    depth, rows, columns = cells
    far = depth - 1
    planes = [x for group in groups for x in group]
    count = len(planes)
    last = early is not None

    def kernel(*refs):
        refs = list(refs)
        lam, rows_ref, aux, heat, porosity, label = refs[:6]
        refs = refs[6:]
        if last:
            b_ref, a_ref, early_ref, fluid_out, heat_out, token, moved, out, sem = refs
            token[...] = jnp.zeros((8, 128), F32)
        else:
            out, moved = refs
        even = lax.rem(lax.axis_index("gx"), 2) == 0

        def place(x):
            return planes.index(x) if isinstance(x, int) else x - groups[-1][0] + count - len(groups[-1])

        def writes(source, n, x, slot):
            return (
                pltpu.make_async_copy(source.at[0:19, n], fluid_out.at[:, x], sem.at[2 * slot]),
                pltpu.make_async_copy(source.at[19:26, n], heat_out.at[:, x], sem.at[2 * slot + 1]),
            )

        def low(slot):
            return pick(even, b_ref[slot], a_ref[slot])

        def high(slot):
            return pick(even, a_ref[slot], b_ref[slot])

        def body(x):
            n = place(x)
            arriving(lam, rows_ref, moved, x, far, low, high)
            for r, c in tiles(rows, columns):
                inlet = label[x, r, c] == 1
                density, ux, uy, uz = (aux[i, x, r, c] for i in range(4))
                warm = [heat[i, x, r, c] for i in range(7)]
                mu = [moved[i, r, c] for i in range(19)]
                nu = [moved[19 + i, r, c] for i in range(7)]
                result, result_heat, _ = collide_adjoint(density, (ux, uy, uz), warm, porosity[x, r, c], inlet, mu, nu)
                for i, value in enumerate(result + result_heat):
                    out[i, n, r, c] = value
            if last:
                for copy in writes(out, n, x, n):
                    copy.start()

        early_copies = []
        if last:
            for n, x in enumerate(early_planes):
                early_copies += writes(early_ref, n, x, count + n)
        for copy in early_copies:
            copy.start()
        for group in groups:
            for_planes(group, body)
        if last:

            def finish(x):
                for copy in writes(out, place(x), x, place(x)):
                    copy.wait()

            for group in groups:
                for_planes(group, finish)
        for copy in early_copies:
            copy.wait()

    buffer = (COUNT, count, rows, columns)
    moved = pltpu.VMEM((COUNT, rows, columns), F32)
    args = (lam, rows_in) + fixed + arrived + ((early,) if last else ())
    if last:
        outs = [hbm(19, *cells), hbm(7, *cells), vmem(8, 128)]
        scratch = [moved, pltpu.VMEM(buffer, F32), pltpu.SemaphoreType.DMA((2 * (count + len(early_planes)),))]
    else:
        outs = [vmem(*buffer)]
        scratch = [moved]
    return call(kernel, name, "v" * len(args), outs, args, scratch=scratch)


def halves(value):
    high = value.astype(jnp.bfloat16)
    return high, (value - high.astype(F32)).astype(jnp.bfloat16)


def multiply(first, second):
    a, b = halves(first)
    c, d = halves(second)
    small = jnp.dot(a, d, preferred_element_type=F32) + jnp.dot(b, c, preferred_element_type=F32)
    return jnp.dot(a, c, preferred_element_type=F32) + small


def hartley(length):
    index = np.arange(length)
    angle = 2.0 * np.pi * ((index[:, None] * index[None, :]) % length) / length
    return (np.cos(angle) + np.sin(angle)) / np.sqrt(length)


def filter_tables(depth, count_y, count_z):
    half = count_z // 2
    wave_z = hartley(count_z)
    waves = np.stack([wave_z[:, :half], wave_z[:, half:]]).astype(np.float32)
    waves_back = np.stack([wave_z[:half], wave_z[half:]]).astype(np.float32)
    wave_y = np.kron(np.eye(depth), hartley(count_y)).astype(np.float32)
    wave_ends = np.kron(np.eye(2), hartley(count_y)).astype(np.float32)
    symbol_y = 2.0 - 2.0 * np.cos(2.0 * np.pi * np.arange(count_y) / count_y)
    symbol_z = 2.0 - 2.0 * np.cos(2.0 * np.pi * np.arange(count_z) / count_z)
    weight = float(RADIUS * RADIUS)
    centre = (1.0 + weight * (2.0 + symbol_y[:, None] + symbol_z[None, :])) / weight
    ratio = 2.0 / (centre + np.sqrt(centre * centre - 4.0))
    peak = 1.0 / (weight * (1.0 / ratio - ratio))
    fields = np.stack([ratio, np.log(ratio) * depth, peak]).astype(np.float32)
    fields = np.stack([fields[:, :, :half], fields[:, :, half:]])
    return waves, waves_back, wave_y, wave_ends, fields


def to_modes(own, other, wave_y, wave_ends, fields):
    count, rows, half = own.shape
    depth = count - 2
    full = 2 * rows
    inside = depth * full

    def kernel(own_ref, other_ref, wave_ref, small_ref, field_ref, modes, ends, both):
        core = lax.axis_index("gy")
        for x in range(count):
            both[x * full : x * full + rows] = own_ref[x]
            both[x * full + rows : (x + 1) * full] = other_ref[x]
        modes[0:inside] = multiply(wave_ref[...], both[0:inside])
        modes[inside : inside + 2 * full] = multiply(small_ref[...], both[inside : inside + 2 * full])
        ratio = field_ref[core, 0]
        before, after = modes[inside : inside + full], modes[inside + full : inside + 2 * full]
        head = before
        for x in range(depth):
            head = head * ratio + modes[x * full : (x + 1) * full]
        ends[0] = head * ratio + after
        tail = after
        for x in range(depth - 1, -1, -1):
            tail = tail * ratio + modes[x * full : (x + 1) * full]
        ends[1] = tail * ratio + before

    return call(
        kernel,
        "to_modes",
        "vvvvv",
        [vmem(count * full, half), vmem(2, full, half)],
        (own, other, wave_y, wave_ends, fields),
        scratch=[pltpu.VMEM((count * full, half), F32)],
    )


def join_segments(ends, arrived, carry, fields, reach, after):
    first = carry is None

    def kernel(*refs):
        ends_ref, in_ref, field_ref = refs[:3]
        carry_ref = None if first else refs[3]
        ends_out, carry_out = refs[-2:]
        core = lax.axis_index("gy")
        index = lax.axis_index("gx")
        place = lax.rem(index, reach)
        upper = lax.rem(lax.div(index, reach), 2) == 1
        rate = field_ref[core, 1]
        whole = jnp.exp(rate * float(reach))
        forward = jnp.exp(rate * place.astype(F32))
        backward = jnp.exp(rate * (reach - 1 - place).astype(F32))
        head, tail = ends_ref[0], ends_ref[1]
        head_in, tail_in = in_ref[0], in_ref[1]
        left = pick(upper, forward * head_in, jnp.zeros_like(head))
        right = pick(upper, jnp.zeros_like(head), backward * tail_in)
        carry_out[0] = left if first else carry_ref[0] + left
        carry_out[1] = right if first else carry_ref[1] + right
        ends_out[0] = pick(upper, head + whole * head_in, head_in + whole * head)
        ends_out[1] = pick(upper, tail_in + whole * tail, tail + whole * tail_in)

    args = (ends, arrived, fields) + (() if first else (carry,)) + after
    return call(kernel, "join_segments", "v" * len(args), [vmem(*ends.shape)] * 2, args, micros=0.0)


def from_modes(modes, ends, carry, wave_y, fields, depth, parts, after):
    half = modes.shape[1]
    full = modes.shape[0] // (depth + 2)
    rows = full // 2
    inside = depth * full

    def kernel(modes_ref, ends_ref, carry_ref, wave_ref, field_ref, after_ref, own, other, solved):
        core = lax.axis_index("gy")
        index = lax.axis_index("gx")
        ratio, rate, peak = field_ref[core, 0], field_ref[core, 1], field_ref[core, 2]
        around = 1.0 / (1.0 - jnp.exp(rate * float(parts)))
        left = carry_ref[0] + jnp.exp(rate * index.astype(F32)) * around * ends_ref[0]
        right = carry_ref[1] + jnp.exp(rate * (parts - 1 - index).astype(F32)) * around * ends_ref[1]
        run = left + ratio * modes_ref[inside : inside + full]
        for x in range(depth):
            run = run + modes_ref[x * full : (x + 1) * full]
            solved[x * full : (x + 1) * full] = run
            run = run * ratio
        run = right + ratio * modes_ref[inside + full : inside + 2 * full]
        for x in range(depth - 1, -1, -1):
            solved[x * full : (x + 1) * full] = peak * (solved[x * full : (x + 1) * full] + run)
            run = ratio * (run + modes_ref[x * full : (x + 1) * full])
        back = multiply(wave_ref[...], solved[...])
        for x in range(depth):
            own[x * rows : (x + 1) * rows] = back[x * full : x * full + rows]
            other[x * rows : (x + 1) * rows] = back[x * full + rows : (x + 1) * full]

    flat = (depth * rows, half)
    return call(
        kernel,
        "from_modes",
        "vvvvvv",
        [vmem(*flat)] * 2,
        (modes, ends, carry, wave_y, fields, after),
        scratch=[pltpu.VMEM((inside, half), F32)],
    )


def last_transform(own, other, waves_back, depth):
    flat, half = own.shape
    rows = flat // depth

    def kernel(own_ref, other_ref, wave_ref, out_ref, out, sem):
        core = lax.axis_index("gy")
        result = multiply(own_ref[...], wave_ref[core]) + multiply(other_ref[...], wave_ref[1 - core])
        out[...] = result.reshape(depth, rows, 2 * half)
        copy = pltpu.make_async_copy(out, out_ref, sem.at[0])
        copy.start()
        copy.wait()

    shape = (depth, rows, 2 * half)
    return call(
        kernel,
        "last_transform",
        "vvv",
        [hbm(*shape)],
        (own, other, waves_back),
        scratch=[pltpu.VMEM(shape, F32), pltpu.SemaphoreType.DMA((1,))],
    )


def per_device(fluid_state, heat_state, design, cell_type, boundary, fluid_adjoint, heat_adjoint):
    depth, rows, columns = design.shape
    far = depth - 1
    parts = lax.axis_size("gx")
    waves, waves_back, wave_y, wave_ends, fields = filter_tables(depth, 2 * rows, columns)

    pairs_a = [(i, i ^ 1) for i in range(parts)]
    pairs_b = [(i, (i + 1) % parts if i % 2 else (i - 1) % parts) for i in range(parts)]

    def across(value):
        return lax.ppermute(value, "gy", [(0, 1), (1, 0)])

    def sideways(first, second):
        first = lax.ppermute(first, "gx", pairs_a)
        second = lax.ppermute(second, "gx", pairs_b)
        return first, second

    adj, hadj = fluid_adjoint, heat_adjoint
    post, heat_edge, aux_edge, porosity, label, chosen, sides, corner = first_boundary(
        *(in_hbm(value) for value in (fluid_state, heat_state, design, cell_type, boundary))
    )
    face_a, face_b, token = first_faces(sides, across(corner), label, aux_edge, heat_edge, porosity, chosen)
    face_a, face_b = sideways(face_a, face_b)
    rate_a, rate_b = face_a, face_b
    heat_zero = heat_state
    post, aux_zero, rows_one = first_interior(
        fluid_state, heat_zero, post, aux_edge, porosity, label, token
    )
    rows_one = across(rows_one)
    post_one, heat_one, aux_one, rows_heat = second_interior(post, rows_one, porosity, label, adj, hadj)
    post_one, heat_one, aux_one, rows_heat = second_boundary(
        post, rows_one, face_a, face_b, porosity, label, hadj, post_one, heat_one, aux_one, rows_heat
    )
    rows_heat = across(rows_heat)
    seed_a, seed_b = second_faces(post_one, hadj, adj, label, rows_heat, aux_zero, heat_zero, porosity, chosen)
    seed_a, seed_b = sideways(seed_a, seed_b)
    fixed = (adj, hadj, post_one, heat_one, aux_one, porosity, label, rows_heat)
    state = second_adjoint(range(2, far - 1), "adjoint_inner", fixed, (), None, 0.0)
    lam, sens_one, lit, rows_two, sides = second_adjoint(
        (0, 1, far - 1, far), "adjoint_outer", fixed, (seed_a, seed_b), tuple(state), 0.0
    )
    rows_two = across(rows_two)
    face_a, face_b = costate_faces(sides, rows_two)
    face_a, face_b = sideways(face_a, face_b)
    fixed = (aux_zero, heat_zero, porosity, label)
    own, other = first_sensitivity(lam, rows_two, fixed + (chosen,), sens_one, seed_a, seed_b, rate_a, rate_b, waves)
    early = first_adjoint(((1,),), "costate_early", lam, rows_two, fixed, (), None, None)
    fluid_costate, heat_costate, token = first_adjoint(
        ((0, far), range(2, far)), "costate_rest", lam, rows_two, fixed, (face_b, face_a), (1,), early
    )
    other = across(other)
    modes, ends = to_modes(own, other, wave_y, wave_ends, fields)
    carry = None
    reach = 1
    while reach < parts:
        arrived = lax.ppermute(ends, "gx", [(i, i ^ reach) for i in range(parts)])
        ends, carry = join_segments(ends, arrived, carry, fields, reach, (early,) if reach == 1 else ())
        reach = 2 * reach
    own, other = from_modes(modes, ends, carry, wave_y, fields, depth, parts, token)
    other = across(other)
    return (fluid_costate, heat_costate, last_transform(own, other, waves_back, depth))


def solution(mesh):
    return jax.shard_map(
        per_device,
        mesh=mesh,
        in_specs=(
            P(None, ("case", "gx"), "gy", None),
            P(None, ("case", "gx"), "gy", None),
            P(("case", "gx"), "gy", None),
            P(("case", "gx"), "gy", None),
            P(("case", "gx"), "gy", None),
            P(None, ("case", "gx"), "gy", None),
            P(None, ("case", "gx"), "gy", None),
        ),
        out_specs=(
            P(None, ("case", "gx"), "gy", None),
            P(None, ("case", "gx"), "gy", None),
            P(("case", "gx"), "gy", None),
        ),
        check_vma=False,
    )
```

```python
import numpy as np
import jax
import jax.numpy as jnp
from jax import lax
from jax.experimental import pallas as pl
from jax.experimental.pallas import tpu as pltpu
from jax.sharding import PartitionSpec as P

RADIUS = 4

fluid_vel = [
    (0, 0, 0),
    (1, 0, 0),
    (-1, 0, 0),
    (0, 1, 0),
    (0, -1, 0),
    (0, 0, 1),
    (0, 0, -1),
    (1, 1, 0),
    (-1, -1, 0),
    (1, -1, 0),
    (-1, 1, 0),
    (1, 0, 1),
    (-1, 0, -1),
    (1, 0, -1),
    (-1, 0, 1),
    (0, 1, 1),
    (0, -1, -1),
    (0, 1, -1),
    (0, -1, 1),
]
fluid_wts = [1.0 / 3.0] + [1.0 / 18.0] * 6 + [1.0 / 36.0] * 12
inlet_speed = 0.05
inlet_eq = [
    weight
    * (
        1.0
        + 3.0 * inlet_speed * entry[2]
        + 4.5 * (inlet_speed * entry[2]) ** 2
        - 1.5 * inlet_speed**2
    )
    for entry, weight in zip(fluid_vel, fluid_wts)
]

VEL = fluid_vel + fluid_vel[:7]
COUNT = len(VEL)
PLUS = [i for i in range(COUNT) if VEL[i][0] == 1]
MINUS = [i for i in range(COUNT) if VEL[i][0] == -1]
YPLUS = [i for i in range(COUNT) if VEL[i][1] == 1]
YMINUS = [i for i in range(COUNT) if VEL[i][1] == -1]
FPLUS = [i for i in PLUS if i < 19]
FMINUS = [i for i in MINUS if i < 19]
FYPLUS = [i for i in YPLUS if i < 19]
FYMINUS = [i for i in YMINUS if i < 19]

VMEM_BYTES = 24 * 1024 * 1024
EARLY = 2
SEEDS = 40
F32 = jnp.float32


def params():
    return pltpu.CompilerParams(vmem_limit_bytes=VMEM_BYTES)


def cost(micros):
    return pl.CostEstimate(flops=int(micros * 1e9), bytes_accessed=0, transcendentals=0)


def shift_y(value, step, ghost):
    if step == 0:
        return value
    rows = value.shape[0]
    moved = pltpu.roll(value, step % rows, 0)
    place = lax.broadcasted_iota(jnp.int32, value.shape, 0)
    edge = 0 if step > 0 else rows - 1
    return jnp.where(place == edge, jnp.broadcast_to(ghost, value.shape), moved)


def shift_z(value, step):
    if step == 0:
        return value
    return pltpu.roll(value, step % value.shape[1], 1)


def pick(flag, first, second):
    return jnp.where(flag, first, second)


def tiles(rows, columns):
    return [
        (slice(r, r + 8), slice(c, c + 128)) for r in range(0, rows, 8) for c in range(0, columns, 128)
    ]


def porosity_of(design, kind):
    return jnp.where(kind == 2, design, jnp.where(kind == 1, 0.0, 1.0))


def heat_rate_of(porosity):
    return 1.0 / (0.55 + 0.9 * (1.0 - porosity))


def moments(pops, porosity):
    density = pops[0]
    for value in pops[1:]:
        density = density + value
    diff = {i: pops[i] - pops[i + 1] for i in range(1, 19, 2)}
    flux_x = diff[1] + diff[7] + diff[9] + diff[11] + diff[13]
    flux_y = diff[3] + diff[7] - diff[9] + diff[15] + diff[17]
    flux_z = diff[5] + diff[11] - diff[13] + diff[15] - diff[17]
    inverse = (0.1 + porosity) / (density * (0.5 + 0.6 * porosity))
    return density, (flux_x * inverse, flux_y * inverse, flux_z * inverse)


def along(entry, vector):
    total = None
    for part, value in zip(entry, vector):
        if part == 0:
            continue
        if total is None:
            total = value if part == 1 else -value
        else:
            total = total + value if part == 1 else total - value
    return total


def collide_fluid(pops, density, velocity, inlet):
    speed = velocity[0] * velocity[0] + velocity[1] * velocity[1] + velocity[2] * velocity[2]
    scaled = 1.25 * density
    base = scaled - 1.5 * scaled * speed
    result = [jnp.where(inlet, inlet_eq[0], base * (1.0 / 3.0) - 0.25 * pops[0])]
    for i in range(1, 19, 2):
        weight = fluid_wts[i]
        part = along(VEL[i], velocity)
        flow = scaled * part
        even = weight * base + (4.5 * weight) * (flow * part)
        odd = (3.0 * weight) * flow
        result.append(jnp.where(inlet, inlet_eq[i], even + odd - 0.25 * pops[i]))
        result.append(jnp.where(inlet, inlet_eq[i + 1], even - odd - 0.25 * pops[i + 1]))
    return result


def collide_heat(pops, velocity, porosity, inlet):
    temper = pops[0]
    for value in pops[1:]:
        temper = temper + value
    rate = heat_rate_of(porosity)
    keep = 1.0 - rate
    warm = rate * temper
    base = warm + (1.0 - porosity)
    result = [jnp.where(inlet, 0.0, keep * pops[0] + 0.25 * base)]
    for axis in range(3):
        i = 1 + 2 * axis
        odd = 0.5 * (warm * velocity[axis])
        even = 0.125 * base
        result.append(jnp.where(inlet, 0.0, keep * pops[i] + (even + odd)))
        result.append(jnp.where(inlet, 0.0, keep * pops[i + 1] + (even - odd)))
    return result


def collide_adjoint(density, velocity, heat, porosity, inlet, mu, nu):
    ux, uy, uz = velocity
    mu = [jnp.where(inlet, 0.0, value) for value in mu]
    nu = [jnp.where(inlet, 0.0, value) for value in nu]
    even = {i: mu[i] + mu[i + 1] for i in range(1, 19, 2)}
    odd = {i: mu[i] - mu[i + 1] for i in range(1, 19, 2)}
    wa, wb = 1.0 / 18.0, 1.0 / 36.0
    xy_sum, xz_sum, yz_sum = even[7] + even[9], even[11] + even[13], even[15] + even[17]
    m0 = mu[0] * (1.0 / 3.0) + wa * (even[1] + even[3] + even[5]) + wb * (xy_sum + xz_sum + yz_sum)
    m1x = wa * odd[1] + wb * (odd[7] + odd[9] + odd[11] + odd[13])
    m1y = wa * odd[3] + wb * (odd[7] - odd[9] + odd[15] + odd[17])
    m1z = wa * odd[5] + wb * (odd[11] - odd[13] + odd[15] - odd[17])
    mxx = wa * even[1] + wb * (xy_sum + xz_sum)
    myy = wa * even[3] + wb * (xy_sum + yz_sum)
    mzz = wa * even[5] + wb * (xz_sum + yz_sum)
    mxy = wb * (even[7] - even[9])
    mxz = wb * (even[11] - even[13])
    myz = wb * (even[15] - even[17])
    vx = mxx * ux + mxy * uy + mxz * uz
    vy = mxy * ux + myy * uy + myz * uz
    vz = mxz * ux + myz * uy + mzz * uz
    speed = ux * ux + uy * uy + uz * uz
    slope = (
        m0 * (1.0 - 1.5 * speed)
        + 3.0 * (ux * m1x + uy * m1y + uz * m1z)
        + 4.5 * (ux * vx + uy * vy + uz * vz)
    )
    rate = heat_rate_of(porosity)
    keep = 1.0 - rate
    temper = heat[0]
    for value in heat[1:]:
        temper = temper + value
    n0 = 0.25 * nu[0] + 0.125 * (nu[1] + nu[2] + nu[3] + nu[4] + nu[5] + nu[6])
    n1x, n1y, n1z = (0.125 * (nu[i] - nu[i + 1]) for i in (1, 3, 5))
    warm = 4.0 * rate * temper
    scaled = 3.75 * density
    bar_x = scaled * (m1x - m0 * ux + 3.0 * vx) + warm * n1x
    bar_y = scaled * (m1y - m0 * uy + 3.0 * vy) + warm * n1y
    bar_z = scaled * (m1z - m0 * uz + 3.0 * vz) + warm * n1z
    work = bar_x * ux + bar_y * uy + bar_z * uz
    ramp = 0.1 + porosity
    drag = 0.5 + 0.6 * porosity
    over = 1.0 / (density * drag)
    inverse = ramp * over
    b = (bar_x * inverse, bar_y * inverse, bar_z * inverse)
    a = 1.25 * slope - work * (drag * over)
    lam = [a - 0.25 * mu[0]]
    for i in range(1, 19, 2):
        part = along(VEL[i], b)
        lam.append((a + part) - 0.25 * mu[i])
        lam.append((a - part) - 0.25 * mu[i + 1])
    pull = n0 + 4.0 * (ux * n1x + uy * n1y + uz * n1z)
    a_heat = rate * pull
    lam_heat = [keep * value + a_heat for value in nu]
    dot = nu[0] * heat[0]
    for first, second in zip(nu[1:], heat[1:]):
        dot = dot + first * second
    sens = work * (0.44 / (ramp * drag)) - n0 + (0.9 * rate * rate) * (temper * pull - dot)
    return lam, lam_heat, sens


IN_VMEM = pl.BlockSpec(memory_space=pltpu.VMEM)
IN_HBM = pl.BlockSpec(memory_space=pltpu.HBM)


def vmem(*shape):
    return pltpu.VMEM(shape, F32)


def hbm(*shape):
    return pltpu.HBM(shape, F32)


def in_hbm(value):
    return pltpu.with_memory_space_constraint(value, pltpu.HBM)


def call(kernel, name, specs, outs, args, scratch=(), aliases=None, micros=0.0):
    spec_of = {"v": IN_VMEM, "h": IN_HBM}
    single = len(outs) == 1
    args = [
        pltpu.with_memory_space_constraint(value, pltpu.VMEM) if letter == "v" else value
        for letter, value in zip(specs, args)
    ]
    out_specs = [IN_HBM if out.memory_space == pltpu.HBM else IN_VMEM for out in outs]
    return pl.pallas_call(
        kernel,
        in_specs=[spec_of[letter] for letter in specs],
        out_specs=out_specs[0] if single else out_specs,
        out_shape=outs[0] if single else outs,
        scratch_shapes=list(scratch),
        input_output_aliases=aliases or {},
        compiler_params=params(),
        cost_estimate=cost(micros),
        name=name,
    )(*args)


def row_slot(i):
    return YPLUS.index(i) if VEL[i][1] > 0 else 6 + YMINUS.index(i)


def adjoint_slot(i):
    return 5 + FYPLUS.index(i) if VEL[i][1] > 0 else 10 + FYMINUS.index(i)


def for_planes(planes, body):
    if isinstance(planes, tuple):
        for x in planes:
            body(x)
    else:

        def step(x, carry):
            body(x)
            return carry

        lax.fori_loop(planes[0], planes[-1] + 1, step, 0)


def neighbour(x, step, far):
    plane = x + step
    if isinstance(x, int) and (plane < 0 or plane > far):
        return None
    return plane


def moved_population(source, i, x, direction, slot_of, rows_ref, low, high, far):
    step = tuple(direction * part for part in VEL[i])
    plane = neighbour(x, -step[0], far)
    if plane is None:
        value = low() if step[0] == 1 else high()
    else:
        value = source[i, plane]
        if step[1]:
            value = shift_y(value, step[1], rows_ref[slot_of(i), pl.ds(plane, 1), :])
    return shift_z(value, step[2])


def corner_rows(direction):
    return ((7, -1), (9, -1), (8, 0), (10, 0)) if direction == 1 else ((7, 0), (9, 0), (8, -1), (10, -1))


def collide_plane(x, fluid, heat, post, aux, porosity, label):
    _, _, rows, columns = post.shape
    for r, c in tiles(rows, columns):
        phi = porosity[x, r, c]
        inlet = label[x, r, c] == 1
        pops = [fluid[i, x, r, c] for i in range(19)]
        density, velocity = moments(pops, phi)
        for i, value in enumerate((density,) + velocity):
            aux[i, x, r, c] = value
        warm = [heat[i, x, r, c] for i in range(7)]
        result = collide_fluid(pops, density, velocity, inlet) + collide_heat(warm, velocity, phi, inlet)
        for i, value in enumerate(result):
            post[i, x, r, c] = value


def first_boundary(fluid, heat, design, kind, label):
    cells = design.shape
    depth, rows, columns = cells
    far = depth - 1
    last = rows - 1

    def kernel(fluid_in, heat_in, design_in, kind_in, label_in, post, heat, aux, porosity, label, chosen,
               sides, corner, design, kind, sem):
        fields = (
            pltpu.make_async_copy(design_in, design, sem.at[0]),
            pltpu.make_async_copy(kind_in, kind, sem.at[1]),
            pltpu.make_async_copy(label_in, label, sem.at[2]),
        )
        loads = []
        for n, x in enumerate((0, far)):
            loads.append(pltpu.make_async_copy(fluid_in.at[:, x], post.at[0:19, x], sem.at[3 + 2 * n]))
            loads.append(pltpu.make_async_copy(heat_in.at[:, x], heat.at[:, x], sem.at[4 + 2 * n]))
        for copy in fields + tuple(loads):
            copy.start()
        for copy in fields:
            copy.wait()
        for x in (0, far):
            porosity[x] = porosity_of(design[x], kind[x])
            chosen[x] = jnp.where(kind[x] == 2, 1.0, 0.0)
        for copy in loads:
            copy.wait()
        collide_plane(0, post, heat, post, aux, porosity, label)
        collide_plane(far, post, heat, post, aux, porosity, label)
        for slot in range(6):
            sides[slot] = post[PLUS[slot], far]
            sides[6 + slot] = post[MINUS[slot], 0]
        corner[...] = jnp.zeros((8, columns), F32)
        for slot, (i, x) in enumerate(corner_rows(1)):
            y = last if VEL[i][1] > 0 else 0
            corner[slot : slot + 1, :] = post[i, x % depth, y : y + 1, :]

    return call(
        kernel,
        "first_boundary",
        "hhhhh",
        [
            vmem(COUNT, *cells),
            vmem(7, *cells),
            vmem(4, *cells),
            vmem(*cells),
            pltpu.VMEM(cells, jnp.int32),
            vmem(*cells),
            vmem(12, rows, columns),
            vmem(8, columns),
            vmem(*cells),
            pltpu.VMEM(cells, jnp.int32),
        ],
        (fluid, heat, design, kind, label),
        scratch=[pltpu.SemaphoreType.DMA((7,))],
    )


def first_interior(fluid, heat, post, aux, porosity, chosen, design, kind, label, after):
    cells = label.shape
    depth, rows, columns = cells
    far = depth - 1
    last = rows - 1

    def kernel(fluid, heat, post_in, aux_in, porosity_in, chosen_in, design, kind, label, after_ref,
               post, aux, porosity, chosen, msg):
        def body(x):
            porosity[x] = porosity_of(design[x], kind[x])
            chosen[x] = jnp.where(kind[x] == 2, 1.0, 0.0)
            collide_plane(x, fluid, heat, post, aux, porosity, label)

        for_planes(range(1, far), body)

        def rows_of(x, carry):
            here = pl.ds(x, 1)
            for i in YPLUS:
                msg[row_slot(i), here, :] = post[i, x, last : last + 1, :]
            for i in YMINUS:
                msg[row_slot(i), here, :] = post[i, x, 0:1, :]
            return carry

        lax.fori_loop(0, depth, rows_of, 0)

    return call(
        kernel,
        "first_interior",
        "vvvvvvvvvv",
        [vmem(COUNT, *cells), vmem(4, *cells), vmem(*cells), vmem(*cells), vmem(12, depth, columns)],
        (fluid, heat, post, aux, porosity, chosen, design, kind, label, after),
        aliases={2: 0, 3: 1, 4: 2, 5: 3},
        micros=1.0,
    )


def source_weights(aux, heat, porosity, label, chosen, x, k):
    density, ux, uy, uz = (aux[i, x] for i in range(4))
    phi = porosity[x]
    valid = jnp.logical_and(label[x] != 1, chosen[x] > 0.0)
    over = 0.44 / ((0.1 + phi) * (0.5 + 0.6 * phi))
    rate = heat_rate_of(phi)
    temper = heat[0, x]
    for i in range(1, 7):
        temper = temper + heat[i, x]
    part = along(VEL[k], (ux, uy, uz))
    weight = over * (0.5 * rate * temper) * part - 0.125
    weight = weight + (0.9 * rate * rate) * (temper * (0.125 + 0.5 * part) - heat[k, x])
    scale = jnp.where(valid, 3.75 * over * density, 0.0)
    return jnp.where(valid, weight, 0.0), scale, ux, uy, uz


def crossing_sides(sides_ref, row_of, direction, slot):
    i, j = PLUS[slot], MINUS[slot]
    plus, minus = sides_ref[slot], sides_ref[6 + slot]
    if VEL[i][1]:
        plus = shift_y(plus, direction * VEL[i][1], row_of(i))
        minus = shift_y(minus, direction * VEL[j][1], row_of(j))
    return (plus, minus) if direction == 1 else (minus, plus)


def first_faces(sides, rows_in, label, aux, heat, porosity, chosen):
    _, rows, columns = sides.shape
    far = label.shape[0] - 1

    def kernel(sides_ref, rows_ref, label, aux, heat, porosity, chosen, a_ref, b_ref, token):
        token[...] = jnp.zeros((8, 128), F32)
        even = lax.rem(lax.axis_index("gx"), 2) == 0

        def row_of(i):
            slot = [entry[0] for entry in corner_rows(1)].index(i)
            return rows_ref[slot : slot + 1, :]

        for slot in range(6):
            high, low = crossing_sides(sides_ref, row_of, 1, slot)
            a_ref[slot] = pick(even, high, low)
            b_ref[slot] = pick(even, low, high)
        highs = source_weights(aux, heat, porosity, label, chosen, far, 1)
        lows = source_weights(aux, heat, porosity, label, chosen, 0, 2)
        for slot in range(EARLY):
            a_ref[6 + slot] = pick(even, highs[slot], lows[slot])
            b_ref[6 + slot] = pick(even, lows[slot], highs[slot])

    return call(
        kernel,
        "first_faces",
        "v" * 7,
        [vmem(6 + EARLY, rows, columns)] * 2 + [vmem(8, 128)],
        (sides, rows_in, label, aux, heat, porosity, chosen),
    )


def costate_faces(sides, rows_in):
    _, rows, columns = sides.shape

    def kernel(sides_ref, rows_ref, a_ref, b_ref):
        even = lax.rem(lax.axis_index("gx"), 2) == 0
        far = rows_ref.shape[1] - 1

        def row_of(i):
            x = 0 if VEL[i][0] > 0 else far
            return rows_ref[row_slot(i), x : x + 1, :]

        for slot in range(6):
            high, low = crossing_sides(sides_ref, row_of, -1, slot)
            a_ref[slot] = pick(even, high, low)
            b_ref[slot] = pick(even, low, high)

    return call(kernel, "costate_faces", "vv", [vmem(6, rows, columns)] * 2, (sides, rows_in))


def second_planes(planes, source, rows_ref, low, high, porosity_ref, label_ref, post, heat, aux, moved):
    _, depth, rows, columns = source.shape
    far = depth - 1

    def body(x):
        for i in range(COUNT):
            value = moved_population(
                source, i, x, 1, row_slot, rows_ref, lambda: low(PLUS.index(i)), lambda: high(MINUS.index(i)), far
            )
            if i < 19:
                moved[i] = value
            else:
                heat[i - 19, x] = value
        for r, c in tiles(rows, columns):
            porosity = porosity_ref[x, r, c]
            inlet = label_ref[x, r, c] == 1
            pops = [moved[i, r, c] for i in range(19)]
            density, velocity = moments(pops, porosity)
            for i, value in enumerate((density,) + velocity):
                aux[i, x, r, c] = value
            warm = [heat[i, x, r, c] for i in range(7)]
            for i, value in enumerate(collide_heat(warm, velocity, porosity, inlet)):
                post[i, x, r, c] = value

    for_planes(planes, body)


def input_rows(x, adj, label, msg):
    here = pl.ds(x, 1)
    last = label.shape[1] - 1
    for i in FYPLUS:
        msg[adjoint_slot(i), here, :] = adj[i, x, 0:1, :]
    for i in FYMINUS:
        msg[adjoint_slot(i), here, :] = adj[i, x, last : last + 1, :]
    msg[15, here, :] = jnp.where(label[x, 0:1, :] == 2, 1.0, 0.0)
    msg[16, here, :] = jnp.where(label[x, last : last + 1, :] == 2, 1.0, 0.0)


def heat_rows(x, post, hadj, label, msg):
    here = pl.ds(x, 1)
    far, last = label.shape[0] - 1, label.shape[1] - 1
    msg[0, here, :] = post[3, x, last : last + 1, :]
    msg[1, here, :] = post[4, x, 0:1, :]
    before, after = neighbour(x, -1, far), neighbour(x, 1, far)
    for slot, y in ((0, 0), (1, last)):
        row = slice(y, y + 1)
        total = post[4, x, 1:2, :] if y == 0 else post[3, x, last - 1 : last, :]
        total = total + post[0, x, row, :]
        total = total + shift_z(post[5, x, row, :], 1) + shift_z(post[6, x, row, :], -1)
        if before is not None:
            total = total + post[1, before, row, :]
        if after is not None:
            total = total + post[2, after, row, :]
        msg[2 + slot, here, :] = hadj[3 + slot, x, row, :] + jnp.where(label[x, row, :] == 2, total, 0.0)


def second_interior(source, rows_in, porosity, label, adjoint, heat_adjoint):
    cells = label.shape
    depth, rows, columns = cells
    far = depth - 1

    def kernel(source, rows_ref, porosity, label, adj, hadj, post, heat, aux, msg, moved):
        second_planes(range(1, far), source, rows_ref, None, None, porosity, label, post, heat, aux, moved)
        for_planes(range(0, depth), lambda x: input_rows(x, adj, label, msg))
        for_planes(range(2, far - 1), lambda x: heat_rows(x, post, hadj, label, msg))

    return call(
        kernel,
        "second_interior",
        "vvvvvv",
        [vmem(7, *cells), vmem(7, *cells), vmem(4, *cells), vmem(17, depth, columns)],
        (source, rows_in, porosity, label, adjoint, heat_adjoint),
        scratch=[pltpu.VMEM((19, rows, columns), F32)],
        micros=0.0,
    )


def second_boundary(source, rows_in, face_a, face_b, porosity, label, heat_adjoint, post, heat, aux, msg):
    cells = label.shape
    depth, rows, columns = cells
    far = depth - 1
    last = rows - 1

    def kernel(source, rows_ref, a_ref, b_ref, porosity, label, hadj, post_in, heat_in, aux_in, msg_in,
               post, heat, aux, msg, moved):
        even = lax.rem(lax.axis_index("gx"), 2) == 0

        def low(slot):
            return pick(even, b_ref[slot], a_ref[slot])

        def high(slot):
            return pick(even, a_ref[slot], b_ref[slot])

        second_planes((0, far), source, rows_ref, low, high, porosity, label, post, heat, aux, moved)

        for x in (0, 1, far - 1, far):
            heat_rows(x, post, hadj, label, msg)
        msg[4] = jnp.zeros((depth, columns), F32)
        msg[4, 0:1, :] = post[1, far, 0:1, :]
        msg[4, 1:2, :] = post[1, far, last : last + 1, :]
        msg[4, 2:3, :] = post[2, 0, 0:1, :]
        msg[4, 3:4, :] = post[2, 0, last : last + 1, :]

    return call(
        kernel,
        "second_boundary",
        "vvvvvvvvvvv",
        [vmem(7, *cells), vmem(7, *cells), vmem(4, *cells), vmem(17, depth, columns)],
        (source, rows_in, face_a, face_b, porosity, label, heat_adjoint, post, heat, aux, msg),
        scratch=[pltpu.VMEM((19, rows, columns), F32)],
        aliases={7: 0, 8: 1, 9: 2, 10: 3},
        micros=0.0,
    )


def plane_of(ref, slot):
    return ref[SEEDS + 16 * slot : SEEDS + 16 * (slot + 1)]


def second_faces(post, heat_adjoint, adjoint, label, rows_in, aux, heat, porosity, chosen):
    depth, rows, columns = label.shape
    far = depth - 1

    def kernel(post, hadj, adj, label, rows_ref, aux, heat, porosity, chosen, a_ref, b_ref):
        even = lax.rem(lax.axis_index("gx"), 2) == 0

        def partial(x, other):
            total = post[0, x] + other
            total = total + shift_y(post[3, x], 1, rows_ref[0, x : x + 1, :])
            total = total + shift_y(post[4, x], -1, rows_ref[1, x : x + 1, :])
            return total + shift_z(post[5, x], 1) + shift_z(post[6, x], -1)

        def put(start, high, low):
            where = slice(start, start + high.shape[0])
            a_ref[where] = pick(even, high, low)
            b_ref[where] = pick(even, low, high)

        put(0, post[1, far], post[2, 0])
        high_seed = hadj[2, far] + jnp.where(label[far] == 2, partial(far, post[1, far - 1]), 0.0)
        low_seed = hadj[1, 0] + jnp.where(label[0] == 2, partial(0, post[2, 1]), 0.0)
        put(rows, high_seed, low_seed)
        place = lax.broadcasted_iota(jnp.int32, (8, columns), 0)

        def spread(slot):
            return jnp.broadcast_to(rows_ref[4, slot : slot + 1, :], (8, columns))

        put(2 * rows, jnp.where(place == 0, spread(1), spread(0)), jnp.where(place == 0, spread(3), spread(2)))
        for slot in range(5):
            i, j = FPLUS[slot], FMINUS[slot]
            low, high = adj[i, 0], adj[j, far]
            if VEL[i][1]:
                low = shift_y(low, -VEL[i][1], rows_ref[adjoint_slot(i), 0:1, :])
                high = shift_y(high, -VEL[j][1], rows_ref[adjoint_slot(j), far : far + 1, :])
            put(SEEDS + 16 * slot, high, low)
        put(SEEDS + 80, jnp.where(label[far] == 2, 1.0, 0.0), jnp.where(label[0] == 2, 1.0, 0.0))
        highs = source_weights(aux, heat, porosity, label, chosen, far, 1)
        lows = source_weights(aux, heat, porosity, label, chosen, 0, 2)
        for slot, (high, low) in enumerate(zip(highs[EARLY:], lows[EARLY:])):
            put(SEEDS + 16 * (6 + slot), high, low)

    shape = (SEEDS + 16 * (11 - EARLY), columns)
    return call(
        kernel,
        "second_faces",
        "v" * 9,
        [vmem(*shape)] * 2,
        (post, heat_adjoint, adjoint, label, rows_in, aux, heat, porosity, chosen),
    )


def costate_rows(x, lam, msg):
    here = pl.ds(x, 1)
    last = lam.shape[2] - 1
    for i in YPLUS:
        msg[row_slot(i), here, :] = lam[i, x, 0:1, :]
    for i in YMINUS:
        msg[row_slot(i), here, :] = lam[i, x, last : last + 1, :]


def second_adjoint(planes, name, fixed, arrived, state, micros):
    adj, hadj, post, heat, aux, porosity, label, rows_in = fixed
    cells = label.shape
    depth, rows, columns = cells
    far = depth - 1
    last = rows - 1
    first = state is None
    boundary = isinstance(planes, tuple)
    lit_planes = range(planes[0] - 1, planes[-1] + 2) if first else ((0, far) if boundary else ())

    def kernel(*refs):
        refs = list(refs)
        adj, hadj, post, heat, aux, porosity, label, rows_ref = refs[:8]
        refs = refs[8:]
        if boundary:
            sa, sb = refs[:2]
        refs = refs[len(arrived) :]
        if not first:
            refs = refs[4:]
        lam, sens, lit, msg = refs[:4]
        sides = refs[4] if boundary else None
        moved = refs[-1]
        even = lax.rem(lax.axis_index("gx"), 2) == 0
        tail = 2 * rows

        def from_left(where):
            return pick(even, sb[where], sa[where])

        def from_right(where):
            return pick(even, sa[where], sb[where])

        def light(x):
            here = pl.ds(x, 1)
            before, after = neighbour(x, -1, far), neighbour(x, 1, far)
            total = post[0, x]
            total = total + (from_left(slice(0, rows)) if before is None else post[1, before])
            total = total + (from_right(slice(0, rows)) if after is None else post[2, after])
            total = total + shift_y(post[3, x], 1, rows_ref[0, here, :])
            total = total + shift_y(post[4, x], -1, rows_ref[1, here, :])
            total = total + shift_z(post[5, x], 1) + shift_z(post[6, x], -1)
            lit[x] = jnp.where(label[x] == 2, total, 0.0)

        if lit_planes:
            for_planes(lit_planes, light)

        def body(x):
            here = pl.ds(x, 1)
            before, after = neighbour(x, -1, far), neighbour(x, 1, far)
            glow = lit[x]
            moved[19] = hadj[0, x] + glow
            if after is None:
                moved[20] = from_right(slice(rows, tail)) + pick(even, plane_of(sa, 5), plane_of(sb, 5)) * post[1, far]
            else:
                moved[20] = hadj[1, after] + lit[after]
            if before is None:
                moved[21] = from_left(slice(rows, tail)) + pick(even, plane_of(sb, 5), plane_of(sa, 5)) * post[2, 0]
            else:
                moved[21] = hadj[2, before] + lit[before]
            above = post[3, x, last : last + 1, :]
            below = post[4, x, 0:1, :]
            if before is None:
                above = above + from_left(slice(tail + 1, tail + 2))
                below = below + from_left(slice(tail, tail + 1))
            if after is None:
                above = above + from_right(slice(tail + 1, tail + 2))
                below = below + from_right(slice(tail, tail + 1))
            moved[22] = shift_y(hadj[3, x] + glow, -1, rows_ref[2, here, :] + rows_ref[15, here, :] * above)
            moved[23] = shift_y(hadj[4, x] + glow, 1, rows_ref[3, here, :] + rows_ref[16, here, :] * below)
            moved[24] = shift_z(hadj[5, x] + glow, -1)
            moved[25] = shift_z(hadj[6, x] + glow, 1)
            for i in range(19):
                moved[i] = moved_population(
                    adj,
                    i,
                    x,
                    -1,
                    adjoint_slot,
                    rows_ref,
                    lambda: pick(even, plane_of(sb, FMINUS.index(i)), plane_of(sa, FMINUS.index(i))),
                    lambda: pick(even, plane_of(sa, FPLUS.index(i)), plane_of(sb, FPLUS.index(i))),
                    far,
                )
            for r, c in tiles(rows, columns):
                inlet = label[x, r, c] == 1
                density, ux, uy, uz = (aux[i, x, r, c] for i in range(4))
                warm = [heat[i, x, r, c] for i in range(7)]
                mu = [moved[i, r, c] for i in range(19)]
                nu = [moved[19 + i, r, c] for i in range(7)]
                result, result_heat, part = collide_adjoint(
                    density, (ux, uy, uz), warm, porosity[x, r, c], inlet, mu, nu
                )
                for i, value in enumerate(result + result_heat):
                    lam[i, x, r, c] = value
                sens[x, r, c] = part

        for_planes(planes, body)
        if boundary:
            for slot in range(6):
                sides[slot] = lam[PLUS[slot], 0]
                sides[6 + slot] = lam[MINUS[slot], far]
        for_planes(planes, lambda x: costate_rows(x, lam, msg))

    outs = [vmem(COUNT, *cells), vmem(*cells), vmem(*cells), vmem(12, depth, columns)]
    if boundary:
        outs.append(vmem(12, rows, columns))
    args = fixed + arrived + (() if first else state)
    base = len(args) - 4
    return call(
        kernel,
        name,
        "v" * len(args),
        outs,
        args,
        scratch=[pltpu.VMEM((COUNT, rows, columns), F32)],
        aliases=None if first else {base + n: n for n in range(4)},
        micros=micros,
    )


def arriving(lam, rows_ref, moved, x, far, low, high):
    for i in range(COUNT):
        moved[i] = moved_population(
            lam, i, x, -1, row_slot, rows_ref, lambda: low(MINUS.index(i)), lambda: high(PLUS.index(i)), far
        )


def first_sensitivity(lam, rows_in, fixed, sens_one, weights_a, weights_b, rate_a, rate_b, waves):
    aux, heat, porosity, label, chosen = fixed
    depth, rows, columns = label.shape
    far = depth - 1
    half = columns // 2
    count = depth + 2

    def kernel(lam, rows_ref, aux, heat, porosity, label, chosen, sens_ref, a_ref, b_ref, ra_ref, rb_ref, waves_ref,
               own, other, moved, total):
        even = lax.rem(lax.axis_index("gx"), 2) == 0
        core = lax.axis_index("gy")

        def nothing(slot):
            return jnp.zeros((rows, columns), F32)

        def body(x):
            arriving(lam, rows_ref, moved, x, far, nothing, nothing)
            for r, c in tiles(rows, columns):
                inlet = label[x, r, c] == 1
                density, ux, uy, uz = (aux[i, x, r, c] for i in range(4))
                warm = [heat[i, x, r, c] for i in range(7)]
                mu = [moved[i, r, c] for i in range(19)]
                nu = [moved[19 + i, r, c] for i in range(7)]
                _, _, part = collide_adjoint(density, (ux, uy, uz), warm, porosity[x, r, c], inlet, mu, nu)
                total[x, r, c] = jnp.where(chosen[x, r, c] > 0.0, part + sens_ref[x, r, c], 0.0)

        for_planes((0, far), body)
        for_planes(range(1, far), body)
        def weights(slot, reverse):
            if slot < EARLY:
                of_a, of_b = ra_ref[6 + slot], rb_ref[6 + slot]
            else:
                of_a, of_b = plane_of(a_ref, 6 + slot - EARLY), plane_of(b_ref, 6 + slot - EARLY)
            return pick(even, of_b, of_a) if reverse else pick(even, of_a, of_b)

        for place, x, members, reverse in ((depth, 0, PLUS, True), (depth + 1, far, MINUS, False)):
            rate, scale, *vector = (weights(slot, reverse) for slot in range(5))
            speed = vector[0] * vector[0] + vector[1] * vector[1] + vector[2] * vector[2]
            result = jnp.zeros((rows, columns), F32)
            for i in members:
                value = lam[i, x]
                if VEL[i][1]:
                    value = shift_y(value, -VEL[i][1], rows_ref[row_slot(i), x : x + 1, :])
                value = shift_z(value, -VEL[i][2])
                if i < 19:
                    part = along(VEL[i], vector)
                    result = result + (fluid_wts[i] * scale) * (part - speed + 3.0 * part * part) * value
                else:
                    result = result + rate * value
            total[place] = result
        flat = total[...].reshape(count * rows, columns)
        own[...] = multiply(flat, waves_ref[core]).reshape(count, rows, half)
        other[...] = multiply(flat, waves_ref[1 - core]).reshape(count, rows, half)

    args = (lam, rows_in) + fixed + (sens_one, weights_a, weights_b, rate_a, rate_b, waves)
    return call(
        kernel,
        "first_sensitivity",
        "v" * len(args),
        [vmem(count, rows, half)] * 2,
        args,
        scratch=[pltpu.VMEM((COUNT, rows, columns), F32), pltpu.VMEM((count, rows, columns), F32)],
    )


def first_adjoint(groups, name, lam, rows_in, fixed, arrived, early_planes, early):
    aux, heat, porosity, label = fixed
    cells = label.shape
    depth, rows, columns = cells
    far = depth - 1
    planes = [x for group in groups for x in group]
    count = len(planes)
    last = early is not None

    def kernel(*refs):
        refs = list(refs)
        lam, rows_ref, aux, heat, porosity, label = refs[:6]
        refs = refs[6:]
        if last:
            b_ref, a_ref, early_ref, fluid_out, heat_out, token, moved, out, sem = refs
            token[...] = jnp.zeros((8, 128), F32)
        else:
            out, moved = refs
        even = lax.rem(lax.axis_index("gx"), 2) == 0

        def place(x):
            return planes.index(x) if isinstance(x, int) else x - groups[-1][0] + count - len(groups[-1])

        def writes(source, n, x, slot):
            return (
                pltpu.make_async_copy(source.at[0:19, n], fluid_out.at[:, x], sem.at[2 * slot]),
                pltpu.make_async_copy(source.at[19:26, n], heat_out.at[:, x], sem.at[2 * slot + 1]),
            )

        def low(slot):
            return pick(even, b_ref[slot], a_ref[slot])

        def high(slot):
            return pick(even, a_ref[slot], b_ref[slot])

        def body(x):
            n = place(x)
            arriving(lam, rows_ref, moved, x, far, low, high)
            for r, c in tiles(rows, columns):
                inlet = label[x, r, c] == 1
                density, ux, uy, uz = (aux[i, x, r, c] for i in range(4))
                warm = [heat[i, x, r, c] for i in range(7)]
                mu = [moved[i, r, c] for i in range(19)]
                nu = [moved[19 + i, r, c] for i in range(7)]
                result, result_heat, _ = collide_adjoint(density, (ux, uy, uz), warm, porosity[x, r, c], inlet, mu, nu)
                for i, value in enumerate(result + result_heat):
                    out[i, n, r, c] = value
            if last:
                for copy in writes(out, n, x, n):
                    copy.start()

        early_copies = []
        if last:
            for n, x in enumerate(early_planes):
                early_copies += writes(early_ref, n, x, count + n)
        for copy in early_copies:
            copy.start()
        for group in groups:
            for_planes(group, body)
        if last:

            def finish(x):
                for copy in writes(out, place(x), x, place(x)):
                    copy.wait()

            for group in groups:
                for_planes(group, finish)
        for copy in early_copies:
            copy.wait()

    buffer = (COUNT, count, rows, columns)
    moved = pltpu.VMEM((COUNT, rows, columns), F32)
    args = (lam, rows_in) + fixed + arrived + ((early,) if last else ())
    if last:
        outs = [hbm(19, *cells), hbm(7, *cells), vmem(8, 128)]
        scratch = [moved, pltpu.VMEM(buffer, F32), pltpu.SemaphoreType.DMA((2 * (count + len(early_planes)),))]
    else:
        outs = [vmem(*buffer)]
        scratch = [moved]
    return call(kernel, name, "v" * len(args), outs, args, scratch=scratch)


def halves(value):
    high = value.astype(jnp.bfloat16)
    return high, (value - high.astype(F32)).astype(jnp.bfloat16)


def multiply(first, second):
    a, b = halves(first)
    c, d = halves(second)
    small = jnp.dot(a, d, preferred_element_type=F32) + jnp.dot(b, c, preferred_element_type=F32)
    return jnp.dot(a, c, preferred_element_type=F32) + small


def hartley(length):
    index = np.arange(length)
    angle = 2.0 * np.pi * ((index[:, None] * index[None, :]) % length) / length
    return (np.cos(angle) + np.sin(angle)) / np.sqrt(length)


def filter_tables(depth, count_y, count_z):
    half = count_z // 2
    wave_z = hartley(count_z)
    waves = np.stack([wave_z[:, :half], wave_z[:, half:]]).astype(np.float32)
    waves_back = np.stack([wave_z[:half], wave_z[half:]]).astype(np.float32)
    wave_y = np.kron(np.eye(depth), hartley(count_y)).astype(np.float32)
    wave_ends = np.kron(np.eye(2), hartley(count_y)).astype(np.float32)
    symbol_y = 2.0 - 2.0 * np.cos(2.0 * np.pi * np.arange(count_y) / count_y)
    symbol_z = 2.0 - 2.0 * np.cos(2.0 * np.pi * np.arange(count_z) / count_z)
    weight = float(RADIUS * RADIUS)
    centre = (1.0 + weight * (2.0 + symbol_y[:, None] + symbol_z[None, :])) / weight
    ratio = 2.0 / (centre + np.sqrt(centre * centre - 4.0))
    peak = 1.0 / (weight * (1.0 / ratio - ratio))
    fields = np.stack([ratio, np.log(ratio) * depth, peak]).astype(np.float32)
    fields = np.stack([fields[:, :, :half], fields[:, :, half:]])
    return waves, waves_back, wave_y, wave_ends, fields


def to_modes(own, other, wave_y, wave_ends, fields):
    count, rows, half = own.shape
    depth = count - 2
    full = 2 * rows
    inside = depth * full

    def kernel(own_ref, other_ref, wave_ref, small_ref, field_ref, modes, ends, both):
        core = lax.axis_index("gy")
        for x in range(count):
            both[x * full : x * full + rows] = own_ref[x]
            both[x * full + rows : (x + 1) * full] = other_ref[x]
        modes[0:inside] = multiply(wave_ref[...], both[0:inside])
        modes[inside : inside + 2 * full] = multiply(small_ref[...], both[inside : inside + 2 * full])
        ratio = field_ref[core, 0]
        before, after = modes[inside : inside + full], modes[inside + full : inside + 2 * full]
        head = before
        for x in range(depth):
            head = head * ratio + modes[x * full : (x + 1) * full]
        ends[0] = head * ratio + after
        tail = after
        for x in range(depth - 1, -1, -1):
            tail = tail * ratio + modes[x * full : (x + 1) * full]
        ends[1] = tail * ratio + before

    return call(
        kernel,
        "to_modes",
        "vvvvv",
        [vmem(count * full, half), vmem(2, full, half)],
        (own, other, wave_y, wave_ends, fields),
        scratch=[pltpu.VMEM((count * full, half), F32)],
    )


def join_segments(ends, arrived, carry, fields, reach, after):
    first = carry is None

    def kernel(*refs):
        ends_ref, in_ref, field_ref = refs[:3]
        carry_ref = None if first else refs[3]
        ends_out, carry_out = refs[-2:]
        core = lax.axis_index("gy")
        index = lax.axis_index("gx")
        place = lax.rem(index, reach)
        upper = lax.rem(lax.div(index, reach), 2) == 1
        rate = field_ref[core, 1]
        whole = jnp.exp(rate * float(reach))
        forward = jnp.exp(rate * place.astype(F32))
        backward = jnp.exp(rate * (reach - 1 - place).astype(F32))
        head, tail = ends_ref[0], ends_ref[1]
        head_in, tail_in = in_ref[0], in_ref[1]
        left = pick(upper, forward * head_in, jnp.zeros_like(head))
        right = pick(upper, jnp.zeros_like(head), backward * tail_in)
        carry_out[0] = left if first else carry_ref[0] + left
        carry_out[1] = right if first else carry_ref[1] + right
        ends_out[0] = pick(upper, head + whole * head_in, head_in + whole * head)
        ends_out[1] = pick(upper, tail_in + whole * tail, tail + whole * tail_in)

    args = (ends, arrived, fields) + (() if first else (carry,)) + after
    return call(kernel, "join_segments", "v" * len(args), [vmem(*ends.shape)] * 2, args, micros=0.0)


def from_modes(modes, ends, carry, wave_y, fields, depth, parts, after):
    half = modes.shape[1]
    full = modes.shape[0] // (depth + 2)
    rows = full // 2
    inside = depth * full

    def kernel(modes_ref, ends_ref, carry_ref, wave_ref, field_ref, after_ref, own, other, solved):
        core = lax.axis_index("gy")
        index = lax.axis_index("gx")
        ratio, rate, peak = field_ref[core, 0], field_ref[core, 1], field_ref[core, 2]
        around = 1.0 / (1.0 - jnp.exp(rate * float(parts)))
        left = carry_ref[0] + jnp.exp(rate * index.astype(F32)) * around * ends_ref[0]
        right = carry_ref[1] + jnp.exp(rate * (parts - 1 - index).astype(F32)) * around * ends_ref[1]
        run = left + ratio * modes_ref[inside : inside + full]
        for x in range(depth):
            run = run + modes_ref[x * full : (x + 1) * full]
            solved[x * full : (x + 1) * full] = run
            run = run * ratio
        run = right + ratio * modes_ref[inside + full : inside + 2 * full]
        for x in range(depth - 1, -1, -1):
            solved[x * full : (x + 1) * full] = peak * (solved[x * full : (x + 1) * full] + run)
            run = ratio * (run + modes_ref[x * full : (x + 1) * full])
        back = multiply(wave_ref[...], solved[...])
        for x in range(depth):
            own[x * rows : (x + 1) * rows] = back[x * full : x * full + rows]
            other[x * rows : (x + 1) * rows] = back[x * full + rows : (x + 1) * full]

    flat = (depth * rows, half)
    return call(
        kernel,
        "from_modes",
        "vvvvvv",
        [vmem(*flat)] * 2,
        (modes, ends, carry, wave_y, fields, after),
        scratch=[pltpu.VMEM((inside, half), F32)],
    )


def own_transform(own, waves_back):
    flat, half = own.shape

    def kernel(own_ref, wave_ref, out):
        out[...] = multiply(own_ref[...], wave_ref[lax.axis_index("gy")])

    return call(kernel, "own_transform", "vv", [vmem(flat, 2 * half)], (own, waves_back))


def last_transform(partial, other, waves_back, depth):
    flat, half = other.shape
    rows = flat // depth
    step = depth // 2

    def kernel(partial_ref, other_ref, wave_ref, out_ref, out, sem):
        copies = []
        for n in range(2):
            where = slice(n * step * rows, (n + 1) * step * rows)
            result = partial_ref[where] + multiply(other_ref[where], wave_ref[1 - lax.axis_index("gy")])
            part = slice(n * step, (n + 1) * step)
            out[part] = result.reshape(step, rows, 2 * half)
            copies.append(pltpu.make_async_copy(out.at[part], out_ref.at[part], sem.at[n]))
            copies[n].start()
        for copy in copies:
            copy.wait()

    shape = (depth, rows, 2 * half)
    return call(
        kernel,
        "last_transform",
        "vvv",
        [hbm(*shape)],
        (partial, other, waves_back),
        scratch=[pltpu.VMEM(shape, F32), pltpu.SemaphoreType.DMA((2,))],
    )


def per_device(fluid_state, heat_state, design, cell_type, boundary, fluid_adjoint, heat_adjoint):
    depth, rows, columns = design.shape
    far = depth - 1
    parts = lax.axis_size("gx")
    waves, waves_back, wave_y, wave_ends, fields = filter_tables(depth, 2 * rows, columns)

    pairs_a = [(i, i ^ 1) for i in range(parts)]
    pairs_b = [(i, (i + 1) % parts if i % 2 else (i - 1) % parts) for i in range(parts)]

    def across(value):
        return lax.ppermute(value, "gy", [(0, 1), (1, 0)])

    def sideways(first, second):
        first = lax.ppermute(first, "gx", pairs_a)
        second = lax.ppermute(second, "gx", pairs_b)
        return first, second

    adj, hadj = fluid_adjoint, heat_adjoint
    post, heat_edge, aux_edge, porosity, label, chosen, sides, corner, design, kind = first_boundary(
        *(in_hbm(value) for value in (fluid_state, heat_state, design, cell_type, boundary))
    )
    face_a, face_b, token = first_faces(sides, across(corner), label, aux_edge, heat_edge, porosity, chosen)
    face_a, face_b = sideways(face_a, face_b)
    rate_a, rate_b = face_a, face_b
    heat_zero = heat_state
    post, aux_zero, porosity, chosen, rows_one = first_interior(
        fluid_state, heat_zero, post, aux_edge, porosity, chosen, design, kind, label, token
    )
    rows_one = across(rows_one)
    post_one, heat_one, aux_one, rows_heat = second_interior(post, rows_one, porosity, label, adj, hadj)
    post_one, heat_one, aux_one, rows_heat = second_boundary(
        post, rows_one, face_a, face_b, porosity, label, hadj, post_one, heat_one, aux_one, rows_heat
    )
    rows_heat = across(rows_heat)
    seed_a, seed_b = second_faces(post_one, hadj, adj, label, rows_heat, aux_zero, heat_zero, porosity, chosen)
    seed_a, seed_b = sideways(seed_a, seed_b)
    fixed = (adj, hadj, post_one, heat_one, aux_one, porosity, label, rows_heat)
    state = second_adjoint(range(2, far - 1), "adjoint_inner", fixed, (), None, 0.0)
    lam, sens_one, lit, rows_two, sides = second_adjoint(
        (0, 1, far - 1, far), "adjoint_outer", fixed, (seed_a, seed_b), tuple(state), 0.0
    )
    rows_two = across(rows_two)
    face_a, face_b = costate_faces(sides, rows_two)
    face_a, face_b = sideways(face_a, face_b)
    fixed = (aux_zero, heat_zero, porosity, label)
    own, other = first_sensitivity(lam, rows_two, fixed + (chosen,), sens_one, seed_a, seed_b, rate_a, rate_b, waves)
    early = first_adjoint(((1,),), "costate_early", lam, rows_two, fixed, (), None, None)
    fluid_costate, heat_costate, token = first_adjoint(
        ((0, far), range(2, far)), "costate_rest", lam, rows_two, fixed, (face_b, face_a), (1,), early
    )
    other = across(other)
    modes, ends = to_modes(own, other, wave_y, wave_ends, fields)
    carry = None
    reach = 1
    while reach < parts:
        arrived = lax.ppermute(ends, "gx", [(i, i ^ reach) for i in range(parts)])
        ends, carry = join_segments(ends, arrived, carry, fields, reach, (early,) if reach == 1 else ())
        reach = 2 * reach
    own, other = from_modes(modes, ends, carry, wave_y, fields, depth, parts, token)
    other = across(other)
    partial = own_transform(own, waves_back)
    return (fluid_costate, heat_costate, last_transform(partial, other, waves_back, depth))


def solution(mesh):
    return jax.shard_map(
        per_device,
        mesh=mesh,
        in_specs=(
            P(None, ("case", "gx"), "gy", None),
            P(None, ("case", "gx"), "gy", None),
            P(("case", "gx"), "gy", None),
            P(("case", "gx"), "gy", None),
            P(("case", "gx"), "gy", None),
            P(None, ("case", "gx"), "gy", None),
            P(None, ("case", "gx"), "gy", None),
        ),
        out_specs=(
            P(None, ("case", "gx"), "gy", None),
            P(None, ("case", "gx"), "gy", None),
            P(("case", "gx"), "gy", None),
        ),
        check_vma=False,
    )
```

```python
import numpy as np
import jax
import jax.numpy as jnp
from jax import lax
from jax.experimental import pallas as pl
from jax.experimental.pallas import tpu as pltpu
from jax.sharding import PartitionSpec as P

RADIUS = 4

fluid_vel = [
    (0, 0, 0),
    (1, 0, 0),
    (-1, 0, 0),
    (0, 1, 0),
    (0, -1, 0),
    (0, 0, 1),
    (0, 0, -1),
    (1, 1, 0),
    (-1, -1, 0),
    (1, -1, 0),
    (-1, 1, 0),
    (1, 0, 1),
    (-1, 0, -1),
    (1, 0, -1),
    (-1, 0, 1),
    (0, 1, 1),
    (0, -1, -1),
    (0, 1, -1),
    (0, -1, 1),
]
fluid_wts = [1.0 / 3.0] + [1.0 / 18.0] * 6 + [1.0 / 36.0] * 12
inlet_speed = 0.05
inlet_eq = [
    weight
    * (
        1.0
        + 3.0 * inlet_speed * entry[2]
        + 4.5 * (inlet_speed * entry[2]) ** 2
        - 1.5 * inlet_speed**2
    )
    for entry, weight in zip(fluid_vel, fluid_wts)
]

VEL = fluid_vel + fluid_vel[:7]
COUNT = len(VEL)
PLUS = [i for i in range(COUNT) if VEL[i][0] == 1]
MINUS = [i for i in range(COUNT) if VEL[i][0] == -1]
YPLUS = [i for i in range(COUNT) if VEL[i][1] == 1]
YMINUS = [i for i in range(COUNT) if VEL[i][1] == -1]
FPLUS = [i for i in PLUS if i < 19]
FMINUS = [i for i in MINUS if i < 19]
FYPLUS = [i for i in YPLUS if i < 19]
FYMINUS = [i for i in YMINUS if i < 19]

VMEM_BYTES = 24 * 1024 * 1024
EARLY = 4
SEEDS = 40
F32 = jnp.float32


def params():
    return pltpu.CompilerParams(vmem_limit_bytes=VMEM_BYTES)


def cost(micros):
    return pl.CostEstimate(flops=int(micros * 1e9), bytes_accessed=0, transcendentals=0)


def shift_y(value, step, ghost):
    if step == 0:
        return value
    rows = value.shape[0]
    moved = pltpu.roll(value, step % rows, 0)
    place = lax.broadcasted_iota(jnp.int32, value.shape, 0)
    edge = 0 if step > 0 else rows - 1
    return jnp.where(place == edge, jnp.broadcast_to(ghost, value.shape), moved)


def shift_z(value, step):
    if step == 0:
        return value
    return pltpu.roll(value, step % value.shape[1], 1)


def pick(flag, first, second):
    return jnp.where(flag, first, second)


def tiles(rows, columns):
    return [
        (slice(r, r + 8), slice(c, c + 128)) for r in range(0, rows, 8) for c in range(0, columns, 128)
    ]


def porosity_of(design, kind):
    return jnp.where(kind == 2, design, jnp.where(kind == 1, 0.0, 1.0))


def heat_rate_of(porosity):
    return 1.0 / (0.55 + 0.9 * (1.0 - porosity))


def moments(pops, porosity):
    density = pops[0]
    for value in pops[1:]:
        density = density + value
    diff = {i: pops[i] - pops[i + 1] for i in range(1, 19, 2)}
    flux_x = diff[1] + diff[7] + diff[9] + diff[11] + diff[13]
    flux_y = diff[3] + diff[7] - diff[9] + diff[15] + diff[17]
    flux_z = diff[5] + diff[11] - diff[13] + diff[15] - diff[17]
    inverse = (0.1 + porosity) / (density * (0.5 + 0.6 * porosity))
    return density, (flux_x * inverse, flux_y * inverse, flux_z * inverse)


def along(entry, vector):
    total = None
    for part, value in zip(entry, vector):
        if part == 0:
            continue
        if total is None:
            total = value if part == 1 else -value
        else:
            total = total + value if part == 1 else total - value
    return total


def collide_fluid(pops, density, velocity, inlet):
    speed = velocity[0] * velocity[0] + velocity[1] * velocity[1] + velocity[2] * velocity[2]
    scaled = 1.25 * density
    base = scaled - 1.5 * scaled * speed
    result = [jnp.where(inlet, inlet_eq[0], base * (1.0 / 3.0) - 0.25 * pops[0])]
    for i in range(1, 19, 2):
        weight = fluid_wts[i]
        part = along(VEL[i], velocity)
        flow = scaled * part
        even = weight * base + (4.5 * weight) * (flow * part)
        odd = (3.0 * weight) * flow
        result.append(jnp.where(inlet, inlet_eq[i], even + odd - 0.25 * pops[i]))
        result.append(jnp.where(inlet, inlet_eq[i + 1], even - odd - 0.25 * pops[i + 1]))
    return result


def collide_heat(pops, velocity, porosity, inlet):
    temper = pops[0]
    for value in pops[1:]:
        temper = temper + value
    rate = heat_rate_of(porosity)
    keep = 1.0 - rate
    warm = rate * temper
    base = warm + (1.0 - porosity)
    result = [jnp.where(inlet, 0.0, keep * pops[0] + 0.25 * base)]
    for axis in range(3):
        i = 1 + 2 * axis
        odd = 0.5 * (warm * velocity[axis])
        even = 0.125 * base
        result.append(jnp.where(inlet, 0.0, keep * pops[i] + (even + odd)))
        result.append(jnp.where(inlet, 0.0, keep * pops[i + 1] + (even - odd)))
    return result


def collide_adjoint(density, velocity, heat, porosity, inlet, mu, nu):
    ux, uy, uz = velocity
    mu = [jnp.where(inlet, 0.0, value) for value in mu]
    nu = [jnp.where(inlet, 0.0, value) for value in nu]
    even = {i: mu[i] + mu[i + 1] for i in range(1, 19, 2)}
    odd = {i: mu[i] - mu[i + 1] for i in range(1, 19, 2)}
    wa, wb = 1.0 / 18.0, 1.0 / 36.0
    xy_sum, xz_sum, yz_sum = even[7] + even[9], even[11] + even[13], even[15] + even[17]
    m0 = mu[0] * (1.0 / 3.0) + wa * (even[1] + even[3] + even[5]) + wb * (xy_sum + xz_sum + yz_sum)
    m1x = wa * odd[1] + wb * (odd[7] + odd[9] + odd[11] + odd[13])
    m1y = wa * odd[3] + wb * (odd[7] - odd[9] + odd[15] + odd[17])
    m1z = wa * odd[5] + wb * (odd[11] - odd[13] + odd[15] - odd[17])
    mxx = wa * even[1] + wb * (xy_sum + xz_sum)
    myy = wa * even[3] + wb * (xy_sum + yz_sum)
    mzz = wa * even[5] + wb * (xz_sum + yz_sum)
    mxy = wb * (even[7] - even[9])
    mxz = wb * (even[11] - even[13])
    myz = wb * (even[15] - even[17])
    vx = mxx * ux + mxy * uy + mxz * uz
    vy = mxy * ux + myy * uy + myz * uz
    vz = mxz * ux + myz * uy + mzz * uz
    speed = ux * ux + uy * uy + uz * uz
    slope = (
        m0 * (1.0 - 1.5 * speed)
        + 3.0 * (ux * m1x + uy * m1y + uz * m1z)
        + 4.5 * (ux * vx + uy * vy + uz * vz)
    )
    rate = heat_rate_of(porosity)
    keep = 1.0 - rate
    temper = heat[0]
    for value in heat[1:]:
        temper = temper + value
    n0 = 0.25 * nu[0] + 0.125 * (nu[1] + nu[2] + nu[3] + nu[4] + nu[5] + nu[6])
    n1x, n1y, n1z = (0.125 * (nu[i] - nu[i + 1]) for i in (1, 3, 5))
    warm = 4.0 * rate * temper
    scaled = 3.75 * density
    bar_x = scaled * (m1x - m0 * ux + 3.0 * vx) + warm * n1x
    bar_y = scaled * (m1y - m0 * uy + 3.0 * vy) + warm * n1y
    bar_z = scaled * (m1z - m0 * uz + 3.0 * vz) + warm * n1z
    work = bar_x * ux + bar_y * uy + bar_z * uz
    ramp = 0.1 + porosity
    drag = 0.5 + 0.6 * porosity
    over = 1.0 / (density * drag)
    inverse = ramp * over
    b = (bar_x * inverse, bar_y * inverse, bar_z * inverse)
    a = 1.25 * slope - work * (drag * over)
    lam = [a - 0.25 * mu[0]]
    for i in range(1, 19, 2):
        part = along(VEL[i], b)
        lam.append((a + part) - 0.25 * mu[i])
        lam.append((a - part) - 0.25 * mu[i + 1])
    pull = n0 + 4.0 * (ux * n1x + uy * n1y + uz * n1z)
    a_heat = rate * pull
    lam_heat = [keep * value + a_heat for value in nu]
    dot = nu[0] * heat[0]
    for first, second in zip(nu[1:], heat[1:]):
        dot = dot + first * second
    sens = work * (0.44 / (ramp * drag)) - n0 + (0.9 * rate * rate) * (temper * pull - dot)
    return lam, lam_heat, sens


IN_VMEM = pl.BlockSpec(memory_space=pltpu.VMEM)
IN_HBM = pl.BlockSpec(memory_space=pltpu.HBM)


def vmem(*shape):
    return pltpu.VMEM(shape, F32)


def hbm(*shape):
    return pltpu.HBM(shape, F32)


def in_hbm(value):
    return pltpu.with_memory_space_constraint(value, pltpu.HBM)


def call(kernel, name, specs, outs, args, scratch=(), aliases=None, micros=0.0):
    spec_of = {"v": IN_VMEM, "h": IN_HBM}
    single = len(outs) == 1
    args = [
        pltpu.with_memory_space_constraint(value, pltpu.VMEM) if letter == "v" else value
        for letter, value in zip(specs, args)
    ]
    out_specs = [IN_HBM if out.memory_space == pltpu.HBM else IN_VMEM for out in outs]
    return pl.pallas_call(
        kernel,
        in_specs=[spec_of[letter] for letter in specs],
        out_specs=out_specs[0] if single else out_specs,
        out_shape=outs[0] if single else outs,
        scratch_shapes=list(scratch),
        input_output_aliases=aliases or {},
        compiler_params=params(),
        cost_estimate=cost(micros),
        name=name,
    )(*args)


def row_slot(i):
    return YPLUS.index(i) if VEL[i][1] > 0 else 6 + YMINUS.index(i)


def adjoint_slot(i):
    return 5 + FYPLUS.index(i) if VEL[i][1] > 0 else 10 + FYMINUS.index(i)


def for_planes(planes, body):
    if isinstance(planes, tuple):
        for x in planes:
            body(x)
    else:

        def step(x, carry):
            body(x)
            return carry

        lax.fori_loop(planes[0], planes[-1] + 1, step, 0)


def neighbour(x, step, far):
    plane = x + step
    if isinstance(x, int) and (plane < 0 or plane > far):
        return None
    return plane


def moved_population(source, i, x, direction, slot_of, rows_ref, low, high, far):
    step = tuple(direction * part for part in VEL[i])
    plane = neighbour(x, -step[0], far)
    if plane is None:
        value = low() if step[0] == 1 else high()
    else:
        value = source[i, plane]
        if step[1]:
            value = shift_y(value, step[1], rows_ref[slot_of(i), pl.ds(plane, 1), :])
    return shift_z(value, step[2])


def corner_rows(direction):
    return ((7, -1), (9, -1), (8, 0), (10, 0)) if direction == 1 else ((7, 0), (9, 0), (8, -1), (10, -1))


def collide_plane(x, fluid, heat, post, aux, porosity, label):
    _, _, rows, columns = post.shape
    for r, c in tiles(rows, columns):
        phi = porosity[x, r, c]
        inlet = label[x, r, c] == 1
        pops = [fluid[i, x, r, c] for i in range(19)]
        density, velocity = moments(pops, phi)
        for i, value in enumerate((density,) + velocity):
            aux[i, x, r, c] = value
        warm = [heat[i, x, r, c] for i in range(7)]
        result = collide_fluid(pops, density, velocity, inlet) + collide_heat(warm, velocity, phi, inlet)
        for i, value in enumerate(result):
            post[i, x, r, c] = value


def first_boundary(fluid, heat, design, kind, label):
    cells = design.shape
    depth, rows, columns = cells
    far = depth - 1
    last = rows - 1

    def kernel(fluid_in, heat_in, design_in, kind_in, label_in, post, heat, aux, porosity, label, chosen,
               sides, corner, design, kind, sem):
        fields = (
            pltpu.make_async_copy(design_in, design, sem.at[0]),
            pltpu.make_async_copy(kind_in, kind, sem.at[1]),
            pltpu.make_async_copy(label_in, label, sem.at[2]),
        )
        loads = []
        for n, x in enumerate((0, far)):
            loads.append(pltpu.make_async_copy(fluid_in.at[:, x], post.at[0:19, x], sem.at[3 + 2 * n]))
            loads.append(pltpu.make_async_copy(heat_in.at[:, x], heat.at[:, x], sem.at[4 + 2 * n]))
        for copy in fields + tuple(loads):
            copy.start()
        for copy in fields:
            copy.wait()
        for x in (0, far):
            porosity[x] = porosity_of(design[x], kind[x])
            chosen[x] = jnp.where(kind[x] == 2, 1.0, 0.0)
        for copy in loads:
            copy.wait()
        collide_plane(0, post, heat, post, aux, porosity, label)
        collide_plane(far, post, heat, post, aux, porosity, label)
        for slot in range(6):
            sides[slot] = post[PLUS[slot], far]
            sides[6 + slot] = post[MINUS[slot], 0]
        corner[...] = jnp.zeros((8, columns), F32)
        for slot, (i, x) in enumerate(corner_rows(1)):
            y = last if VEL[i][1] > 0 else 0
            corner[slot : slot + 1, :] = post[i, x % depth, y : y + 1, :]

    return call(
        kernel,
        "first_boundary",
        "hhhhh",
        [
            vmem(COUNT, *cells),
            vmem(7, *cells),
            vmem(4, *cells),
            vmem(*cells),
            pltpu.VMEM(cells, jnp.int32),
            vmem(*cells),
            vmem(12, rows, columns),
            vmem(8, columns),
            vmem(*cells),
            pltpu.VMEM(cells, jnp.int32),
        ],
        (fluid, heat, design, kind, label),
        scratch=[pltpu.SemaphoreType.DMA((7,))],
    )


def first_interior(fluid, heat, post, aux, porosity, chosen, design, kind, label, after):
    cells = label.shape
    depth, rows, columns = cells
    far = depth - 1
    last = rows - 1

    def kernel(fluid, heat, post_in, aux_in, porosity_in, chosen_in, design, kind, label, after_ref,
               post, aux, porosity, chosen, msg):
        def body(x):
            porosity[x] = porosity_of(design[x], kind[x])
            chosen[x] = jnp.where(kind[x] == 2, 1.0, 0.0)
            collide_plane(x, fluid, heat, post, aux, porosity, label)

        for_planes(range(1, far), body)

        def rows_of(x, carry):
            here = pl.ds(x, 1)
            for i in YPLUS:
                msg[row_slot(i), here, :] = post[i, x, last : last + 1, :]
            for i in YMINUS:
                msg[row_slot(i), here, :] = post[i, x, 0:1, :]
            return carry

        lax.fori_loop(0, depth, rows_of, 0)

    return call(
        kernel,
        "first_interior",
        "vvvvvvvvvv",
        [vmem(COUNT, *cells), vmem(4, *cells), vmem(*cells), vmem(*cells), vmem(12, depth, columns)],
        (fluid, heat, post, aux, porosity, chosen, design, kind, label, after),
        aliases={2: 0, 3: 1, 4: 2, 5: 3},
        micros=1.0,
    )


def source_weights(aux, heat, porosity, label, chosen, x, k):
    density, ux, uy, uz = (aux[i, x] for i in range(4))
    phi = porosity[x]
    valid = jnp.logical_and(label[x] != 1, chosen[x] > 0.0)
    over = 0.44 / ((0.1 + phi) * (0.5 + 0.6 * phi))
    rate = heat_rate_of(phi)
    temper = heat[0, x]
    for i in range(1, 7):
        temper = temper + heat[i, x]
    part = along(VEL[k], (ux, uy, uz))
    weight = over * (0.5 * rate * temper) * part - 0.125
    weight = weight + (0.9 * rate * rate) * (temper * (0.125 + 0.5 * part) - heat[k, x])
    scale = jnp.where(valid, 3.75 * over * density, 0.0)
    return jnp.where(valid, weight, 0.0), scale, ux, uy, uz


def crossing_sides(sides_ref, row_of, direction, slot):
    i, j = PLUS[slot], MINUS[slot]
    plus, minus = sides_ref[slot], sides_ref[6 + slot]
    if VEL[i][1]:
        plus = shift_y(plus, direction * VEL[i][1], row_of(i))
        minus = shift_y(minus, direction * VEL[j][1], row_of(j))
    return (plus, minus) if direction == 1 else (minus, plus)


def first_faces(sides, rows_in, label, aux, heat, porosity, chosen):
    _, rows, columns = sides.shape
    far = label.shape[0] - 1

    def kernel(sides_ref, rows_ref, label, aux, heat, porosity, chosen, a_ref, b_ref, token):
        token[...] = jnp.zeros((8, 128), F32)
        even = lax.rem(lax.axis_index("gx"), 2) == 0

        def row_of(i):
            slot = [entry[0] for entry in corner_rows(1)].index(i)
            return rows_ref[slot : slot + 1, :]

        for slot in range(6):
            high, low = crossing_sides(sides_ref, row_of, 1, slot)
            a_ref[slot] = pick(even, high, low)
            b_ref[slot] = pick(even, low, high)
        highs = source_weights(aux, heat, porosity, label, chosen, far, 1)
        lows = source_weights(aux, heat, porosity, label, chosen, 0, 2)
        for slot in range(EARLY):
            a_ref[6 + slot] = pick(even, highs[slot], lows[slot])
            b_ref[6 + slot] = pick(even, lows[slot], highs[slot])

    return call(
        kernel,
        "first_faces",
        "v" * 7,
        [vmem(6 + EARLY, rows, columns)] * 2 + [vmem(8, 128)],
        (sides, rows_in, label, aux, heat, porosity, chosen),
    )


def costate_faces(sides, rows_in):
    _, rows, columns = sides.shape

    def kernel(sides_ref, rows_ref, a_ref, b_ref):
        even = lax.rem(lax.axis_index("gx"), 2) == 0
        far = rows_ref.shape[1] - 1

        def row_of(i):
            x = 0 if VEL[i][0] > 0 else far
            return rows_ref[row_slot(i), x : x + 1, :]

        for slot in range(6):
            high, low = crossing_sides(sides_ref, row_of, -1, slot)
            a_ref[slot] = pick(even, high, low)
            b_ref[slot] = pick(even, low, high)

    return call(kernel, "costate_faces", "vv", [vmem(6, rows, columns)] * 2, (sides, rows_in))


def second_planes(planes, source, rows_ref, low, high, porosity_ref, label_ref, post, heat, aux, moved):
    _, depth, rows, columns = source.shape
    far = depth - 1

    def body(x):
        for i in range(COUNT):
            value = moved_population(
                source, i, x, 1, row_slot, rows_ref, lambda: low(PLUS.index(i)), lambda: high(MINUS.index(i)), far
            )
            if i < 19:
                moved[i] = value
            else:
                heat[i - 19, x] = value
        for r, c in tiles(rows, columns):
            porosity = porosity_ref[x, r, c]
            inlet = label_ref[x, r, c] == 1
            pops = [moved[i, r, c] for i in range(19)]
            density, velocity = moments(pops, porosity)
            for i, value in enumerate((density,) + velocity):
                aux[i, x, r, c] = value
            warm = [heat[i, x, r, c] for i in range(7)]
            for i, value in enumerate(collide_heat(warm, velocity, porosity, inlet)):
                post[i, x, r, c] = value

    for_planes(planes, body)


def input_rows(x, adj, label, msg):
    here = pl.ds(x, 1)
    last = label.shape[1] - 1
    for i in FYPLUS:
        msg[adjoint_slot(i), here, :] = adj[i, x, 0:1, :]
    for i in FYMINUS:
        msg[adjoint_slot(i), here, :] = adj[i, x, last : last + 1, :]
    msg[15, here, :] = jnp.where(label[x, 0:1, :] == 2, 1.0, 0.0)
    msg[16, here, :] = jnp.where(label[x, last : last + 1, :] == 2, 1.0, 0.0)


def heat_rows(x, post, hadj, label, msg):
    here = pl.ds(x, 1)
    far, last = label.shape[0] - 1, label.shape[1] - 1
    msg[0, here, :] = post[3, x, last : last + 1, :]
    msg[1, here, :] = post[4, x, 0:1, :]
    before, after = neighbour(x, -1, far), neighbour(x, 1, far)
    for slot, y in ((0, 0), (1, last)):
        row = slice(y, y + 1)
        total = post[4, x, 1:2, :] if y == 0 else post[3, x, last - 1 : last, :]
        total = total + post[0, x, row, :]
        total = total + shift_z(post[5, x, row, :], 1) + shift_z(post[6, x, row, :], -1)
        if before is not None:
            total = total + post[1, before, row, :]
        if after is not None:
            total = total + post[2, after, row, :]
        msg[2 + slot, here, :] = hadj[3 + slot, x, row, :] + jnp.where(label[x, row, :] == 2, total, 0.0)


def second_interior(source, rows_in, porosity, label, adjoint, heat_adjoint):
    cells = label.shape
    depth, rows, columns = cells
    far = depth - 1

    def kernel(source, rows_ref, porosity, label, adj, hadj, post, heat, aux, msg, moved):
        second_planes(range(1, far), source, rows_ref, None, None, porosity, label, post, heat, aux, moved)
        for_planes(range(0, depth), lambda x: input_rows(x, adj, label, msg))
        for_planes(range(2, far - 1), lambda x: heat_rows(x, post, hadj, label, msg))

    return call(
        kernel,
        "second_interior",
        "vvvvvv",
        [vmem(7, *cells), vmem(7, *cells), vmem(4, *cells), vmem(17, depth, columns)],
        (source, rows_in, porosity, label, adjoint, heat_adjoint),
        scratch=[pltpu.VMEM((19, rows, columns), F32)],
        micros=0.0,
    )


def second_boundary(source, rows_in, face_a, face_b, porosity, label, heat_adjoint, post, heat, aux, msg):
    cells = label.shape
    depth, rows, columns = cells
    far = depth - 1
    last = rows - 1

    def kernel(source, rows_ref, a_ref, b_ref, porosity, label, hadj, post_in, heat_in, aux_in, msg_in,
               post, heat, aux, msg, moved):
        even = lax.rem(lax.axis_index("gx"), 2) == 0

        def low(slot):
            return pick(even, b_ref[slot], a_ref[slot])

        def high(slot):
            return pick(even, a_ref[slot], b_ref[slot])

        second_planes((0, far), source, rows_ref, low, high, porosity, label, post, heat, aux, moved)

        for x in (0, 1, far - 1, far):
            heat_rows(x, post, hadj, label, msg)
        msg[4] = jnp.zeros((depth, columns), F32)
        msg[4, 0:1, :] = post[1, far, 0:1, :]
        msg[4, 1:2, :] = post[1, far, last : last + 1, :]
        msg[4, 2:3, :] = post[2, 0, 0:1, :]
        msg[4, 3:4, :] = post[2, 0, last : last + 1, :]

    return call(
        kernel,
        "second_boundary",
        "vvvvvvvvvvv",
        [vmem(7, *cells), vmem(7, *cells), vmem(4, *cells), vmem(17, depth, columns)],
        (source, rows_in, face_a, face_b, porosity, label, heat_adjoint, post, heat, aux, msg),
        scratch=[pltpu.VMEM((19, rows, columns), F32)],
        aliases={7: 0, 8: 1, 9: 2, 10: 3},
        micros=0.0,
    )


def plane_of(ref, slot):
    return ref[SEEDS + 16 * slot : SEEDS + 16 * (slot + 1)]


def second_faces(post, heat_adjoint, adjoint, label, rows_in, aux, heat, porosity, chosen):
    depth, rows, columns = label.shape
    far = depth - 1

    def kernel(post, hadj, adj, label, rows_ref, aux, heat, porosity, chosen, a_ref, b_ref):
        even = lax.rem(lax.axis_index("gx"), 2) == 0

        def partial(x, other):
            total = post[0, x] + other
            total = total + shift_y(post[3, x], 1, rows_ref[0, x : x + 1, :])
            total = total + shift_y(post[4, x], -1, rows_ref[1, x : x + 1, :])
            return total + shift_z(post[5, x], 1) + shift_z(post[6, x], -1)

        def put(start, high, low):
            where = slice(start, start + high.shape[0])
            a_ref[where] = pick(even, high, low)
            b_ref[where] = pick(even, low, high)

        put(0, post[1, far], post[2, 0])
        high_seed = hadj[2, far] + jnp.where(label[far] == 2, partial(far, post[1, far - 1]), 0.0)
        low_seed = hadj[1, 0] + jnp.where(label[0] == 2, partial(0, post[2, 1]), 0.0)
        put(rows, high_seed, low_seed)
        place = lax.broadcasted_iota(jnp.int32, (8, columns), 0)

        def spread(slot):
            return jnp.broadcast_to(rows_ref[4, slot : slot + 1, :], (8, columns))

        put(2 * rows, jnp.where(place == 0, spread(1), spread(0)), jnp.where(place == 0, spread(3), spread(2)))
        for slot in range(5):
            i, j = FPLUS[slot], FMINUS[slot]
            low, high = adj[i, 0], adj[j, far]
            if VEL[i][1]:
                low = shift_y(low, -VEL[i][1], rows_ref[adjoint_slot(i), 0:1, :])
                high = shift_y(high, -VEL[j][1], rows_ref[adjoint_slot(j), far : far + 1, :])
            put(SEEDS + 16 * slot, high, low)
        put(SEEDS + 80, jnp.where(label[far] == 2, 1.0, 0.0), jnp.where(label[0] == 2, 1.0, 0.0))
        highs = source_weights(aux, heat, porosity, label, chosen, far, 1)
        lows = source_weights(aux, heat, porosity, label, chosen, 0, 2)
        for slot, (high, low) in enumerate(zip(highs[EARLY:], lows[EARLY:])):
            put(SEEDS + 16 * (6 + slot), high, low)

    shape = (SEEDS + 16 * (11 - EARLY), columns)
    return call(
        kernel,
        "second_faces",
        "v" * 9,
        [vmem(*shape)] * 2,
        (post, heat_adjoint, adjoint, label, rows_in, aux, heat, porosity, chosen),
    )


def costate_rows(x, lam, msg):
    here = pl.ds(x, 1)
    last = lam.shape[2] - 1
    for i in YPLUS:
        msg[row_slot(i), here, :] = lam[i, x, 0:1, :]
    for i in YMINUS:
        msg[row_slot(i), here, :] = lam[i, x, last : last + 1, :]


def second_adjoint(planes, name, fixed, arrived, state, micros):
    adj, hadj, post, heat, aux, porosity, label, rows_in = fixed
    cells = label.shape
    depth, rows, columns = cells
    far = depth - 1
    last = rows - 1
    first = state is None
    boundary = isinstance(planes, tuple)
    lit_planes = range(planes[0] - 1, planes[-1] + 2) if first else ((0, far) if boundary else ())

    def kernel(*refs):
        refs = list(refs)
        adj, hadj, post, heat, aux, porosity, label, rows_ref = refs[:8]
        refs = refs[8:]
        if boundary:
            sa, sb = refs[:2]
        refs = refs[len(arrived) :]
        if not first:
            refs = refs[4:]
        lam, sens, lit, msg = refs[:4]
        sides = refs[4] if boundary else None
        moved = refs[-1]
        even = lax.rem(lax.axis_index("gx"), 2) == 0
        tail = 2 * rows

        def from_left(where):
            return pick(even, sb[where], sa[where])

        def from_right(where):
            return pick(even, sa[where], sb[where])

        def light(x):
            here = pl.ds(x, 1)
            before, after = neighbour(x, -1, far), neighbour(x, 1, far)
            total = post[0, x]
            total = total + (from_left(slice(0, rows)) if before is None else post[1, before])
            total = total + (from_right(slice(0, rows)) if after is None else post[2, after])
            total = total + shift_y(post[3, x], 1, rows_ref[0, here, :])
            total = total + shift_y(post[4, x], -1, rows_ref[1, here, :])
            total = total + shift_z(post[5, x], 1) + shift_z(post[6, x], -1)
            lit[x] = jnp.where(label[x] == 2, total, 0.0)

        if lit_planes:
            for_planes(lit_planes, light)

        def body(x):
            here = pl.ds(x, 1)
            before, after = neighbour(x, -1, far), neighbour(x, 1, far)
            glow = lit[x]
            moved[19] = hadj[0, x] + glow
            if after is None:
                moved[20] = from_right(slice(rows, tail)) + pick(even, plane_of(sa, 5), plane_of(sb, 5)) * post[1, far]
            else:
                moved[20] = hadj[1, after] + lit[after]
            if before is None:
                moved[21] = from_left(slice(rows, tail)) + pick(even, plane_of(sb, 5), plane_of(sa, 5)) * post[2, 0]
            else:
                moved[21] = hadj[2, before] + lit[before]
            above = post[3, x, last : last + 1, :]
            below = post[4, x, 0:1, :]
            if before is None:
                above = above + from_left(slice(tail + 1, tail + 2))
                below = below + from_left(slice(tail, tail + 1))
            if after is None:
                above = above + from_right(slice(tail + 1, tail + 2))
                below = below + from_right(slice(tail, tail + 1))
            moved[22] = shift_y(hadj[3, x] + glow, -1, rows_ref[2, here, :] + rows_ref[15, here, :] * above)
            moved[23] = shift_y(hadj[4, x] + glow, 1, rows_ref[3, here, :] + rows_ref[16, here, :] * below)
            moved[24] = shift_z(hadj[5, x] + glow, -1)
            moved[25] = shift_z(hadj[6, x] + glow, 1)
            for i in range(19):
                moved[i] = moved_population(
                    adj,
                    i,
                    x,
                    -1,
                    adjoint_slot,
                    rows_ref,
                    lambda: pick(even, plane_of(sb, FMINUS.index(i)), plane_of(sa, FMINUS.index(i))),
                    lambda: pick(even, plane_of(sa, FPLUS.index(i)), plane_of(sb, FPLUS.index(i))),
                    far,
                )
            for r, c in tiles(rows, columns):
                inlet = label[x, r, c] == 1
                density, ux, uy, uz = (aux[i, x, r, c] for i in range(4))
                warm = [heat[i, x, r, c] for i in range(7)]
                mu = [moved[i, r, c] for i in range(19)]
                nu = [moved[19 + i, r, c] for i in range(7)]
                result, result_heat, part = collide_adjoint(
                    density, (ux, uy, uz), warm, porosity[x, r, c], inlet, mu, nu
                )
                for i, value in enumerate(result + result_heat):
                    lam[i, x, r, c] = value
                sens[x, r, c] = part

        for_planes(planes, body)
        if boundary:
            for slot in range(6):
                sides[slot] = lam[PLUS[slot], 0]
                sides[6 + slot] = lam[MINUS[slot], far]
        for_planes(planes, lambda x: costate_rows(x, lam, msg))

    outs = [vmem(COUNT, *cells), vmem(*cells), vmem(*cells), vmem(12, depth, columns)]
    if boundary:
        outs.append(vmem(12, rows, columns))
    args = fixed + arrived + (() if first else state)
    base = len(args) - 4
    return call(
        kernel,
        name,
        "v" * len(args),
        outs,
        args,
        scratch=[pltpu.VMEM((COUNT, rows, columns), F32)],
        aliases=None if first else {base + n: n for n in range(4)},
        micros=micros,
    )


def arriving(lam, rows_ref, moved, x, far, low, high):
    for i in range(COUNT):
        moved[i] = moved_population(
            lam, i, x, -1, row_slot, rows_ref, lambda: low(MINUS.index(i)), lambda: high(PLUS.index(i)), far
        )


def first_sensitivity(lam, rows_in, fixed, sens_one, weights_a, weights_b, rate_a, rate_b, waves):
    aux, heat, porosity, label, chosen = fixed
    depth, rows, columns = label.shape
    far = depth - 1
    half = columns // 2
    count = depth + 2

    def kernel(lam, rows_ref, aux, heat, porosity, label, chosen, sens_ref, a_ref, b_ref, ra_ref, rb_ref, waves_ref,
               own, other, moved, total):
        even = lax.rem(lax.axis_index("gx"), 2) == 0
        core = lax.axis_index("gy")

        def nothing(slot):
            return jnp.zeros((rows, columns), F32)

        def body(x):
            arriving(lam, rows_ref, moved, x, far, nothing, nothing)
            for r, c in tiles(rows, columns):
                inlet = label[x, r, c] == 1
                density, ux, uy, uz = (aux[i, x, r, c] for i in range(4))
                warm = [heat[i, x, r, c] for i in range(7)]
                mu = [moved[i, r, c] for i in range(19)]
                nu = [moved[19 + i, r, c] for i in range(7)]
                _, _, part = collide_adjoint(density, (ux, uy, uz), warm, porosity[x, r, c], inlet, mu, nu)
                total[x, r, c] = jnp.where(chosen[x, r, c] > 0.0, part + sens_ref[x, r, c], 0.0)

        for_planes((0, far), body)
        for_planes(range(1, far), body)
        def weights(slot, reverse):
            if slot < EARLY:
                of_a, of_b = ra_ref[6 + slot], rb_ref[6 + slot]
            else:
                of_a, of_b = plane_of(a_ref, 6 + slot - EARLY), plane_of(b_ref, 6 + slot - EARLY)
            return pick(even, of_b, of_a) if reverse else pick(even, of_a, of_b)

        for place, x, members, reverse in ((depth, 0, PLUS, True), (depth + 1, far, MINUS, False)):
            rate, scale, *vector = (weights(slot, reverse) for slot in range(5))
            speed = vector[0] * vector[0] + vector[1] * vector[1] + vector[2] * vector[2]
            result = jnp.zeros((rows, columns), F32)
            for i in members:
                value = lam[i, x]
                if VEL[i][1]:
                    value = shift_y(value, -VEL[i][1], rows_ref[row_slot(i), x : x + 1, :])
                value = shift_z(value, -VEL[i][2])
                if i < 19:
                    part = along(VEL[i], vector)
                    result = result + (fluid_wts[i] * scale) * (part - speed + 3.0 * part * part) * value
                else:
                    result = result + rate * value
            total[place] = result
        flat = total[...].reshape(count * rows, columns)
        own[...] = multiply(flat, waves_ref[core]).reshape(count, rows, half)
        other[...] = multiply(flat, waves_ref[1 - core]).reshape(count, rows, half)

    args = (lam, rows_in) + fixed + (sens_one, weights_a, weights_b, rate_a, rate_b, waves)
    return call(
        kernel,
        "first_sensitivity",
        "v" * len(args),
        [vmem(count, rows, half)] * 2,
        args,
        scratch=[pltpu.VMEM((COUNT, rows, columns), F32), pltpu.VMEM((count, rows, columns), F32)],
    )


def first_adjoint(groups, name, lam, rows_in, fixed, arrived, early_planes, early):
    aux, heat, porosity, label = fixed
    cells = label.shape
    depth, rows, columns = cells
    far = depth - 1
    planes = [x for group in groups for x in group]
    count = len(planes)
    last = early is not None

    def kernel(*refs):
        refs = list(refs)
        lam, rows_ref, aux, heat, porosity, label = refs[:6]
        refs = refs[6:]
        if last:
            b_ref, a_ref, early_ref, fluid_out, heat_out, token, moved, out, sem = refs
            token[...] = jnp.zeros((8, 128), F32)
        else:
            out, moved = refs
        even = lax.rem(lax.axis_index("gx"), 2) == 0

        def place(x):
            return planes.index(x) if isinstance(x, int) else x - groups[-1][0] + count - len(groups[-1])

        def writes(source, n, x, slot):
            return (
                pltpu.make_async_copy(source.at[0:19, n], fluid_out.at[:, x], sem.at[2 * slot]),
                pltpu.make_async_copy(source.at[19:26, n], heat_out.at[:, x], sem.at[2 * slot + 1]),
            )

        def low(slot):
            return pick(even, b_ref[slot], a_ref[slot])

        def high(slot):
            return pick(even, a_ref[slot], b_ref[slot])

        def body(x):
            n = place(x)
            arriving(lam, rows_ref, moved, x, far, low, high)
            for r, c in tiles(rows, columns):
                inlet = label[x, r, c] == 1
                density, ux, uy, uz = (aux[i, x, r, c] for i in range(4))
                warm = [heat[i, x, r, c] for i in range(7)]
                mu = [moved[i, r, c] for i in range(19)]
                nu = [moved[19 + i, r, c] for i in range(7)]
                result, result_heat, _ = collide_adjoint(density, (ux, uy, uz), warm, porosity[x, r, c], inlet, mu, nu)
                for i, value in enumerate(result + result_heat):
                    out[i, n, r, c] = value
            if last:
                for copy in writes(out, n, x, n):
                    copy.start()

        early_copies = []
        if last:
            for n, x in enumerate(early_planes):
                early_copies += writes(early_ref, n, x, count + n)
        for copy in early_copies:
            copy.start()
        for group in groups:
            for_planes(group, body)
        if last:

            def finish(x):
                for copy in writes(out, place(x), x, place(x)):
                    copy.wait()

            for group in groups:
                for_planes(group, finish)
        for copy in early_copies:
            copy.wait()

    buffer = (COUNT, count, rows, columns)
    moved = pltpu.VMEM((COUNT, rows, columns), F32)
    args = (lam, rows_in) + fixed + arrived + ((early,) if last else ())
    if last:
        outs = [hbm(19, *cells), hbm(7, *cells), vmem(8, 128)]
        scratch = [moved, pltpu.VMEM(buffer, F32), pltpu.SemaphoreType.DMA((2 * (count + len(early_planes)),))]
    else:
        outs = [vmem(*buffer)]
        scratch = [moved]
    return call(kernel, name, "v" * len(args), outs, args, scratch=scratch)


def halves(value):
    high = value.astype(jnp.bfloat16)
    return high, (value - high.astype(F32)).astype(jnp.bfloat16)


def multiply(first, second):
    a, b = halves(first)
    c, d = halves(second)
    small = jnp.dot(a, d, preferred_element_type=F32) + jnp.dot(b, c, preferred_element_type=F32)
    return jnp.dot(a, c, preferred_element_type=F32) + small


def hartley(length):
    index = np.arange(length)
    angle = 2.0 * np.pi * ((index[:, None] * index[None, :]) % length) / length
    return (np.cos(angle) + np.sin(angle)) / np.sqrt(length)


def filter_tables(depth, count_y, count_z):
    half = count_z // 2
    wave_z = hartley(count_z)
    waves = np.stack([wave_z[:, :half], wave_z[:, half:]]).astype(np.float32)
    waves_back = np.stack([wave_z[:half], wave_z[half:]]).astype(np.float32)
    wave_y = np.kron(np.eye(depth), hartley(count_y)).astype(np.float32)
    wave_ends = np.kron(np.eye(2), hartley(count_y)).astype(np.float32)
    symbol_y = 2.0 - 2.0 * np.cos(2.0 * np.pi * np.arange(count_y) / count_y)
    symbol_z = 2.0 - 2.0 * np.cos(2.0 * np.pi * np.arange(count_z) / count_z)
    weight = float(RADIUS * RADIUS)
    centre = (1.0 + weight * (2.0 + symbol_y[:, None] + symbol_z[None, :])) / weight
    ratio = 2.0 / (centre + np.sqrt(centre * centre - 4.0))
    peak = 1.0 / (weight * (1.0 / ratio - ratio))
    fields = np.stack([ratio, np.log(ratio) * depth, peak]).astype(np.float32)
    fields = np.stack([fields[:, :, :half], fields[:, :, half:]])
    return waves, waves_back, wave_y, wave_ends, fields


def to_modes(own, other, wave_y, wave_ends, fields):
    count, rows, half = own.shape
    depth = count - 2
    full = 2 * rows
    inside = depth * full

    def kernel(own_ref, other_ref, wave_ref, small_ref, field_ref, modes, ends, both):
        core = lax.axis_index("gy")
        for x in range(count):
            both[x * full : x * full + rows] = own_ref[x]
            both[x * full + rows : (x + 1) * full] = other_ref[x]
        modes[0:inside] = multiply(wave_ref[...], both[0:inside])
        modes[inside : inside + 2 * full] = multiply(small_ref[...], both[inside : inside + 2 * full])
        ratio = field_ref[core, 0]
        before, after = modes[inside : inside + full], modes[inside + full : inside + 2 * full]
        head = before
        for x in range(depth):
            head = head * ratio + modes[x * full : (x + 1) * full]
        ends[0] = head * ratio + after
        tail = after
        for x in range(depth - 1, -1, -1):
            tail = tail * ratio + modes[x * full : (x + 1) * full]
        ends[1] = tail * ratio + before

    return call(
        kernel,
        "to_modes",
        "vvvvv",
        [vmem(count * full, half), vmem(2, full, half)],
        (own, other, wave_y, wave_ends, fields),
        scratch=[pltpu.VMEM((count * full, half), F32)],
    )


def join_segments(ends, arrived, carry, fields, reach, after):
    first = carry is None

    def kernel(*refs):
        ends_ref, in_ref, field_ref = refs[:3]
        carry_ref = None if first else refs[3]
        ends_out, carry_out = refs[-2:]
        core = lax.axis_index("gy")
        index = lax.axis_index("gx")
        place = lax.rem(index, reach)
        upper = lax.rem(lax.div(index, reach), 2) == 1
        rate = field_ref[core, 1]
        whole = jnp.exp(rate * float(reach))
        forward = jnp.exp(rate * place.astype(F32))
        backward = jnp.exp(rate * (reach - 1 - place).astype(F32))
        head, tail = ends_ref[0], ends_ref[1]
        head_in, tail_in = in_ref[0], in_ref[1]
        left = pick(upper, forward * head_in, jnp.zeros_like(head))
        right = pick(upper, jnp.zeros_like(head), backward * tail_in)
        carry_out[0] = left if first else carry_ref[0] + left
        carry_out[1] = right if first else carry_ref[1] + right
        ends_out[0] = pick(upper, head + whole * head_in, head_in + whole * head)
        ends_out[1] = pick(upper, tail_in + whole * tail, tail + whole * tail_in)

    args = (ends, arrived, fields) + (() if first else (carry,)) + after
    return call(kernel, "join_segments", "v" * len(args), [vmem(*ends.shape)] * 2, args, micros=0.0)


def from_modes(modes, ends, carry, wave_y, fields, depth, parts, after):
    half = modes.shape[1]
    full = modes.shape[0] // (depth + 2)
    rows = full // 2
    inside = depth * full

    def kernel(modes_ref, ends_ref, carry_ref, wave_ref, field_ref, after_ref, own, other, solved):
        core = lax.axis_index("gy")
        index = lax.axis_index("gx")
        ratio, rate, peak = field_ref[core, 0], field_ref[core, 1], field_ref[core, 2]
        around = 1.0 / (1.0 - jnp.exp(rate * float(parts)))
        left = carry_ref[0] + jnp.exp(rate * index.astype(F32)) * around * ends_ref[0]
        right = carry_ref[1] + jnp.exp(rate * (parts - 1 - index).astype(F32)) * around * ends_ref[1]
        run = left + ratio * modes_ref[inside : inside + full]
        for x in range(depth):
            run = run + modes_ref[x * full : (x + 1) * full]
            solved[x * full : (x + 1) * full] = run
            run = run * ratio
        run = right + ratio * modes_ref[inside + full : inside + 2 * full]
        for x in range(depth - 1, -1, -1):
            solved[x * full : (x + 1) * full] = peak * (solved[x * full : (x + 1) * full] + run)
            run = ratio * (run + modes_ref[x * full : (x + 1) * full])
        back = multiply(wave_ref[...], solved[...])
        for x in range(depth):
            own[x * rows : (x + 1) * rows] = back[x * full : x * full + rows]
            other[x * rows : (x + 1) * rows] = back[x * full + rows : (x + 1) * full]

    flat = (depth * rows, half)
    return call(
        kernel,
        "from_modes",
        "vvvvvv",
        [vmem(*flat)] * 2,
        (modes, ends, carry, wave_y, fields, after),
        scratch=[pltpu.VMEM((inside, half), F32)],
    )


def own_transform(own, waves_back):
    flat, half = own.shape

    def kernel(own_ref, wave_ref, out):
        out[...] = multiply(own_ref[...], wave_ref[lax.axis_index("gy")])

    return call(kernel, "own_transform", "vv", [vmem(flat, 2 * half)], (own, waves_back))


def last_transform(partial, other, waves_back, depth):
    flat, half = other.shape
    rows = flat // depth
    step = depth // 2

    def kernel(partial_ref, other_ref, wave_ref, out_ref, out, sem):
        copies = []
        for n in range(2):
            where = slice(n * step * rows, (n + 1) * step * rows)
            result = partial_ref[where] + multiply(other_ref[where], wave_ref[1 - lax.axis_index("gy")])
            part = slice(n * step, (n + 1) * step)
            out[part] = result.reshape(step, rows, 2 * half)
            copies.append(pltpu.make_async_copy(out.at[part], out_ref.at[part], sem.at[n]))
            copies[n].start()
        for copy in copies:
            copy.wait()

    shape = (depth, rows, 2 * half)
    return call(
        kernel,
        "last_transform",
        "vvv",
        [hbm(*shape)],
        (partial, other, waves_back),
        scratch=[pltpu.VMEM(shape, F32), pltpu.SemaphoreType.DMA((2,))],
    )


def per_device(fluid_state, heat_state, design, cell_type, boundary, fluid_adjoint, heat_adjoint):
    depth, rows, columns = design.shape
    far = depth - 1
    parts = lax.axis_size("gx")
    waves, waves_back, wave_y, wave_ends, fields = filter_tables(depth, 2 * rows, columns)

    pairs_a = [(i, i ^ 1) for i in range(parts)]
    pairs_b = [(i, (i + 1) % parts if i % 2 else (i - 1) % parts) for i in range(parts)]

    def across(value):
        return lax.ppermute(value, "gy", [(0, 1), (1, 0)])

    def sideways(first, second):
        first = lax.ppermute(first, "gx", pairs_a)
        second = lax.ppermute(second, "gx", pairs_b)
        return first, second

    adj, hadj = fluid_adjoint, heat_adjoint
    post, heat_edge, aux_edge, porosity, label, chosen, sides, corner, design, kind = first_boundary(
        *(in_hbm(value) for value in (fluid_state, heat_state, design, cell_type, boundary))
    )
    face_a, face_b, token = first_faces(sides, across(corner), label, aux_edge, heat_edge, porosity, chosen)
    face_a, face_b = sideways(face_a, face_b)
    rate_a, rate_b = face_a, face_b
    heat_zero = heat_state
    post, aux_zero, porosity, chosen, rows_one = first_interior(
        fluid_state, heat_zero, post, aux_edge, porosity, chosen, design, kind, label, token
    )
    rows_one = across(rows_one)
    post_one, heat_one, aux_one, rows_heat = second_interior(post, rows_one, porosity, label, adj, hadj)
    post_one, heat_one, aux_one, rows_heat = second_boundary(
        post, rows_one, face_a, face_b, porosity, label, hadj, post_one, heat_one, aux_one, rows_heat
    )
    rows_heat = across(rows_heat)
    seed_a, seed_b = second_faces(post_one, hadj, adj, label, rows_heat, aux_zero, heat_zero, porosity, chosen)
    seed_a, seed_b = sideways(seed_a, seed_b)
    fixed = (adj, hadj, post_one, heat_one, aux_one, porosity, label, rows_heat)
    state = second_adjoint(range(2, far - 1), "adjoint_inner", fixed, (), None, 0.0)
    lam, sens_one, lit, rows_two, sides = second_adjoint(
        (0, 1, far - 1, far), "adjoint_outer", fixed, (seed_a, seed_b), tuple(state), 0.0
    )
    rows_two = across(rows_two)
    face_a, face_b = costate_faces(sides, rows_two)
    face_a, face_b = sideways(face_a, face_b)
    fixed = (aux_zero, heat_zero, porosity, label)
    own, other = first_sensitivity(lam, rows_two, fixed + (chosen,), sens_one, seed_a, seed_b, rate_a, rate_b, waves)
    early = first_adjoint(((1,),), "costate_early", lam, rows_two, fixed, (), None, None)
    fluid_costate, heat_costate, token = first_adjoint(
        ((0, far), range(2, far)), "costate_rest", lam, rows_two, fixed, (face_b, face_a), (1,), early
    )
    other = across(other)
    modes, ends = to_modes(own, other, wave_y, wave_ends, fields)
    carry = None
    reach = 1
    while reach < parts:
        arrived = lax.ppermute(ends, "gx", [(i, i ^ reach) for i in range(parts)])
        ends, carry = join_segments(ends, arrived, carry, fields, reach, (early,) if reach == 1 else ())
        reach = 2 * reach
    own, other = from_modes(modes, ends, carry, wave_y, fields, depth, parts, token)
    other = across(other)
    partial = own_transform(own, waves_back)
    return (fluid_costate, heat_costate, last_transform(partial, other, waves_back, depth))


def solution(mesh):
    return jax.shard_map(
        per_device,
        mesh=mesh,
        in_specs=(
            P(None, ("case", "gx"), "gy", None),
            P(None, ("case", "gx"), "gy", None),
            P(("case", "gx"), "gy", None),
            P(("case", "gx"), "gy", None),
            P(("case", "gx"), "gy", None),
            P(None, ("case", "gx"), "gy", None),
            P(None, ("case", "gx"), "gy", None),
        ),
        out_specs=(
            P(None, ("case", "gx"), "gy", None),
            P(None, ("case", "gx"), "gy", None),
            P(("case", "gx"), "gy", None),
        ),
        check_vma=False,
    )
```
